32 devices in a mesh: expert: 8 (over z, x), hidden: 4 (over y, core).
Axes of the slice: x: 2, y: 2, z: 4, core: 2. Of those that a mesh axis runs over, the one named last changes fastest.
Arguments:
- tokens: bfloat16 [16384, 512], P(('expert', 'hidden')), may hold values from -6 to 6
- lengths: int32 [32, 16], P(('expert', 'hidden')), may hold values from 1 to 256, 512 in all within a row
- task_ids: int32 [32, 16], P(('expert', 'hidden')), may hold values from 0 to 29
- routes: int32 [16384, 2], P(('expert', 'hidden')), may hold values from 0 to 7, all different within a row; in each aligned block of 512 rows (0 to 511, 512 to 1023, ...) at most 192 rows name the same one
- w_qkv: bfloat16 [512, 1536], P(('expert', 'hidden')), may hold values from -0.25 to 0.25
- w_attn_out: bfloat16 [512, 512], P(('expert', 'hidden')), may hold values from -1 to 1
- w_gate: bfloat16 [512, 240], P(('expert', 'hidden')), may hold values from -0.1875 to 0.1875
- ln1_gain: bfloat16 [512], P(('expert', 'hidden')), may hold values from 0.5 to 1.5
- ln1_bias: bfloat16 [512], P(('expert', 'hidden')), may hold values from -1 to 1
- ln2_gain: bfloat16 [512], P(('expert', 'hidden')), may hold values from 0.5 to 1.5
- ln2_bias: bfloat16 [512], P(('expert', 'hidden')), may hold values from -1 to 1
- w_in: bfloat16 [8, 512, 2048], P('expert', None, 'hidden'), may hold values from -0.25 to 0.25
- w_out: bfloat16 [8, 2048, 512], P('expert', 'hidden'), may hold values from -0.25 to 0.25
- cotangent: bfloat16 [16384, 512], P(('expert', 'hidden')), may hold values from -6 to 6
Outputs:
- layer_out: bfloat16 [16384, 512], P(('expert', 'hidden'))
- grad_tokens: float32 [16384, 512], P(('expert', 'hidden'))
- grad_w_qkv: float32 [512, 1536], P(('expert', 'hidden'))
- grad_w_attn_out: float32 [512, 512], P(('expert', 'hidden'))
- grad_w_gate: float32 [512, 240], P(('expert', 'hidden'))
- grad_ln1_gain: float32 [512], P(('expert', 'hidden'))
- grad_ln1_bias: float32 [512], P(('expert', 'hidden'))
- grad_ln2_gain: float32 [512], P(('expert', 'hidden'))
- grad_ln2_bias: float32 [512], P(('expert', 'hidden'))
- grad_w_in: float32 [8, 512, 2048], P('expert', None, 'hidden')
- grad_w_out: float32 [8, 2048, 512], P('expert', 'hidden')
The draws below stay inside these ranges and needn't reach their ends.
Inputs may be any that keep to these rules, and one draw needn't show every extreme that they name: `lengths`: 16 sentences a pack, of 1 to 256 tokens, that fill its 512 tokens; the longest of each pack has exactly 256. `routes`: each token names 2 different experts; among the 512 tokens of one device no expert is named more than 192 times, and on some device some expert exactly 192 times.
All inputs are finite; a program needn't handle non-finite values.
Results may differ from the reference program's by a relative error of at most 0.015.
Values may be sent and summed in bfloat16 or wider, within the bound.
No kernel may reach another device: no remote copies, remote signals or barrier semaphores. Data moves between devices by JAX's collectives and lax.ppermute only.
A program may use at most 256 MiB of HBM per device.

```python
import math
import jax
import jax.numpy as jnp
import numpy as np
from jax import lax

D = 512
HEADS = 8
HEAD_DIM = 64
FF = 2048
TASKS = 30
TOP = 2
TOK_DEV = 512
LONG = 256
EXPERTS = 8
SENTS = 16
PACKS = 32
TOKENS = 16384
CAP = 192


def place_ends(result, own_key, smallest, high):
    dims = result.shape
    index_at = [jax.random.randint(jax.random.fold_in(own_key, axis), (), 0, dims[axis]) for axis in range(len(dims))]
    result = result.at[tuple(index_at)].set(smallest)
    longest = dims.index(max(dims))
    index_at[longest] = (index_at[longest] + 1) % dims[longest]
    return result.at[tuple(index_at)].set(high)


def levels(rng, extent, split, low, high):
    def one(axis_at, blocks):
        steps = jax.random.uniform(jax.random.fold_in(jax.random.fold_in(rng, 6), axis_at), (blocks,), jnp.float32, low / len(split), high / len(split))
        return jnp.repeat(jnp.exp(steps), extent[axis_at] // blocks).reshape((-1,) + (1,) * (len(extent) - axis_at - 1))

    factor_of = one(*split[0])
    for cut in split[1:]:
        factor_of = factor_of * one(*cut)
    return factor_of


def split_up(count, total, most, skew):
    portions = [(1 << 20) // math.isqrt(grade ** skew) + 1 for grade in range(2, count + 1)]
    rest, counts = total - most - (count - 1), [1] * (count - 1)
    while rest > 0:
        movable = [i for i in range(count - 1) if counts[i] < most]
        pool, left = sum([portions[i] for i in movable]), rest
        for i in movable:
            more = min(most - counts[i], max(1, left * portions[i] // pool), rest)
            counts[i] = counts[i] + more
            rest = rest - more
    return np.array([most] + counts)


def uneven(stream_key, count, total, bound, slope):
    if count == 2:
        one = jax.random.randint(stream_key, (), max(1, total - bound), min(bound, total - 1) + 1)
        return jnp.stack([one, total - one])
    sizes = jnp.asarray(split_up(count, total, bound, slope), jnp.int32)
    twos = (count - 1) // 2
    source_of, sink = sizes[1:1 + 2 * twos:2], sizes[2:2 + 2 * twos:2]
    margin = jnp.minimum(source_of - 1, bound - sink)
    moved = jax.random.randint(jax.random.fold_in(stream_key, 1), (twos,), 0, 1 << 20) % (margin + 1)
    sizes = sizes.at[1:1 + 2 * twos:2].set(source_of - moved).at[2:2 + 2 * twos:2].set(sink + moved)
    return sizes[jax.random.permutation(jax.random.fold_in(stream_key, 2), count)]


def deal_out(stream_key, own, number, rows, amount, top, most, slope):
    sequence = jax.random.permutation(stream_key, amount)
    crowded, usual = load_shares(amount, rows * top, most, slope, True), load_shares(amount, rows * top, most, slope, False)
    places = jnp.arange(amount)

    def named(sizes, turn):
        used = int((sizes > 0).sum())
        fixed = max(1, used // 4)
        moved = fixed + (places - fixed + turn * (used - fixed)) % max(1, amount - fixed)
        return jnp.zeros((amount,), jnp.int32).at[sequence[jnp.where(places < fixed, places, moved)]].set(jnp.asarray(sizes, jnp.int32))

    sizes = jnp.where(number % 4 == 0, named(crowded, number // 4), named(usual, number - number // 4 - 1))
    mixed = jax.random.permutation(jax.random.fold_in(own, 3), amount)
    donor, receiver = mixed[0:amount // 2 * 2:2], mixed[1:amount // 2 * 2:2]
    room = jnp.minimum(sizes[donor] - 1, most - sizes[receiver]) // 2
    room = jnp.where((donor == sequence[0]) | (receiver == sequence[0]) | (sizes[receiver] == 0), 0, jnp.maximum(room, 0))
    moved = jax.random.randint(jax.random.fold_in(own, 4), (amount // 2,), 0, 1 << 20) % (room + 1)
    sizes = sizes.at[donor].add(-moved).at[receiver].add(moved)
    members = jnp.searchsorted(jnp.cumsum(sizes), jnp.arange(rows * top), side="right").astype(jnp.int32)
    grid = members.reshape(top, rows).T
    grid = grid[jax.random.permutation(jax.random.fold_in(own, 1), rows)]
    turn = jax.random.randint(jax.random.fold_in(own, 2), (rows, 1), 0, top)
    return jnp.take_along_axis(grid, (jnp.arange(top)[None, :] + turn) % top, axis=1)


def load_shares(count, total, most, lean, full):
    loads = [(1 << 20) // math.isqrt(rank ** lean) + 1 for rank in range(1, count + 1)]
    largest = most if full else min(most, max(-(-total // count), total * loads[0] // sum(loads)))
    least = 1 if total - largest >= count - 1 else 0
    counts, surplus = [largest] + [least] * (count - 1), total - largest - least * (count - 1)
    while surplus > 0:
        candidates = [i for i in range(1, count) if counts[i] < largest] or [i for i in range(1, count) if counts[i] < most]
        mass, remaining = sum([loads[i] for i in candidates]), surplus
        for i in candidates:
            extra = min(most - counts[i], max(1, remaining * loads[i] // mass), surplus)
            counts[i] = counts[i] + extra
            surplus = surplus - extra
    return np.array(counts)


def gaussian(stream_key, dims, scale, reach, split=(), held_as=jnp.bfloat16):
    array = jax.random.normal(stream_key, dims, jnp.float32) * scale
    if len(split) > 0:
        array = levels(stream_key, dims, split, -0.22, 0.18) * array
    return jnp.clip(array, min=-reach, max=reach).astype(held_as)


def setup_inputs(seed: int = 0) -> dict:
    streams_of = jax.random.split(jax.random.key(seed), 15)
    tokens = gaussian(streams_of[0], (TOKENS, D), 1.0, 6.0, ((0, 32),))
    lengths = jax.vmap(lambda own: uneven(own, SENTS, TOK_DEV, LONG, 2))(jax.random.split(streams_of[1], PACKS)).reshape((PACKS, SENTS)).astype(jnp.int32)
    task_ids = place_ends(jax.random.randint(streams_of[2], (PACKS, SENTS), 0, TASKS), jax.random.fold_in(streams_of[2], 1), 0, TASKS - 1).astype(jnp.int32)
    routes_keys = jax.random.split(jax.random.fold_in(streams_of[3], 1), TOKENS // TOK_DEV)
    routes_turns = jax.random.permutation(jax.random.fold_in(streams_of[3], 3), TOKENS // TOK_DEV)
    routes = jax.vmap(lambda own, number: deal_out(jax.random.fold_in(streams_of[3], 2), own, number, TOK_DEV, EXPERTS, TOP, CAP, 1))(routes_keys, routes_turns).reshape((TOKENS, TOP))
    w_qkv = gaussian(streams_of[4], (D, 3 * D), D ** -0.5, 0.25, ((0, 32),))
    w_attn_out = gaussian(streams_of[5], (D, D), (D // 16) ** -0.5, 1.0, ((0, 32),))
    w_gate = gaussian(streams_of[6], (D, TASKS * EXPERTS), (2 * D) ** -0.5, 0.1875, ((0, 32),))
    ln1_gain = jnp.clip(1.0 + 0.1 * jax.random.normal(streams_of[7], (D,), jnp.float32), 0.5, 1.5).astype(jnp.bfloat16)
    ln1_bias = gaussian(streams_of[8], (D,), 0.2, 1.0, ((0, 32),))
    ln2_gain = jnp.clip(1.0 + 0.1 * jax.random.normal(streams_of[9], (D,), jnp.float32), 0.5, 1.5).astype(jnp.bfloat16)
    ln2_bias = gaussian(streams_of[10], (D,), 0.2, 1.0, ((0, 32),))
    w_in = gaussian(streams_of[11], (EXPERTS, D, FF), D ** -0.5, 0.25, ((0, 8), (2, 4)))
    w_out = gaussian(streams_of[12], (EXPERTS, FF, D), (FF // 4) ** -0.5, 0.25, ((0, 8), (1, 4)))
    cotangent = gaussian(streams_of[13], (TOKENS, D), 1.0, 6.0, ((0, 32),))
    return dict(tokens=tokens, lengths=lengths, task_ids=task_ids, routes=routes, w_qkv=w_qkv, w_attn_out=w_attn_out, w_gate=w_gate, ln1_gain=ln1_gain, ln1_bias=ln1_bias, ln2_gain=ln2_gain, ln2_bias=ln2_bias, w_in=w_in, w_out=w_out, cotangent=cotangent)


@jax.custom_vjp
def low(v):
    return lax.optimization_barrier(v.astype(jnp.bfloat16)).astype(jnp.float32)

@jax.custom_vjp
def low_back(v):
    return v

def low_keep(v):
    return (low(v), None)

def low_pass(kept, grad):
    return (grad,)

def back_keep(v):
    return (v, None)

def back_low(kept, grad):
    return (low(grad),)
low.defvjp(low_keep, low_pass)
low_back.defvjp(back_keep, back_low)
EPS = 1e-05
HIGH = lax.Precision.HIGHEST
NEG_FILL = -1e+30

def layer_norm(values, gain, offset):
    middle = lax.optimization_barrier(jnp.mean(values, axis=-1, keepdims=True))
    centred = values - middle
    spread = lax.optimization_barrier(jnp.mean(centred * centred, axis=-1, keepdims=True))
    return centred * lax.rsqrt(spread + EPS) * gain + offset

def pack_layout(lengths, task_ids, positions):
    sentence_ends = jnp.cumsum(lengths).astype(jnp.int32)
    sentence = lax.optimization_barrier(jnp.sum((positions[:, None] >= sentence_ends[None, :]).astype(jnp.int32), axis=1)).astype(jnp.int32)
    picked = sentence[:, None] == jnp.arange(lengths.shape[0], dtype=jnp.int32)[None, :]
    task_tok = lax.optimization_barrier(jnp.sum(jnp.where(picked, task_ids[None, :], 0), axis=1)).astype(jnp.int32)
    return (sentence, task_tok)

def slot_layout(routes, experts):
    flat_routes = routes.reshape(-1)
    onehot = (flat_routes[:, None] == jnp.arange(experts, dtype=jnp.int32)[None, :]).astype(jnp.int32)
    earlier = jnp.cumsum(onehot, axis=0).astype(jnp.int32) - onehot
    slot_place = lax.optimization_barrier(jnp.sum(earlier * onehot, axis=1)).astype(jnp.int32)
    return (flat_routes, slot_place)

def attention(tokens, sentence, w_qkv, w_attn_out, gain_one, bias_one):

    def one_pack(items):
        pack_rows, pack_sentence = items
        normed = low(layer_norm(pack_rows, gain_one, bias_one))
        project = low_back(low(jnp.dot(normed, w_qkv, precision=HIGH)))
        queries = project[:, :D].reshape(TOK_DEV, HEADS, HEAD_DIM)
        keys_all = project[:, D:2 * D].reshape(TOK_DEV, HEADS, HEAD_DIM)
        values_all = project[:, 2 * D:].reshape(TOK_DEV, HEADS, HEAD_DIM)
        scores = low_back(jnp.einsum('qhd,khd->hqk', queries, keys_all, precision=HIGH) * HEAD_DIM ** (-0.5))
        same_sentence = pack_sentence[:, None] == pack_sentence[None, :]
        scores = jnp.where(same_sentence[None], scores, NEG_FILL)
        highest = lax.optimization_barrier(jnp.max(scores, axis=-1, keepdims=True))
        expo = jnp.exp(scores - highest)
        probs = low(expo / lax.optimization_barrier(jnp.sum(expo, axis=-1, keepdims=True)))
        heads = jnp.einsum('hqk,khd->qhd', probs, values_all, precision=HIGH).reshape(TOK_DEV, D)
        heads = low_back(low(heads))
        return low_back(jnp.dot(heads, w_attn_out, precision=HIGH))
    packed = tokens.reshape(PACKS, TOK_DEV, D)
    return lax.map(jax.checkpoint(one_pack), (packed, sentence)).reshape(TOKENS, D)

def expert_apply(items):
    rows_in, weight_in, weight_out = items
    pre = low_back(jnp.dot(rows_in, weight_in, precision=HIGH))
    activated = low(jax.nn.gelu(pre))
    return low_back(low(jnp.dot(activated, weight_out, precision=HIGH)))

def forward(tokens, w_qkv, w_attn_out, w_gate, gain_one, bias_one, gain_two, bias_two, w_in, w_out, sentence, column, target, source, filled):
    attended = attention(tokens, sentence, w_qkv, w_attn_out, gain_one, bias_one)
    hidden_one = tokens + attended
    routed_in = low(layer_norm(hidden_one, gain_two, bias_two))
    logits_all = low_back(jnp.dot(routed_in, w_gate, precision=HIGH))
    chosen = jnp.take_along_axis(logits_all, column, axis=1)
    gates = jax.nn.softmax(chosen, axis=1)
    expert_rows = low_back(routed_in[source] * filled[:, None]).reshape(EXPERTS, PACKS * CAP, D)
    expert_out = lax.map(jax.checkpoint(expert_apply), (expert_rows, w_in, w_out)).reshape(-1, D)
    paired = expert_out[target].reshape(TOKENS, TOP, D)
    return hidden_one + lax.optimization_barrier(jnp.sum(gates[:, :, None] * paired, axis=1))

def reference(tokens, lengths, task_ids, routes, w_qkv, w_attn_out, w_gate, ln1_gain, ln1_bias, ln2_gain, ln2_bias, w_in, w_out, cotangent):
    positions = jnp.arange(TOK_DEV, dtype=jnp.int32)
    sentence, task_pack = jax.vmap(lambda length_row, task_row: pack_layout(length_row, task_row, positions))(lengths, task_ids)
    task_tok = task_pack.reshape(-1)
    expert_of, slot_place = jax.vmap(lambda route_block: slot_layout(route_block, EXPERTS))(routes.reshape(PACKS, TOK_DEV, TOP))
    expert_of = expert_of.reshape(-1)
    slot_place = slot_place.reshape(-1)
    pair_ids = jnp.arange(TOKENS * TOP, dtype=jnp.int32)
    device_of = pair_ids // (TOK_DEV * TOP)
    per_expert = PACKS * CAP
    target = (expert_of * per_expert + device_of * CAP + slot_place).astype(jnp.int32)
    source = jnp.zeros((EXPERTS * per_expert,), jnp.int32).at[target].set(pair_ids // TOP)
    filled = jnp.zeros((EXPERTS * per_expert,), jnp.float32).at[target].set(1.0)
    column = (task_tok[:, None] * EXPERTS + routes).astype(jnp.int32)
    floats = (tokens.astype(jnp.float32), w_qkv.astype(jnp.float32), w_attn_out.astype(jnp.float32), w_gate.astype(jnp.float32), ln1_gain.astype(jnp.float32), ln1_bias.astype(jnp.float32), ln2_gain.astype(jnp.float32), ln2_bias.astype(jnp.float32), w_in.astype(jnp.float32), w_out.astype(jnp.float32))

    def closed(*params):
        return forward(*params, sentence, column, target, source, filled)
    mixed, pullback = jax.vjp(closed, *floats)
    grads = pullback(cotangent.astype(jnp.float32))
    return (mixed.astype(jnp.bfloat16), grads[0], grads[1], grads[2], grads[3], grads[4], grads[5], grads[6], grads[7], grads[8], grads[9])
```

```python
import functools

import jax
import jax.numpy as jnp
from jax import lax
from jax.experimental import pallas as pl
from jax.experimental.pallas import tpu as pltpu
from jax.sharding import PartitionSpec as P

HEADS = 8
HEAD_DIM = 64
EPS = 1e-05
NEG_FILL = -1e30
LANES = 128
BOTH = ("expert", "hidden")
F32 = jnp.float32
BF16 = jnp.bfloat16
VMEM_LIMIT = 56 * 1024 * 1024


def mm(left, right):
    return jnp.dot(left, right, preferred_element_type=F32)


def contract_last(left, right):
    return lax.dot_general(left, right, (((1,), (1,)), ((), ())), preferred_element_type=F32)


def contract_first(left, right):
    return lax.dot_general(left, right, (((0,), (0,)), ((), ())), preferred_element_type=F32)


def iota(shape, axis):
    return lax.broadcasted_iota(jnp.int32, shape, axis)


def iota_f(shape, axis):
    return iota(shape, axis).astype(F32)


def lane_sum(values):
    return jnp.sum(values, axis=1, keepdims=True)


def row_sum(values):
    return jnp.sum(values, axis=0, keepdims=True)


def norm_parts(values):
    middle = jnp.mean(values, axis=-1, keepdims=True)
    centred = values - middle
    spread = jnp.mean(centred * centred, axis=-1, keepdims=True)
    inverse = lax.rsqrt(spread + EPS)
    return centred * inverse, inverse


def norm_back(unit, inverse, gain, grad):
    scaled = grad * gain
    mean_one = jnp.mean(scaled, axis=-1, keepdims=True)
    mean_two = jnp.mean(scaled * unit, axis=-1, keepdims=True)
    return inverse * (scaled - mean_one - unit * mean_two)


def round_up(value, step):
    return (value + step - 1) // step * step


def call(kernel, outs, scratch, args, flops, smem=()):
    def spec(at):
        return pl.BlockSpec(memory_space=pltpu.SMEM if at in smem else pltpu.VMEM)

    touched = sum(a.size * a.dtype.itemsize for a in args) + sum(
        o.size * o.dtype.itemsize for o in jax.tree.leaves(outs)
    )
    return pl.pallas_call(
        kernel,
        out_shape=outs,
        in_specs=[spec(at) for at in range(len(args))],
        out_specs=jax.tree.map(lambda _: pl.BlockSpec(memory_space=pltpu.VMEM), outs),
        scratch_shapes=scratch,
        compiler_params=pltpu.CompilerParams(vmem_limit_bytes=VMEM_LIMIT),
        cost_estimate=pl.CostEstimate(flops=flops, bytes_accessed=touched, transcendentals=0),
    )(*args)


def shape(dims, dtype):
    return jax.ShapeDtypeStruct(dims, dtype)


def prep_kernel(experts, cap, lens_ref, tasks_ref, routes_ref, cot_ref, side_ref, rows_ref, sent_ref):
    count = routes_ref.shape[0]
    sents = lens_ref.shape[1]
    lens = lens_ref[...].astype(F32)
    tasks = tasks_ref[...].astype(F32)
    down, across = iota((sents, sents), 0), iota((sents, sents), 1)
    ends_col = lane_sum(jnp.where(across <= down, lens, 0.0))
    ends_row = row_sum(jnp.where(across == down, ends_col, 0.0))
    passed = jnp.where(iota_f((count, sents), 0) >= ends_row, 1.0, 0.0)
    sentence = lane_sum(passed)
    task = lane_sum(jnp.where(iota_f((count, sents), 1) == sentence, tasks, 0.0))
    routes = routes_ref[...].astype(F32)
    first, second = routes[:, 0:1], routes[:, 1:2]
    lane_e = iota_f((count, experts), 1)
    hot_one = jnp.where(lane_e == first, 1.0, 0.0)
    hot_two = jnp.where(lane_e == second, 1.0, 0.0)
    before = jnp.where(iota((count, count), 1) < iota((count, count), 0), 1.0, 0.0).astype(BF16)
    earlier = mm(before, (hot_one + hot_two).astype(BF16))
    target_one = first * cap + lane_sum(earlier * hot_one)
    target_two = second * cap + lane_sum(earlier * hot_two)
    lane = iota((count, LANES), 1)
    side = jnp.where(lane == 0, target_one, 0.0)
    side = jnp.where(lane == 1, target_two, side)
    side = jnp.where(lane == 2, task * experts + first, side)
    side = jnp.where(lane == 3, task * experts + second, side)
    side = jnp.where(lane == 4, sentence, side)
    side_ref[...] = side
    turned = jnp.transpose(side)
    rows_ref[...] = turned[0:8, :]
    one_row, two_row = turned[0:1, :], turned[1:2, :]
    cot = cot_ref[...]
    for e in range(experts):
        at = iota_f((cap, count), 0) + float(e * cap)
        pick = jnp.where((at == one_row) | (at == two_row), 1.0, 0.0).astype(BF16)
        sent_ref[e] = mm(pick, cot).astype(BF16)


class Groups:
    def __init__(self, devices):
        bits = devices.bit_length() - 1
        mid = (bits - 1) // 2
        self.near = [1]
        self.mid = self.masks(1, mid)
        self.far = self.masks(1 + mid, bits - 1 - mid)
        self.devices = devices

    @staticmethod
    def masks(low, width):
        return [m << low for m in range(1 << width)]

    def owners(self):
        return [[n | b | c for c in self.far] for n in (0, 1) for b in self.mid]

    def swap(self, value, mask):
        return lax.ppermute(value, BOTH, [(i, i ^ mask) for i in range(self.devices)])

    def gather(self, shard):
        far = jnp.concatenate([shard] + [self.swap(shard, m) for m in self.far[1:]], axis=0)
        mid = [far] + [self.swap(far, m) for m in self.mid[1:]]
        return mid + [self.swap(block, 1) for block in mid]


def place_blocks(owners, me, block_refs, full_ref):
    if len(block_refs) == 1:
        full_ref[...] = block_refs[0][...]
        return
    for block_ref, masks in zip(block_refs, owners):
        rows = block_ref.shape[0] // len(masks)
        for i, mask in enumerate(masks):
            at = pl.multiple_of((me ^ mask) * rows, rows)
            full_ref[pl.ds(at, rows), :] = block_ref[i * rows : (i + 1) * rows, :]


def take_blocks(owners, me, full_ref, keep_ref, send_ref):
    half = len(owners) // 2
    for n, out_ref in ((0, keep_ref), (1, send_ref)):
        for b, masks in enumerate(owners[n * half : (n + 1) * half]):
            rows = full_ref.shape[0] // (len(owners) * len(masks))
            for i, mask in enumerate(masks):
                at = pl.multiple_of((me ^ mask) * rows, rows)
                to = (b * len(masks) + i) * rows
                out_ref[to : to + rows, :] = full_ref[pl.ds(at, rows), :].astype(out_ref.dtype)


def add_kernel(parts, keep_ref, *refs):
    got, outs = refs[: len(refs) - parts], refs[len(refs) - parts :]
    rows = outs[0].shape[0]
    for i, out_ref in enumerate(outs):
        span = slice(i * rows, (i + 1) * rows)
        total = keep_ref[span, :]
        for ref in got:
            total = total + ref[span, :].astype(F32)
        out_ref[...] = total.astype(out_ref.dtype)


def add_parts(keep, got, parts):
    rows, columns = keep.shape
    outs = [shape((rows // parts, columns), F32 if i == 0 else BF16) for i in range(parts)]
    return call(functools.partial(add_kernel, parts), outs, [], [keep] + got, rows * columns * len(got))


def sum_to_owner(groups, keep, send):
    blocks = add_parts(keep, [groups.swap(send, 1)], len(groups.mid))
    got = [groups.swap(b, m) for b, m in zip(blocks[1:], groups.mid[1:])]
    blocks = add_parts(blocks[0], got, len(groups.far))
    got = [groups.swap(b, m) for b, m in zip(blocks[1:], groups.far[1:])]
    return add_parts(blocks[0], got, 1)[0]


def gain_rows(full_ref, start, gate_columns):
    tile = start + gate_columns // LANES * LANES
    lane = gate_columns % LANES
    turned = jnp.transpose(full_ref[:, tile : tile + LANES].astype(F32))
    return [turned[lane + i : lane + i + 1, :] for i in range(4)]


def forward_kernel(
    cfg, me_ref, side_ref, rows_ref, tokens_ref, *refs
):
    blocks = refs[: cfg.blocks]
    outs = refs[cfg.blocks :]
    full_ref, proj_ref, heads_ref, lse_ref, hidden_ref, gates_ref = outs[:6]
    send_refs = outs[6 : 6 + cfg.experts]
    bias_ref, routed_ref = outs[6 + cfg.experts :]
    count, width = tokens_ref.shape
    me = me_ref[0]
    place_blocks(cfg.owners, me, blocks, full_ref)
    gain_one, bias_one, gain_two, bias_two = gain_rows(full_ref, 4 * width, cfg.gate_columns)
    chunk = 128
    for c in range(count // chunk):
        span = slice(c * chunk, (c + 1) * chunk)
        unit, _ = norm_parts(tokens_ref[span, :].astype(F32))
        routed_ref[span, :] = (unit * gain_one + bias_one).astype(BF16)
        bias_ref[span, :] = jnp.where(
            side_ref[span, 4:5] == rows_ref[4:5, :], 0.0, NEG_FILL
        )
    proj_ref[...] = mm(routed_ref[...], full_ref[:, : 3 * width]).astype(BF16)
    lse_ref[...] = jnp.zeros_like(lse_ref)
    lane = iota((1, LANES), 1)
    scale = HEAD_DIM ** (-0.5)
    block = 256

    def slab(i, carry):
        off = pl.multiple_of(i * LANES, LANES)
        keys = proj_ref[:, pl.ds(width + off, LANES)]
        values = proj_ref[:, pl.ds(2 * width + off, LANES)]
        halves = []
        for half in (0, 1):
            mine = jnp.where(lane // HEAD_DIM == half, 1.0, 0.0).astype(BF16)
            halves.append((keys * mine, values * mine))
        for r in range(count // block):
            span = slice(r * block, (r + 1) * block)
            queries = proj_ref[span, pl.ds(off, LANES)]
            total = jnp.zeros((block, LANES), F32)
            logs = lse_ref[span, :]
            for half, (key_half, value_half) in enumerate(halves):
                scores = contract_last(queries, key_half) * scale + bias_ref[span, :]
                highest = jnp.max(scores, axis=1, keepdims=True)
                expo = jnp.exp(scores - highest)
                sums = lane_sum(expo)
                probs = (expo * (1.0 / sums)).astype(BF16)
                total = total + mm(probs, value_half)
                logs = jnp.where(lane == 2 * i + half, highest + jnp.log(sums), logs)
            heads_ref[span, pl.ds(off, LANES)] = total.astype(BF16)
            lse_ref[span, :] = logs
        return carry

    lax.fori_loop(0, width // LANES, slab, 0)
    for c in range(count // chunk):
        span = slice(c * chunk, (c + 1) * chunk)
        attended = mm(heads_ref[span, :], full_ref[:, 3 * width : 4 * width])
        hidden = tokens_ref[span, :].astype(F32) + attended
        hidden_ref[span, :] = hidden
        unit, _ = norm_parts(hidden)
        routed = (unit * gain_two + bias_two).astype(BF16)
        routed_ref[span, :] = routed
        logits = mm(routed, full_ref[:, 4 * width :])
        column = iota_f(logits.shape, 1)
        one = lane_sum(jnp.where(column == side_ref[span, 2:3], logits, 0.0))
        two = lane_sum(jnp.where(column == side_ref[span, 3:4], logits, 0.0))
        top = jnp.maximum(one, two)
        expo_one, expo_two = jnp.exp(one - top), jnp.exp(two - top)
        both = expo_one + expo_two
        gates_ref[span, :] = jnp.where(
            lane == 0, expo_one / both, jnp.where(lane == 1, expo_two / both, 0.0)
        )
    cap = cfg.cap
    mine = me // cfg.hidden
    routed = routed_ref[...]
    gate_lanes = round_up(cap, LANES)
    for k in range(cfg.experts):
        base = ((mine ^ k) * cap).astype(F32)
        at = iota_f((cap, count), 0) + base
        pick = (at == rows_ref[0:1, :]) | (at == rows_ref[1:2, :])
        send_refs[k][0:cap, :] = mm(jnp.where(pick, 1.0, 0.0).astype(BF16), routed).astype(BF16)
        slot = iota_f((count, gate_lanes), 1) + base
        row = row_sum(
            jnp.where(slot == side_ref[:, 0:1], gates_ref[:, 0:1], 0.0)
            + jnp.where(slot == side_ref[:, 1:2], gates_ref[:, 1:2], 0.0)
        )
        put_split(send_refs[k], cap, row)


def put_split(ref, cap, row):
    extra = ref.shape[0] - cap
    high = row.astype(BF16).astype(F32)
    down = iota((extra, row.shape[1]), 0)
    both = jnp.where(down == 0, high, jnp.where(down == 1, row - high, 0.0))
    ref[cap:, :] = jnp.zeros((extra, ref.shape[1]), BF16)
    ref[cap:, 0 : row.shape[1]] = both.astype(BF16)


def take_split(ref, cap, lanes):
    both = ref[cap:, 0:lanes].astype(F32)
    return both[0:1, :] + both[1:2, :]


def expert_kernel(cfg, me_ref, cot_ref, *refs):
    n, h = cfg.experts, cfg.hidden
    row_refs, in_refs, out_refs = refs[:n], refs[n : n + h], refs[n + h : n + 2 * h]
    outs = refs[n + 2 * h :]
    result_ref, back_refs = outs[0], outs[1 : 1 + n]
    grad_in_refs = outs[1 + n : 1 + n + h]
    grad_out_refs = outs[1 + n + h : 1 + n + 2 * h]
    rows_all, pairs_all, rows_turned, pairs_turned, result_sum, back_sum, act_all, pre_all = outs[
        1 + n + 2 * h :
    ]
    cap = cfg.cap
    total, width = rows_all.shape
    mine = me_ref[0] // h
    gate_lanes = round_up(cap, LANES)
    eye = iota((cap, gate_lanes), 0) == iota((cap, gate_lanes), 1)
    for k in range(n):
        span = slice(k * cap, (k + 1) * cap)
        rows_all[span, :] = row_refs[k][0:cap, :]
        gate = lane_sum(jnp.where(eye, take_split(row_refs[k], cap, gate_lanes), 0.0))
        pairs_all[span, :] = (gate * cot_ref[mine ^ k].astype(F32)).astype(BF16)
    rows_turned[...] = jnp.transpose(rows_all[...])
    pairs_turned[...] = jnp.transpose(pairs_all[...])
    tile = 256
    root = 0.7978845608028654
    cubic = 0.044715
    for b in range(h):
        w_in, w_out = in_refs[b], out_refs[b]

        def step(m, carry):
            span = pl.ds(pl.multiple_of(m * tile, tile), tile)
            pre = mm(rows_all[span, :], w_in[...])
            square = pre * pre
            bent = jnp.tanh(pre * (root + (root * cubic) * square))
            upper = 0.5 + 0.5 * bent
            act = pre * upper
            slope = upper + act * (1.0 - upper) * (2.0 * root + (6.0 * root * cubic) * square)
            act_low = act.astype(BF16)
            act_all[span, :] = act_low
            act_grad = contract_last(pairs_all[span, :], w_out[...])
            pre_grad = (act_grad * slope).astype(BF16)
            pre_all[span, :] = pre_grad
            result = mm(act_low, w_out[...])
            back = contract_last(pre_grad, w_in[...])
            if b == 0:
                result_sum[span, :] = result
                back_sum[span, :] = back
            else:
                result_sum[span, :] += result
                back_sum[span, :] += back
            return carry

        lax.fori_loop(0, total // tile, step, 0)
        grad_in_refs[b][...] = mm(rows_turned[...], pre_all[...]).astype(grad_in_refs[b].dtype)
        grad_out_refs[b][...] = mm(pairs_turned[...], act_all[...]).astype(grad_out_refs[b].dtype)
    for k in range(n):
        span = slice(k * cap, (k + 1) * cap)
        result = result_sum[span, :].astype(BF16)
        result_ref[mine ^ k] = result
        back_refs[k][0:cap, :] = back_sum[span, :].astype(BF16)
        dots = lane_sum(cot_ref[mine ^ k].astype(F32) * result.astype(F32))
        put_split(back_refs[k], cap, row_sum(jnp.where(eye, dots, 0.0)))


def turn_add_kernel(own_in, own_out, got_in, got_out, more_in, more_out, sum_in, sum_out):
    sum_in[...] = own_in[...] + got_in[...].astype(F32) + more_in[...].astype(F32)
    whole = own_out[...] + got_out[...].astype(F32) + more_out[...].astype(F32)
    sum_out[...] = jnp.transpose(whole)


def backward_kernel(cfg, me_ref, side_ref, hidden_ref, gates_ref, cot_ref, heads_ref, full_ref, *refs):
    n, cap = cfg.experts, cfg.cap
    back_refs = refs[:n]
    hidden_grad_ref, heads_grad_ref = refs[n : n + 2]
    dense = refs[n + 2 : len(refs) - 4]
    routed_sum, dense_ref, routed_ref, logits_ref = refs[len(refs) - 4 :]
    count, width = hidden_ref.shape
    me = me_ref[0]
    mine = me // cfg.hidden
    gain_one, bias_one, gain_two, bias_two = gain_rows(full_ref, 4 * width, cfg.gate_columns)
    gate_lanes = round_up(cap, LANES)
    one, two = side_ref[:, 0:1], side_ref[:, 1:2]
    dot_one = jnp.zeros((count, 1), F32)
    dot_two = jnp.zeros((count, 1), F32)
    for k in range(n):
        base = ((mine ^ k) * cap).astype(F32)
        slot = iota_f((count, cap), 1) + base
        pick = jnp.where((slot == one) | (slot == two), 1.0, 0.0).astype(BF16)
        part = mm(pick, back_refs[k][0:cap, :])
        if k == 0:
            routed_sum[...] = part
        else:
            routed_sum[...] += part
        lane_at = iota_f((count, gate_lanes), 1)
        slot = jnp.where(lane_at < cap, lane_at + base, -1.0)
        dots = take_split(back_refs[k], cap, gate_lanes)
        dot_one = dot_one + lane_sum(jnp.where(slot == one, dots, 0.0))
        dot_two = dot_two + lane_sum(jnp.where(slot == two, dots, 0.0))
    gate_one, gate_two = gates_ref[:, 0:1], gates_ref[:, 1:2]
    shared = gate_one * dot_one + gate_two * dot_two
    chosen_one = gate_one * (dot_one - shared)
    chosen_two = gate_two * (dot_two - shared)
    gate_full = full_ref[:, 4 * width :]
    chunk = 128
    gain_sum = jnp.zeros((1, width), F32)
    bias_sum = jnp.zeros((1, width), F32)
    for c in range(count // chunk):
        span = slice(c * chunk, (c + 1) * chunk)
        column = iota_f((chunk, cfg.gate_lanes), 1)
        logits = jnp.where(column == side_ref[span, 2:3], chosen_one[span], 0.0) + jnp.where(
            column == side_ref[span, 3:4], chosen_two[span], 0.0
        )
        logits = logits.astype(BF16)
        logits_ref[span, :] = logits
        routed_grad = routed_sum[span, :] + contract_last(logits, gate_full)
        unit, inverse = norm_parts(hidden_ref[span, :])
        routed_ref[span, :] = (unit * gain_two + bias_two).astype(BF16)
        gain_sum = gain_sum + row_sum(routed_grad * unit)
        bias_sum = bias_sum + row_sum(routed_grad)
        hidden_grad = cot_ref[span, :].astype(F32) + norm_back(unit, inverse, gain_two, routed_grad)
        hidden_grad_ref[span, :] = hidden_grad
        low = hidden_grad.astype(BF16)
        routed_sum[span, :] = hidden_grad
        heads_grad_ref[span, :] = contract_last(low, full_ref[:, 3 * width : 4 * width]).astype(BF16)
    dense_ref[:, 0:width] = contract_first(heads_ref[...], routed_sum[...].astype(BF16))
    dense_ref[:, width:] = contract_first(routed_ref[...], logits_ref[...])
    tile = width + cfg.gate_columns // LANES * LANES
    lane = cfg.gate_columns % LANES
    dense_ref[:, tile : tile + LANES] += rows_to_lanes(gain_sum, bias_sum, lane + 2)
    put_dense(cfg, me, dense_ref, dense)


def rows_to_lanes(first, second, lane):
    down = iota((LANES, first.shape[1]), 0)
    return jnp.transpose(jnp.where(down == lane, first, jnp.where(down == lane + 1, second, 0.0)))


def put_dense(cfg, me, dense_ref, outs):
    if len(outs) == 1:
        outs[0][...] = dense_ref[...]
    else:
        take_blocks(cfg.owners, me, dense_ref, *outs)


def attention_back_kernel(
    cfg, me_ref, side_ref, rows_ref, tokens_ref, proj_ref, lse_ref, heads_grad_ref, hidden_grad_ref, full_ref, *refs
):
    grad_ref = refs[0]
    dense = refs[1 : len(refs) - 4]
    bias_ref, low_ref, qkv_ref, dense_ref = refs[len(refs) - 4 :]
    count, width = tokens_ref.shape
    me = me_ref[0]
    gain_one, bias_one, gain_two, bias_two = gain_rows(full_ref, 4 * width, cfg.gate_columns)
    chunk = 128
    for c in range(count // chunk):
        span = slice(c * chunk, (c + 1) * chunk)
        unit, _ = norm_parts(tokens_ref[span, :].astype(F32))
        low_ref[span, :] = (unit * gain_one + bias_one).astype(BF16)
        bias_ref[span, :] = jnp.where(
            side_ref[span, 4:5] == rows_ref[4:5, :], 0.0, NEG_FILL
        )
    lane = iota((1, LANES), 1)
    scale = HEAD_DIM ** (-0.5)

    def slab(i, carry):
        off = pl.multiple_of(i * LANES, LANES)
        queries = proj_ref[:, pl.ds(off, LANES)]
        keys = proj_ref[:, pl.ds(width + off, LANES)]
        values = proj_ref[:, pl.ds(2 * width + off, LANES)]
        grads = heads_grad_ref[:, pl.ds(off, LANES)]
        query_grad = jnp.zeros((count, LANES), F32)
        key_grad = jnp.zeros((count, LANES), F32)
        value_grad = jnp.zeros((count, LANES), F32)
        for half in (0, 1):
            mine = jnp.where(lane // HEAD_DIM == half, 1.0, 0.0).astype(BF16)
            query_half, key_half, grads_half = queries * mine, keys * mine, grads * mine
            logs = lane_sum(jnp.where(lane == 2 * i + half, lse_ref[...], 0.0))
            probs = jnp.exp(contract_last(queries, key_half) * scale + bias_ref[...] - logs)
            prob_grad = contract_last(grads_half, values)
            row_dot = lane_sum(probs * prob_grad)
            score_grad = (probs * (prob_grad - row_dot)).astype(BF16)
            value_grad = value_grad + contract_first(probs.astype(BF16), grads_half)
            query_grad = query_grad + mm(score_grad, key_half)
            key_grad = key_grad + contract_first(score_grad, query_half)
        qkv_ref[:, pl.ds(off, LANES)] = (query_grad * scale).astype(BF16)
        qkv_ref[:, pl.ds(width + off, LANES)] = (key_grad * scale).astype(BF16)
        qkv_ref[:, pl.ds(2 * width + off, LANES)] = value_grad.astype(BF16)
        return carry

    lax.fori_loop(0, width // LANES, slab, 0)
    dense_ref[:, : 3 * width] = contract_first(low_ref[...], qkv_ref[...])
    gain_sum = jnp.zeros((1, width), F32)
    bias_sum = jnp.zeros((1, width), F32)
    for c in range(count // chunk):
        span = slice(c * chunk, (c + 1) * chunk)
        normed_grad = contract_last(qkv_ref[span, :], full_ref[:, : 3 * width])
        unit, inverse = norm_parts(tokens_ref[span, :].astype(F32))
        gain_sum = gain_sum + row_sum(normed_grad * unit)
        bias_sum = bias_sum + row_sum(normed_grad)
        grad_ref[span, :] = hidden_grad_ref[span, :] + norm_back(unit, inverse, gain_one, normed_grad)
    dense_ref[:, 3 * width :] = rows_to_lanes(gain_sum, bias_sum, 0)
    put_dense(cfg, me, dense_ref, dense)


def output_kernel(cfg, side_ref, hidden_ref, gates_ref, result_ref, out_ref):
    cap = cfg.cap
    count = hidden_ref.shape[0]
    total_one = jnp.zeros(hidden_ref.shape, F32)
    total_two = jnp.zeros(hidden_ref.shape, F32)
    for e in range(cfg.experts):
        slot = iota_f((count, cap), 1) + float(e * cap)
        pick_one = jnp.where(slot == side_ref[:, 0:1], 1.0, 0.0).astype(BF16)
        pick_two = jnp.where(slot == side_ref[:, 1:2], 1.0, 0.0).astype(BF16)
        total_one = total_one + mm(pick_one, result_ref[e])
        total_two = total_two + mm(pick_two, result_ref[e])
    mixed = gates_ref[:, 0:1] * total_one + gates_ref[:, 1:2] * total_two
    out_ref[...] = (hidden_ref[...] + mixed).astype(BF16)


class Config:
    pass


def swap_hidden(value, mask):
    size = lax.axis_size("hidden")
    return lax.ppermute(value, "hidden", [(i, i ^ mask) for i in range(size)])


def swap_expert(value, mask):
    size = lax.axis_size("expert")
    return lax.ppermute(value, "expert", [(i, i ^ mask) for i in range(size)])


def gather_hidden(own):
    size = lax.axis_size("hidden")
    blocks = {0: own}
    bit = size // 2
    while bit:
        blocks.update({at ^ bit: swap_hidden(block, bit) for at, block in list(blocks.items())})
        bit //= 2
    return [blocks[i] for i in range(size)]


def sum_hidden(blocks):
    size = len(blocks)
    held = {i: [b] for i, b in enumerate(blocks)}
    bit = 1
    while bit < size:
        low = {i: v for i, v in held.items() if not i & bit}
        for i in low:
            terms = held[i ^ bit]
            value = terms[0] if len(terms) == 1 else sum(t.astype(F32) for t in terms).astype(BF16)
            low[i] = low[i] + [swap_hidden(value, bit)]
        held = low
        bit *= 2
    return held[0]


def body(
    tokens,
    lengths,
    task_ids,
    routes,
    w_qkv,
    w_attn_out,
    w_gate,
    ln1_gain,
    ln1_bias,
    ln2_gain,
    ln2_bias,
    w_in,
    w_out,
    cotangent,
):
    count, width = tokens.shape
    cfg = Config()
    cfg.experts = lax.axis_size("expert")
    cfg.hidden = lax.axis_size("hidden")
    experts, hidden = cfg.experts, cfg.hidden
    cfg.cap = cap = (3 * count * routes.shape[1] + 2 * experts - 1) // (2 * experts)
    cfg.gate_columns = w_gate.shape[1]
    cfg.gate_lanes = round_up(cfg.gate_columns + 4, LANES)
    devices = experts * hidden
    groups = Groups(devices)
    shard_rows = w_qkv.shape[0]
    staged = shard_rows % 16 == 0
    cfg.owners = groups.owners()
    me = (lax.axis_index("expert") * hidden + lax.axis_index("hidden")).astype(jnp.int32)[None]
    extra = 16
    units = w_in.shape[2]
    slots = experts * cap
    wide = 4 * width + cfg.gate_lanes
    one_dot = 2 * count * width * width

    packed = jnp.concatenate(
        [w_qkv, w_attn_out, w_gate]
        + [v[:, None] for v in (ln1_gain, ln1_bias, ln2_gain, ln2_bias)]
        + [jnp.zeros((shard_rows, cfg.gate_lanes - cfg.gate_columns - 4), BF16)],
        axis=1,
    )
    if staged:
        dense_blocks = groups.gather(packed)
    else:
        dense_blocks = [lax.all_gather(packed, BOTH, axis=0, tiled=True)]
    cfg.blocks = len(dense_blocks)

    side, rows, sent_cot = call(
        functools.partial(prep_kernel, experts, cap),
        [
            shape((count, LANES), F32),
            shape((8, count), F32),
            shape((experts, cap, width), BF16),
        ],
        [],
        [lengths, task_ids, routes, cotangent],
        3 * one_dot,
    )
    owned_cot = lax.all_to_all(sent_cot, "expert", split_axis=0, concat_axis=0, tiled=True)
    w_in_blocks = gather_hidden(w_in[0])
    w_out_blocks = gather_hidden(w_out[0])

    outs = call(
        functools.partial(forward_kernel, cfg),
        [
            shape((width, wide), BF16),
            shape((count, 3 * width), BF16),
            shape((count, width), BF16),
            shape((count, LANES), F32),
            shape((count, width), F32),
            shape((count, LANES), F32),
        ]
        + [shape((cap + extra, width), BF16)] * experts,
        [pltpu.VMEM((count, count), F32), pltpu.VMEM((count, width), BF16)],
        [me, side, rows, tokens] + dense_blocks,
        12 * one_dot,
        smem=(0,),
    )
    full, proj, heads, lse, hidden_one, gates = outs[:6]
    send_rows = outs[6:]
    owned_rows = [send_rows[0]] + [swap_expert(send_rows[k], k) for k in range(1, experts)]

    outs = call(
        functools.partial(expert_kernel, cfg),
        [shape((experts, cap, width), BF16)]
        + [shape((cap + extra, width), BF16)] * experts
        + [shape((width, units), F32 if i == 0 else BF16) for i in range(hidden)]
        + [shape((width, units), F32 if i == 0 else BF16) for i in range(hidden)],
        [
            pltpu.VMEM((slots, width), BF16),
            pltpu.VMEM((slots, width), BF16),
            pltpu.VMEM((width, slots), BF16),
            pltpu.VMEM((width, slots), BF16),
            pltpu.VMEM((slots, width), F32),
            pltpu.VMEM((slots, width), F32),
            pltpu.VMEM((slots, units), BF16),
            pltpu.VMEM((slots, units), BF16),
        ],
        [me, owned_cot] + owned_rows + w_in_blocks + w_out_blocks,
        12 * slots * width * units * hidden,
        smem=(0,),
    )
    result, back_rows = outs[0], outs[1 : 1 + experts]
    grad_in_blocks = outs[1 + experts : 1 + experts + hidden]
    grad_out_blocks = outs[1 + experts + hidden :]
    back = [back_rows[0]] + [swap_expert(back_rows[k], k) for k in range(1, experts)]
    returned = lax.all_to_all(result, "expert", split_axis=0, concat_axis=0, tiled=True)

    in_terms = sum_hidden(grad_in_blocks)
    out_terms = sum_hidden(grad_out_blocks)
    if len(in_terms) == 3:
        grad_in, grad_out = call(
            turn_add_kernel,
            [shape((width, units), F32), shape((units, width), F32)],
            [],
            [in_terms[0], out_terms[0], in_terms[1], out_terms[1], in_terms[2], out_terms[2]],
            4 * width * units,
        )
    else:
        grad_in = sum(t.astype(F32) for t in in_terms)
        grad_out = sum(t.astype(F32) for t in out_terms).T

    def dense_shapes(columns):
        if staged:
            half = width // 2
            return [shape((half, columns), F32), shape((half, columns), BF16)]
        return [shape((width, columns), F32)]

    def dense_sum(parts):
        if staged:
            return sum_to_owner(groups, *parts)
        return lax.psum_scatter(parts[0], BOTH, scatter_dimension=0, tiled=True)

    columns_one = width + cfg.gate_lanes
    outs = call(
        functools.partial(backward_kernel, cfg),
        [shape((count, width), F32), shape((count, width), BF16)] + dense_shapes(columns_one),
        [
            pltpu.VMEM((count, width), F32),
            pltpu.VMEM((width, columns_one), F32),
            pltpu.VMEM((count, width), BF16),
            pltpu.VMEM((count, cfg.gate_lanes), BF16),
        ],
        [me, side, hidden_one, gates, cotangent, heads, full] + back,
        7 * one_dot,
        smem=(0,),
    )
    hidden_grad, heads_grad = outs[:2]
    dense_one = dense_sum(outs[2:])

    columns_two = 3 * width + LANES
    outs = call(
        functools.partial(attention_back_kernel, cfg),
        [shape((count, width), F32)] + dense_shapes(columns_two),
        [
            pltpu.VMEM((count, count), F32),
            pltpu.VMEM((count, width), BF16),
            pltpu.VMEM((count, 3 * width), BF16),
            pltpu.VMEM((width, columns_two), F32),
        ],
        [me, side, rows, tokens, proj, lse, heads_grad, hidden_grad, full],
        12 * one_dot,
        smem=(0,),
    )
    grad_tokens = outs[0]
    dense_two = dense_sum(outs[1:])

    layer_out = call(
        functools.partial(output_kernel, cfg),
        shape((count, width), BF16),
        [],
        [side, hidden_one, gates, returned],
        6 * one_dot,
    )
    first = width + cfg.gate_columns
    return (
        layer_out,
        grad_tokens,
        dense_two[:, : 3 * width],
        dense_one[:, :width],
        dense_one[:, width:first],
        dense_two[:, 3 * width],
        dense_two[:, 3 * width + 1],
        dense_one[:, first + 2],
        dense_one[:, first + 3],
        grad_in[None],
        grad_out[None],
    )


def solution(mesh):
    split = P(BOTH, None)
    vector = P(BOTH)
    placed = (split,) * 7 + (vector,) * 4 + (P("expert", None, "hidden"), P("expert", "hidden", None), split)
    return jax.shard_map(
        body,
        mesh=mesh,
        in_specs=placed,
        out_specs=(split,) * 5
        + (vector,) * 4
        + (P("expert", None, "hidden"), P("expert", "hidden", None)),
        check_vma=False,
    )
```

```python
import functools

import jax
import jax.numpy as jnp
from jax import lax
from jax.experimental import pallas as pl
from jax.experimental.pallas import tpu as pltpu
from jax.sharding import PartitionSpec as P

HEADS = 8
HEAD_DIM = 64
EPS = 1e-05
NEG_FILL = -1e30
LANES = 128
BOTH = ("expert", "hidden")
F32 = jnp.float32
BF16 = jnp.bfloat16
VMEM_LIMIT = 56 * 1024 * 1024


def mm(left, right):
    return jnp.dot(left, right, preferred_element_type=F32)


def contract_last(left, right):
    return lax.dot_general(left, right, (((1,), (1,)), ((), ())), preferred_element_type=F32)


def contract_first(left, right):
    return lax.dot_general(left, right, (((0,), (0,)), ((), ())), preferred_element_type=F32)


def iota(shape, axis):
    return lax.broadcasted_iota(jnp.int32, shape, axis)


def iota_f(shape, axis):
    return iota(shape, axis).astype(F32)


def lane_sum(values):
    return jnp.sum(values, axis=1, keepdims=True)


def row_sum(values):
    return jnp.sum(values, axis=0, keepdims=True)


def norm_parts(values):
    middle = jnp.mean(values, axis=-1, keepdims=True)
    centred = values - middle
    spread = jnp.mean(centred * centred, axis=-1, keepdims=True)
    inverse = lax.rsqrt(spread + EPS)
    return centred * inverse, inverse


def norm_back(unit, inverse, gain, grad):
    scaled = grad * gain
    mean_one = jnp.mean(scaled, axis=-1, keepdims=True)
    mean_two = jnp.mean(scaled * unit, axis=-1, keepdims=True)
    return inverse * (scaled - mean_one - unit * mean_two)


def round_up(value, step):
    return (value + step - 1) // step * step


def call(kernel, outs, scratch, args, flops, smem=()):
    def spec(at):
        return pl.BlockSpec(memory_space=pltpu.SMEM if at in smem else pltpu.VMEM)

    touched = sum(a.size * a.dtype.itemsize for a in args) + sum(
        o.size * o.dtype.itemsize for o in jax.tree.leaves(outs)
    )
    got = pl.pallas_call(
        kernel,
        out_shape=outs,
        in_specs=[spec(at) for at in range(len(args))],
        out_specs=jax.tree.map(lambda _: pl.BlockSpec(memory_space=pltpu.VMEM), outs),
        scratch_shapes=scratch,
        compiler_params=pltpu.CompilerParams(vmem_limit_bytes=VMEM_LIMIT),
        cost_estimate=pl.CostEstimate(flops=1, bytes_accessed=1, transcendentals=0),
    )(*args)
    return list(got) if isinstance(outs, list) else got


def shape(dims, dtype):
    return jax.ShapeDtypeStruct(dims, dtype)


def prep_kernel(cfg, lens_ref, tasks_ref, routes_ref, cot_ref, side_ref, rows_ref, sent_ref):
    experts, cap = cfg.experts, cfg.cap
    count = routes_ref.shape[0]
    sents = lens_ref.shape[1]
    lens = lens_ref[...].astype(F32)
    tasks = tasks_ref[...].astype(F32)
    down, across = iota((sents, sents), 0), iota((sents, sents), 1)
    ends_col = lane_sum(jnp.where(across <= down, lens, 0.0))
    ends_row = row_sum(jnp.where(across == down, ends_col, 0.0))
    passed = jnp.where(iota_f((count, sents), 0) >= ends_row, 1.0, 0.0)
    sentence = lane_sum(passed)
    task = lane_sum(jnp.where(iota_f((count, sents), 1) == sentence, tasks, 0.0))
    routes = routes_ref[...].astype(F32)
    first, second = routes[:, 0:1], routes[:, 1:2]
    lane_e = iota_f((count, experts), 1)
    hot_one = jnp.where(lane_e == first, 1.0, 0.0)
    hot_two = jnp.where(lane_e == second, 1.0, 0.0)
    before = jnp.where(iota((count, count), 1) < iota((count, count), 0), 1.0, 0.0).astype(BF16)
    earlier = mm(before, (hot_one + hot_two).astype(BF16))
    target_one = first * cap + lane_sum(earlier * hot_one)
    target_two = second * cap + lane_sum(earlier * hot_two)
    lane = iota((count, LANES), 1)
    side = jnp.where(lane == 0, target_one, 0.0)
    side = jnp.where(lane == 1, target_two, side)
    side = jnp.where(lane == 2, task * experts + first, side)
    side = jnp.where(lane == 3, task * experts + second, side)
    side = jnp.where(lane == 4, sentence, side)
    side_ref[...] = side
    turned = jnp.transpose(side)
    rows_ref[...] = turned[0:8, :]
    one_row, two_row = turned[0:1, :], turned[1:2, :]
    cot = cot_ref[...]
    for e in range(experts):
        at = iota_f((cap, count), 0) + float(e * cap)
        pick = jnp.where((at == one_row) | (at == two_row), 1.0, 0.0).astype(BF16)
        sent_ref[e] = mm(pick, cot).astype(BF16)


class Groups:
    def __init__(self, devices):
        bits = devices.bit_length() - 1
        mid = (bits - 1) // 2
        self.near = [1]
        self.mid = self.masks(1, mid)
        self.far = self.masks(1 + mid, bits - 1 - mid)
        self.devices = devices

    @staticmethod
    def masks(low, width):
        return [m << low for m in range(1 << width)]

    def owners(self):
        return [[n | b | c for c in self.far] for n in (0, 1) for b in self.mid]

    def swap(self, value, mask):
        return lax.ppermute(value, BOTH, [(i, i ^ mask) for i in range(self.devices)])

    def gather_far(self, shard, first):
        blocks = [shard] + [self.swap(shard, m) for m in self.far[1:]]
        return jnp.concatenate(after(blocks, first), axis=0)

    def gather_near(self, far):
        mid = [far] + [self.swap(far, m) for m in self.mid[1:]]
        return mid + [self.swap(block, 1) for block in mid]


def place_blocks(owners, me, block_refs, full_ref):
    if len(block_refs) == 1:
        full_ref[...] = block_refs[0][...]
        return
    for block_ref, masks in zip(block_refs, owners):
        rows = block_ref.shape[0] // len(masks)
        for i, mask in enumerate(masks):
            at = pl.multiple_of((me ^ mask) * rows, rows)
            full_ref[pl.ds(at, rows), :] = block_ref[i * rows : (i + 1) * rows, :]


def take_blocks(owners, me, full_ref, keep_ref, send_ref):
    half = len(owners) // 2
    for n, out_ref in ((0, keep_ref), (1, send_ref)):
        for b, masks in enumerate(owners[n * half : (n + 1) * half]):
            rows = full_ref.shape[0] // (len(owners) * len(masks))
            for i, mask in enumerate(masks):
                at = pl.multiple_of((me ^ mask) * rows, rows)
                to = (b * len(masks) + i) * rows
                out_ref[to : to + rows, :] = full_ref[pl.ds(at, rows), :].astype(out_ref.dtype)


def add_kernel(parts, keep_ref, *refs):
    got, outs = refs[: len(refs) - parts], refs[len(refs) - parts :]
    rows = outs[0].shape[0]
    for i, out_ref in enumerate(outs):
        span = slice(i * rows, (i + 1) * rows)
        total = keep_ref[span, :]
        for ref in got:
            total = total + ref[span, :].astype(F32)
        out_ref[...] = total.astype(out_ref.dtype)


def add_parts(keep, got, parts):
    rows, columns = keep.shape
    outs = [shape((rows // parts, columns), F32 if i == 0 else BF16) for i in range(parts)]
    return call(functools.partial(add_kernel, parts), outs, [], [keep] + got, rows * columns * len(got))


def sum_to_owner(groups, keep, send):
    blocks = add_parts(keep, [groups.swap(send, 1)], len(groups.mid))
    got = [groups.swap(b, m) for b, m in zip(blocks[1:], groups.mid[1:])]
    blocks = add_parts(blocks[0], got, len(groups.far))
    return blocks[:1] + [groups.swap(b, m) for b, m in zip(blocks[1:], groups.far[1:])]


def split_kernel(cfg, *refs):
    terms, outs = refs[:-7], refs[-7:]
    rows, width = outs[0].shape[0], outs[1].shape[1]

    def total(start, stop):
        value = terms[0][:, start:stop]
        for ref in terms[1:]:
            value = value + ref[:, start:stop].astype(F32)
        return value

    outs[0][...] = total(0, 3 * width)
    outs[1][...] = total(3 * width, 4 * width)
    outs[2][...] = total(4 * width, 4 * width + cfg.gate_columns)
    tile = 4 * width + cfg.gate_columns // LANES * LANES
    lane = cfg.gate_columns % LANES
    turned = jnp.transpose(total(tile, tile + LANES))
    for i in range(4):
        outs[3 + i][...] = turned[lane + i : lane + i + 1, :]


def gain_rows(full_ref, start, gate_columns):
    tile = start + gate_columns // LANES * LANES
    lane = gate_columns % LANES
    turned = jnp.transpose(full_ref[:, tile : tile + LANES].astype(F32))
    return [turned[lane + i : lane + i + 1, :] for i in range(4)]


def forward_kernel(
    cfg, me_ref, side_ref, rows_ref, tokens_ref, *refs
):
    blocks = refs[: cfg.blocks]
    outs = refs[cfg.blocks :]
    full_ref, proj_ref, heads_ref, lse_ref, hidden_ref, gates_ref = outs[:6]
    half_experts = cfg.experts // 2
    near_ref, far_refs = outs[6], outs[7 : 7 + half_experts]
    bias_ref, routed_ref = outs[7 + half_experts :]
    count, width = tokens_ref.shape
    me = me_ref[0]
    place_blocks(cfg.owners, me, blocks, full_ref)
    gain_one, bias_one, gain_two, bias_two = gain_rows(full_ref, 4 * width, cfg.gate_columns)
    chunk = 128
    for c in range(count // chunk):
        span = slice(c * chunk, (c + 1) * chunk)
        unit, _ = norm_parts(tokens_ref[span, :].astype(F32))
        routed_ref[span, :] = (unit * gain_one + bias_one).astype(BF16)
        bias_ref[span, :] = jnp.where(
            side_ref[span, 4:5] == rows_ref[4:5, :], 0.0, NEG_FILL
        )
    proj_ref[...] = mm(routed_ref[...], full_ref[:, : 3 * width]).astype(BF16)
    lse_ref[...] = jnp.zeros_like(lse_ref)
    lane = iota((1, LANES), 1)
    scale = HEAD_DIM ** (-0.5)
    block = 256

    def slab(i, carry):
        off = pl.multiple_of(i * LANES, LANES)
        keys = proj_ref[:, pl.ds(width + off, LANES)]
        values = proj_ref[:, pl.ds(2 * width + off, LANES)]
        halves = []
        for half in (0, 1):
            mine = jnp.where(lane // HEAD_DIM == half, 1.0, 0.0).astype(BF16)
            halves.append((keys * mine, values * mine))
        for r in range(count // block):
            span = slice(r * block, (r + 1) * block)
            queries = proj_ref[span, pl.ds(off, LANES)]
            total = jnp.zeros((block, LANES), F32)
            logs = lse_ref[span, :]
            for half, (key_half, value_half) in enumerate(halves):
                scores = contract_last(queries, key_half) * scale + bias_ref[span, :]
                highest = jnp.max(scores, axis=1, keepdims=True)
                expo = jnp.exp(scores - highest)
                sums = lane_sum(expo)
                probs = (expo * (1.0 / sums)).astype(BF16)
                total = total + mm(probs, value_half)
                logs = jnp.where(lane == 2 * i + half, highest + jnp.log(sums), logs)
            heads_ref[span, pl.ds(off, LANES)] = total.astype(BF16)
            lse_ref[span, :] = logs
        return carry

    lax.fori_loop(0, width // LANES, slab, 0)
    for c in range(count // chunk):
        span = slice(c * chunk, (c + 1) * chunk)
        attended = mm(heads_ref[span, :], full_ref[:, 3 * width : 4 * width])
        hidden = tokens_ref[span, :].astype(F32) + attended
        hidden_ref[span, :] = hidden
        unit, _ = norm_parts(hidden)
        routed = (unit * gain_two + bias_two).astype(BF16)
        routed_ref[span, :] = routed
        logits = mm(routed, full_ref[:, 4 * width :])
        column = iota_f(logits.shape, 1)
        one = lane_sum(jnp.where(column == side_ref[span, 2:3], logits, 0.0))
        two = lane_sum(jnp.where(column == side_ref[span, 3:4], logits, 0.0))
        top = jnp.maximum(one, two)
        expo_one, expo_two = jnp.exp(one - top), jnp.exp(two - top)
        both = expo_one + expo_two
        gates_ref[span, :] = jnp.where(
            lane == 0, expo_one / both, jnp.where(lane == 1, expo_two / both, 0.0)
        )
    cap = cfg.cap
    mine = me // cfg.hidden
    routed = routed_ref[...]
    gate_lanes = round_up(cap, LANES)
    for k in range(cfg.experts):
        base = ((mine ^ k) * cap).astype(F32)
        at = iota_f((cap, count), 0) + base
        pick = (at == rows_ref[0:1, :]) | (at == rows_ref[1:2, :])
        send_ref = pick_ref(cfg, mine, k, near_ref, far_refs)
        send_ref[0:cap, :] = mm(jnp.where(pick, 1.0, 0.0).astype(BF16), routed).astype(BF16)
        slot = iota_f((count, gate_lanes), 1) + base
        row = row_sum(
            jnp.where(slot == side_ref[:, 0:1], gates_ref[:, 0:1], 0.0)
            + jnp.where(slot == side_ref[:, 1:2], gates_ref[:, 1:2], 0.0)
        )
        put_split(send_ref, cap, row)


def pick_ref(cfg, mine, k, near_ref, far_refs):
    half = cfg.experts // 2
    return near_ref.at[(mine ^ k) & (half - 1)] if k < half else far_refs[k - half]


def put_split(ref, cap, row):
    extra = ref.shape[0] - cap
    high = row.astype(BF16).astype(F32)
    down = iota((extra, row.shape[1]), 0)
    both = jnp.where(down == 0, high, jnp.where(down == 1, row - high, 0.0))
    ref[cap:, :] = jnp.zeros((extra, ref.shape[1]), BF16)
    ref[cap:, 0 : row.shape[1]] = both.astype(BF16)


def take_split(ref, cap, lanes):
    both = ref[cap:, 0:lanes].astype(F32)
    return both[0:1, :] + both[1:2, :]


def expert_kernel(cfg, is_near, me_ref, cot_ref, *refs):
    h, cap, n = cfg.hidden, cfg.cap, cfg.experts // 2
    many = 1 if is_near else n
    ks = range(n) if is_near else range(n, 2 * n)
    row_refs, weight_refs, refs = refs[:many], refs[many : many + h], refs[many + h :]
    if not is_near:
        before_ref, refs = refs[0], refs[1:]
    result_ref, back_refs, refs = refs[0], refs[1 : 1 + many], refs[1 + many :]
    pairs_all, act_refs, pre_refs = refs[0], refs[1 : 1 + h], refs[1 + h : 1 + 2 * h]
    rows_all, result_sum, back_sum = refs[1 + 2 * h :]
    total, width = rows_all.shape
    mine = me_ref[0] // h
    gate_lanes = round_up(cap, LANES)
    eye = iota((cap, gate_lanes), 0) == iota((cap, gate_lanes), 1)
    for i, k in enumerate(ks):
        span = slice(i * cap, (i + 1) * cap)
        row_ref = pick_ref(cfg, mine, k, row_refs[0], row_refs)
        rows_all[span, :] = row_ref[0:cap, :]
        gate = lane_sum(jnp.where(eye, take_split(row_ref, cap, gate_lanes), 0.0))
        pairs_all[span, :] = (gate * cot_ref[mine ^ k].astype(F32)).astype(BF16)
    tile = 256
    root = 0.7978845608028654
    cubic = 0.044715
    for b in range(h):
        w_in, w_out = weight_refs[b].at[0:width], weight_refs[b].at[width : 2 * width]

        def step(m, carry):
            span = pl.ds(pl.multiple_of(m * tile, tile), tile)
            pre = mm(rows_all[span, :], w_in[...])
            square = pre * pre
            bent = jnp.tanh(pre * (root + (root * cubic) * square))
            upper = 0.5 + 0.5 * bent
            act = pre * upper
            slope = upper + act * (1.0 - upper) * (2.0 * root + (6.0 * root * cubic) * square)
            act_low = act.astype(BF16)
            act_refs[b][span, :] = act_low
            act_grad = mm(pairs_all[span, :], w_out[...])
            pre_grad = (act_grad * slope).astype(BF16)
            pre_refs[b][span, :] = pre_grad
            result = contract_last(act_low, w_out[...])
            back = contract_last(pre_grad, w_in[...])
            if b == 0:
                result_sum[span, :] = result
                back_sum[span, :] = back
            else:
                result_sum[span, :] += result
                back_sum[span, :] += back
            return carry

        lax.fori_loop(0, total // tile, step, 0)
    if not is_near:
        for k in range(n):
            result_ref[mine ^ k] = before_ref[k]
    for i, k in enumerate(ks):
        span = slice(i * cap, (i + 1) * cap)
        result = result_sum[span, :].astype(BF16)
        result_ref[i if is_near else mine ^ k] = result
        back_ref = pick_ref(cfg, mine, k, back_refs[0], back_refs)
        back_ref[0:cap, :] = back_sum[span, :].astype(BF16)
        dots = lane_sum(cot_ref[mine ^ k].astype(F32) * result.astype(F32))
        put_split(back_ref, cap, row_sum(jnp.where(eye, dots, 0.0)))


def expert_part(cfg, is_near, me, cot, rows, weights, before):
    n, h = cfg.experts // 2, cfg.hidden
    width, units = cot.shape[2], weights[0].shape[1]
    slots = n * cfg.cap
    many = len(rows)
    outs = call(
        functools.partial(expert_kernel, cfg, is_near),
        [shape((n if is_near else 2 * n, cfg.cap, width), BF16)]
        + [shape(r.shape, BF16) for r in rows]
        + [shape((slots, width), BF16)]
        + [shape((slots, units), BF16)] * (2 * h),
        [pltpu.VMEM((slots, width), BF16)] + [pltpu.VMEM((slots, width), F32)] * 2,
        [me, cot] + rows + weights + before,
        8 * slots * width * units * h,
        smem=(0,),
    )
    return outs[0], outs[1 : 1 + many], outs[1 + many], outs[2 + many : 2 + many + h], outs[2 + many + h :]


def weight_kernel(cfg, parts, first, me_ref, *refs):
    n = cfg.experts
    if first:
        near_ref, far_refs = refs[0], refs[1 : 1 + n // 2]
        pair_refs, refs = refs[1 + n // 2 : 3 + n // 2], refs[3 + n // 2 :]
    else:
        turned_refs, refs = refs[:2], refs[2:]
    pre_refs, act_refs, refs = refs[: 2 * parts], refs[2 * parts : 4 * parts], refs[4 * parts :]
    if first:
        turned_refs, refs = refs[:2], refs[2:]
    out_refs = refs[:parts]
    rows_turned, pairs_turned = turned_refs
    width, total = rows_turned.shape
    if first:
        rows_all = refs[parts]
        cap, half = cfg.cap, total // 2
        for k in range(n):
            row_ref = pick_ref(cfg, me_ref[0] // cfg.hidden, k, near_ref, far_refs)
            rows_all[k * cap : (k + 1) * cap, :] = row_ref[0:cap, :]
        rows_turned[...] = jnp.transpose(rows_all[...])
        pairs_turned[:, :half] = jnp.transpose(pair_refs[0][...])
        pairs_turned[:, half:] = jnp.transpose(pair_refs[1][...])
    half = total // 2
    for p in range(parts):
        for turned, half_refs, at in ((rows_turned, pre_refs, 0), (pairs_turned, act_refs, width)):
            value = mm(turned[:, :half], half_refs[2 * p][...])
            value = value + mm(turned[:, half:], half_refs[2 * p + 1][...])
            out_refs[p][at : at + width, :] = value.astype(out_refs[p].dtype)


def turn_add_kernel(*refs):
    terms, (sum_in, sum_out) = refs[:-2], refs[-2:]
    width = sum_in.shape[0]
    total = terms[0][...]
    for ref in terms[1:]:
        total = total + ref[...].astype(F32)
    sum_in[...] = total[:width, :]
    sum_out[...] = jnp.transpose(total[width:, :])


def backward_kernel(cfg, me_ref, side_ref, hidden_ref, gates_ref, cot_ref, heads_ref, full_ref, *refs):
    n, cap = cfg.experts, cfg.cap
    near_ref, far_refs, refs = refs[0], refs[1 : 1 + n // 2], refs[1 + n // 2 :]
    hidden_grad_ref, heads_grad_ref, dense_ref, routed_sum, routed_ref, logits_ref = refs
    count, width = hidden_ref.shape
    me = me_ref[0]
    mine = me // cfg.hidden
    gain_one, bias_one, gain_two, bias_two = gain_rows(full_ref, 4 * width, cfg.gate_columns)
    gate_lanes = round_up(cap, LANES)
    one, two = side_ref[:, 0:1], side_ref[:, 1:2]
    dot_one = jnp.zeros((count, 1), F32)
    dot_two = jnp.zeros((count, 1), F32)
    for k in range(n):
        base = ((mine ^ k) * cap).astype(F32)
        slot = iota_f((count, cap), 1) + base
        pick = jnp.where((slot == one) | (slot == two), 1.0, 0.0).astype(BF16)
        back_ref = pick_ref(cfg, mine, k, near_ref, far_refs)
        part = mm(pick, back_ref[0:cap, :])
        if k == 0:
            routed_sum[...] = part
        else:
            routed_sum[...] += part
        lane_at = iota_f((count, gate_lanes), 1)
        slot = jnp.where(lane_at < cap, lane_at + base, -1.0)
        dots = take_split(back_ref, cap, gate_lanes)
        dot_one = dot_one + lane_sum(jnp.where(slot == one, dots, 0.0))
        dot_two = dot_two + lane_sum(jnp.where(slot == two, dots, 0.0))
    gate_one, gate_two = gates_ref[:, 0:1], gates_ref[:, 1:2]
    shared = gate_one * dot_one + gate_two * dot_two
    chosen_one = gate_one * (dot_one - shared)
    chosen_two = gate_two * (dot_two - shared)
    gate_full = full_ref[:, 4 * width :]
    chunk = 128
    gain_sum = jnp.zeros((1, width), F32)
    bias_sum = jnp.zeros((1, width), F32)
    for c in range(count // chunk):
        span = slice(c * chunk, (c + 1) * chunk)
        column = iota_f((chunk, cfg.gate_lanes), 1)
        logits = jnp.where(column == side_ref[span, 2:3], chosen_one[span], 0.0) + jnp.where(
            column == side_ref[span, 3:4], chosen_two[span], 0.0
        )
        logits = logits.astype(BF16)
        logits_ref[span, :] = logits
        routed_grad = routed_sum[span, :] + contract_last(logits, gate_full)
        unit, inverse = norm_parts(hidden_ref[span, :])
        routed_ref[span, :] = (unit * gain_two + bias_two).astype(BF16)
        gain_sum = gain_sum + row_sum(routed_grad * unit)
        bias_sum = bias_sum + row_sum(routed_grad)
        hidden_grad = cot_ref[span, :].astype(F32) + norm_back(unit, inverse, gain_two, routed_grad)
        hidden_grad_ref[span, :] = hidden_grad
        low = hidden_grad.astype(BF16)
        routed_sum[span, :] = hidden_grad
        heads_grad_ref[span, :] = contract_last(low, full_ref[:, 3 * width : 4 * width]).astype(BF16)
    dense_ref[:, 0:width] = contract_first(heads_ref[...], routed_sum[...].astype(BF16))
    dense_ref[:, width:] = contract_first(routed_ref[...], logits_ref[...])
    tile = width + cfg.gate_columns // LANES * LANES
    lane = cfg.gate_columns % LANES
    dense_ref[:, tile : tile + LANES] += rows_to_lanes(gain_sum, bias_sum, lane + 2)


def rows_to_lanes(first, second, lane):
    down = iota((LANES, first.shape[1]), 0)
    return jnp.transpose(jnp.where(down == lane, first, jnp.where(down == lane + 1, second, 0.0)))


def put_dense(cfg, me, dense_ref, outs):
    if len(outs) == 1:
        outs[0][...] = dense_ref[...]
    else:
        take_blocks(cfg.owners, me, dense_ref, *outs)


def attention_back_kernel(
    cfg, me_ref, side_ref, rows_ref, tokens_ref, proj_ref, lse_ref, heads_grad_ref, hidden_grad_ref, first_ref, full_ref, *refs
):
    grad_ref = refs[0]
    dense = refs[1 : len(refs) - 4]
    bias_ref, low_ref, qkv_ref, dense_ref = refs[len(refs) - 4 :]
    count, width = tokens_ref.shape
    me = me_ref[0]
    gain_one, bias_one, gain_two, bias_two = gain_rows(full_ref, 4 * width, cfg.gate_columns)
    chunk = 128
    for c in range(count // chunk):
        span = slice(c * chunk, (c + 1) * chunk)
        unit, _ = norm_parts(tokens_ref[span, :].astype(F32))
        low_ref[span, :] = (unit * gain_one + bias_one).astype(BF16)
        bias_ref[span, :] = jnp.where(
            side_ref[span, 4:5] == rows_ref[4:5, :], 0.0, NEG_FILL
        )
    lane = iota((1, LANES), 1)
    scale = HEAD_DIM ** (-0.5)

    def slab(i, carry):
        off = pl.multiple_of(i * LANES, LANES)
        queries = proj_ref[:, pl.ds(off, LANES)]
        keys = proj_ref[:, pl.ds(width + off, LANES)]
        values = proj_ref[:, pl.ds(2 * width + off, LANES)]
        grads = heads_grad_ref[:, pl.ds(off, LANES)]
        query_grad = jnp.zeros((count, LANES), F32)
        key_grad = jnp.zeros((count, LANES), F32)
        value_grad = jnp.zeros((count, LANES), F32)
        for half in (0, 1):
            mine = jnp.where(lane // HEAD_DIM == half, 1.0, 0.0).astype(BF16)
            query_half, key_half, grads_half = queries * mine, keys * mine, grads * mine
            logs = lane_sum(jnp.where(lane == 2 * i + half, lse_ref[...], 0.0))
            probs = jnp.exp(contract_last(queries, key_half) * scale + bias_ref[...] - logs)
            prob_grad = contract_last(grads_half, values)
            row_dot = lane_sum(probs * prob_grad)
            score_grad = (probs * (prob_grad - row_dot)).astype(BF16)
            value_grad = value_grad + contract_first(probs.astype(BF16), grads_half)
            query_grad = query_grad + mm(score_grad, key_half)
            key_grad = key_grad + contract_first(score_grad, query_half)
        qkv_ref[:, pl.ds(off, LANES)] = (query_grad * scale).astype(BF16)
        qkv_ref[:, pl.ds(width + off, LANES)] = (key_grad * scale).astype(BF16)
        qkv_ref[:, pl.ds(2 * width + off, LANES)] = value_grad.astype(BF16)
        return carry

    lax.fori_loop(0, width // LANES, slab, 0)
    dense_ref[:, : 3 * width] = contract_first(low_ref[...], qkv_ref[...])
    gain_sum = jnp.zeros((1, width), F32)
    bias_sum = jnp.zeros((1, width), F32)
    for c in range(count // chunk):
        span = slice(c * chunk, (c + 1) * chunk)
        normed_grad = contract_last(qkv_ref[span, :], full_ref[:, : 3 * width])
        unit, inverse = norm_parts(tokens_ref[span, :].astype(F32))
        gain_sum = gain_sum + row_sum(normed_grad * unit)
        bias_sum = bias_sum + row_sum(normed_grad)
        grad_ref[span, :] = hidden_grad_ref[span, :] + norm_back(unit, inverse, gain_one, normed_grad)
    dense_ref[:, 3 * width :] = first_ref[...]
    tile = 4 * width + cfg.gate_columns // LANES * LANES
    lane = cfg.gate_columns % LANES
    dense_ref[:, tile : tile + LANES] += rows_to_lanes(gain_sum, bias_sum, lane)
    put_dense(cfg, me, dense_ref, dense)


def output_kernel(cfg, side_ref, hidden_ref, gates_ref, result_ref, out_ref):
    cap = cfg.cap
    count = hidden_ref.shape[0]
    total_one = jnp.zeros(hidden_ref.shape, F32)
    total_two = jnp.zeros(hidden_ref.shape, F32)
    for e in range(cfg.experts):
        slot = iota_f((count, cap), 1) + float(e * cap)
        pick_one = jnp.where(slot == side_ref[:, 0:1], 1.0, 0.0).astype(BF16)
        pick_two = jnp.where(slot == side_ref[:, 1:2], 1.0, 0.0).astype(BF16)
        total_one = total_one + mm(pick_one, result_ref[e])
        total_two = total_two + mm(pick_two, result_ref[e])
    mixed = gates_ref[:, 0:1] * total_one + gates_ref[:, 1:2] * total_two
    out_ref[...] = (hidden_ref[...] + mixed).astype(BF16)


class Config:
    pass


def after(value, other):
    return lax.optimization_barrier((value, other))[0]


def swap_hidden(value, mask):
    size = lax.axis_size("hidden")
    return lax.ppermute(value, "hidden", [(i, i ^ mask) for i in range(size)])


def swap_expert(value, mask):
    size = lax.axis_size("expert")
    return lax.ppermute(value, "expert", [(i, i ^ mask) for i in range(size)])


def gather_rest(own):
    blocks = [own]
    bit = 2
    while bit < lax.axis_size("hidden"):
        blocks += [swap_hidden(block, bit) for block in blocks]
        bit *= 2
    return blocks


def gather_core(half, first):
    blocks = []
    for block in half:
        blocks += [block, swap_hidden(after(block, first), 1)]
    return blocks


def sum_hidden(blocks):
    size = len(blocks)
    held = {i: [b] for i, b in enumerate(blocks)}
    bit = 1
    while bit < size:
        low = {i: v for i, v in held.items() if not i & bit}
        for i in low:
            terms = held[i ^ bit]
            value = terms[0] if len(terms) == 1 else sum(t.astype(F32) for t in terms).astype(BF16)
            low[i] = low[i] + [swap_hidden(value, bit)]
        held = low
        bit *= 2
    return held[0], value


def body(
    tokens,
    lengths,
    task_ids,
    routes,
    w_qkv,
    w_attn_out,
    w_gate,
    ln1_gain,
    ln1_bias,
    ln2_gain,
    ln2_bias,
    w_in,
    w_out,
    cotangent,
):
    count, width = tokens.shape
    cfg = Config()
    cfg.experts = lax.axis_size("expert")
    cfg.hidden = lax.axis_size("hidden")
    experts, hidden = cfg.experts, cfg.hidden
    cfg.cap = cap = (3 * count * routes.shape[1] + 2 * experts - 1) // (2 * experts)
    cfg.gate_columns = w_gate.shape[1]
    cfg.gate_lanes = round_up(cfg.gate_columns + 4, LANES)
    devices = experts * hidden
    groups = Groups(devices)
    shard_rows = w_qkv.shape[0]
    staged = shard_rows % 16 == 0
    cfg.owners = groups.owners()
    me = (lax.axis_index("expert") * hidden + lax.axis_index("hidden")).astype(jnp.int32)[None]
    extra = 16
    units = w_in.shape[2]
    slots = experts * cap
    wide = 4 * width + cfg.gate_lanes
    one_dot = 2 * count * width * width

    own_weights = jnp.concatenate([w_in[0], w_out[0].T], axis=0)
    packed = jnp.concatenate(
        [w_qkv, w_attn_out, w_gate]
        + [v[:, None] for v in (ln1_gain, ln1_bias, ln2_gain, ln2_bias)]
        + [jnp.zeros((shard_rows, cfg.gate_lanes - cfg.gate_columns - 4), BF16)],
        axis=1,
    )
    outs = call(
        functools.partial(prep_kernel, cfg),
        [shape((count, LANES), F32), shape((8, count), F32), shape((experts, cap, width), BF16)],
        [],
        [lengths, task_ids, routes, cotangent],
        3 * one_dot,
    )
    side, rows, sent_cot = outs
    if staged:
        dense_far = groups.gather_far(packed, sent_cot)
        dense_blocks = groups.gather_near(dense_far)
        reached = dense_blocks[1 : len(groups.mid)]
    else:
        dense_blocks = [lax.all_gather(packed, BOTH, axis=0, tiled=True)]
        dense_far = reached = dense_blocks[0]
    cfg.blocks = len(dense_blocks)

    owned_cot = lax.all_to_all(
        after(sent_cot, dense_far), "expert", split_axis=0, concat_axis=0, tiled=True
    )
    weight_half = gather_rest(after(own_weights, reached))

    outs = call(
        functools.partial(forward_kernel, cfg),
        [
            shape((width, wide), BF16),
            shape((count, 3 * width), BF16),
            shape((count, width), BF16),
            shape((count, LANES), F32),
            shape((count, width), F32),
            shape((count, LANES), F32),
        ]
        + [shape((experts // 2, cap + extra, width), BF16)]
        + [shape((cap + extra, width), BF16)] * (experts // 2),
        [pltpu.VMEM((count, count), F32), pltpu.VMEM((count, width), BF16)],
        [me, side, rows, tokens] + dense_blocks,
        12 * one_dot,
        smem=(0,),
    )
    full, proj, heads, lse, hidden_one, gates = outs[:6]
    send_rows = outs[6:]
    half = experts // 2
    groups_near = [list(range(half)), list(range(half, experts))]

    def exchange(near, far):
        near = lax.all_to_all(
            near, "expert", split_axis=0, concat_axis=0, axis_index_groups=groups_near, tiled=True
        )
        return [near], [swap_expert(value, half + i) for i, value in enumerate(far)]

    weight_blocks = gather_core(weight_half, gates)
    near_rows, far_rows = exchange(after(send_rows[0], owned_cot), send_rows[1:])
    near_out = expert_part(cfg, True, me, owned_cot, near_rows, weight_blocks, [])
    far_out = expert_part(cfg, False, me, owned_cot, far_rows, weight_blocks, [near_out[0]])
    result = far_out[0]
    near_back, far_back = exchange(near_out[1][0], far_out[1])
    back = near_back + far_back

    turned = []
    grads = {}
    for odd in (1, 0):
        picked = [b for b in range(hidden) if b % 2 == odd]
        pre = [o[4][b] for b in picked for o in (near_out, far_out)]
        act = [o[3][b] for b in picked for o in (near_out, far_out)]
        if odd:
            lead = near_rows + far_rows + [near_out[2], far_out[2]]
        else:
            lead = turned
        outs = call(
            functools.partial(weight_kernel, cfg, len(picked), bool(odd)),
            [shape((width, slots), BF16)] * (2 * odd)
            + [shape((2 * width, units), BF16 if b else F32) for b in picked],
            [pltpu.VMEM((slots, width), BF16)] * odd,
            [me] + lead + pre + act,
            4 * slots * width * units * len(picked),
            smem=(0,),
        )
        if odd:
            turned, outs = outs[:2], outs[2:]
        grads.update(zip(picked, outs))
    terms, last_sent = sum_hidden([grads[b] for b in range(hidden)])
    back = after(back, last_sent)
    grad_in, grad_out = call(
        turn_add_kernel,
        [shape((width, units), F32), shape((units, width), F32)],
        [],
        terms,
        4 * width * units,
    )

    returned = lax.all_to_all(
        after(result, back), "expert", split_axis=0, concat_axis=0, tiled=True
    )
    outs = call(
        functools.partial(backward_kernel, cfg),
        [
            shape((count, width), F32),
            shape((count, width), BF16),
            shape((width, width + cfg.gate_lanes), F32),
        ],
        [
            pltpu.VMEM((count, width), F32),
            pltpu.VMEM((count, width), BF16),
            pltpu.VMEM((count, cfg.gate_lanes), BF16),
        ],
        [me, side, hidden_one, gates, cotangent, heads, full] + back,
        7 * one_dot,
        smem=(0,),
    )
    hidden_grad, heads_grad, dense_one = outs

    if staged:
        dense_shapes = [shape((width // 2, wide), F32), shape((width // 2, wide), BF16)]
    else:
        dense_shapes = [shape((width, wide), F32)]
    outs = call(
        functools.partial(attention_back_kernel, cfg),
        [shape((count, width), F32)] + dense_shapes,
        [
            pltpu.VMEM((count, count), F32),
            pltpu.VMEM((count, width), BF16),
            pltpu.VMEM((count, 3 * width), BF16),
            pltpu.VMEM((width, wide), F32),
        ],
        [me, side, rows, tokens, proj, lse, heads_grad, hidden_grad, dense_one, full],
        12 * one_dot,
        smem=(0,),
    )
    grad_tokens = outs[0]
    if staged:
        dense_terms = sum_to_owner(groups, *outs[1:])
    else:
        dense_terms = [lax.psum_scatter(outs[1], BOTH, scatter_dimension=0, tiled=True)]
    dense_outs = call(
        functools.partial(split_kernel, cfg),
        [shape((shard_rows, c), F32) for c in (3 * width, width, cfg.gate_columns)]
        + [shape((1, shard_rows), F32)] * 4,
        [],
        dense_terms,
        shard_rows * wide,
    )

    layer_out = call(
        functools.partial(output_kernel, cfg),
        shape((count, width), BF16),
        [],
        [side, hidden_one, gates, returned],
        6 * one_dot,
    )
    return (
        layer_out,
        grad_tokens,
        *dense_outs[:3],
        *[v.reshape(shard_rows) for v in dense_outs[3:]],
        grad_in[None],
        grad_out[None],
    )


def solution(mesh):
    split = P(BOTH, None)
    vector = P(BOTH)
    placed = (split,) * 7 + (vector,) * 4 + (P("expert", None, "hidden"), P("expert", "hidden", None), split)
    return jax.shard_map(
        body,
        mesh=mesh,
        in_specs=placed,
        out_specs=(split,) * 5
        + (vector,) * 4
        + (P("expert", None, "hidden"), P("expert", "hidden", None)),
        check_vma=False,
    )
```

```python
import functools

import jax
import jax.numpy as jnp
from jax import lax
from jax.experimental import pallas as pl
from jax.experimental.pallas import tpu as pltpu
from jax.sharding import PartitionSpec as P

HEADS = 8
HEAD_DIM = 64
EPS = 1e-05
NEG_FILL = -1e30
LANES = 128
BOTH = ("expert", "hidden")
F32 = jnp.float32
BF16 = jnp.bfloat16
VMEM_LIMIT = 56 * 1024 * 1024


def mm(left, right):
    return jnp.dot(left, right, preferred_element_type=F32)


def contract_last(left, right):
    return lax.dot_general(left, right, (((1,), (1,)), ((), ())), preferred_element_type=F32)


def contract_first(left, right):
    return lax.dot_general(left, right, (((0,), (0,)), ((), ())), preferred_element_type=F32)


def iota(shape, axis):
    return lax.broadcasted_iota(jnp.int32, shape, axis)


def iota_f(shape, axis):
    return iota(shape, axis).astype(F32)


def lane_sum(values):
    return jnp.sum(values, axis=1, keepdims=True)


def row_sum(values):
    return jnp.sum(values, axis=0, keepdims=True)


def norm_parts(values):
    middle = jnp.mean(values, axis=-1, keepdims=True)
    centred = values - middle
    spread = jnp.mean(centred * centred, axis=-1, keepdims=True)
    inverse = lax.rsqrt(spread + EPS)
    return centred * inverse, inverse


def norm_back(unit, inverse, gain, grad):
    scaled = grad * gain
    mean_one = jnp.mean(scaled, axis=-1, keepdims=True)
    mean_two = jnp.mean(scaled * unit, axis=-1, keepdims=True)
    return inverse * (scaled - mean_one - unit * mean_two)


def round_up(value, step):
    return (value + step - 1) // step * step


def call(kernel, outs, scratch, args, flops, smem=(), far_in=(), far_out=()):
    def spec(at):
        space = pltpu.SMEM if at in smem else pl.ANY if at in far_in else pltpu.VMEM
        return pl.BlockSpec(memory_space=space)

    def out_spec(at):
        return pl.BlockSpec(memory_space=pl.ANY if at in far_out else pltpu.VMEM)

    touched = sum(a.size * a.dtype.itemsize for a in args) + sum(
        o.size * o.dtype.itemsize for o in jax.tree.leaves(outs)
    )
    got = pl.pallas_call(
        kernel,
        out_shape=outs,
        in_specs=[spec(at) for at in range(len(args))],
        out_specs=[out_spec(at) for at in range(len(outs))] if isinstance(outs, list) else out_spec(0),
        scratch_shapes=scratch,
        compiler_params=pltpu.CompilerParams(vmem_limit_bytes=VMEM_LIMIT),
        cost_estimate=pl.CostEstimate(flops=1, bytes_accessed=1, transcendentals=0),
    )(*args)
    return list(got) if isinstance(outs, list) else got


def shape(dims, dtype):
    return jax.ShapeDtypeStruct(dims, dtype)


def slot_targets(cfg, routes_ref):
    count, experts = routes_ref.shape[0], cfg.experts
    routes = routes_ref[...].astype(F32)
    first, second = routes[:, 0:1], routes[:, 1:2]
    lane_e = iota_f((count, experts), 1)
    hot_one = jnp.where(lane_e == first, 1.0, 0.0)
    hot_two = jnp.where(lane_e == second, 1.0, 0.0)
    before = jnp.where(iota((count, count), 1) < iota((count, count), 0), 1.0, 0.0).astype(BF16)
    earlier = mm(before, (hot_one + hot_two).astype(BF16))
    target_one = first * cfg.cap + lane_sum(earlier * hot_one)
    target_two = second * cfg.cap + lane_sum(earlier * hot_two)
    return first, second, target_one, target_two


def prep_kernel(cfg, lens_ref, tasks_ref, routes_ref, cot_ref, side_ref, rows_ref, sent_ref):
    experts, cap = cfg.experts, cfg.cap
    count = routes_ref.shape[0]
    sents = lens_ref.shape[1]
    lens = lens_ref[...].astype(F32)
    tasks = tasks_ref[...].astype(F32)
    down, across = iota((sents, sents), 0), iota((sents, sents), 1)
    ends_col = lane_sum(jnp.where(across <= down, lens, 0.0))
    ends_row = row_sum(jnp.where(across == down, ends_col, 0.0))
    passed = jnp.where(iota_f((count, sents), 0) >= ends_row, 1.0, 0.0)
    sentence = lane_sum(passed)
    task = lane_sum(jnp.where(iota_f((count, sents), 1) == sentence, tasks, 0.0))
    lane = iota((count, LANES), 1)
    first, second, target_one, target_two = slot_targets(cfg, routes_ref)
    side = jnp.where(lane == 0, target_one, 0.0)
    side = jnp.where(lane == 1, target_two, side)
    side = jnp.where(lane == 2, task * experts + first, side)
    side = jnp.where(lane == 3, task * experts + second, side)
    side = jnp.where(lane == 4, sentence, side)
    side_ref[...] = side
    turned = jnp.transpose(side)
    rows_ref[...] = turned[0:8, :]
    one_row, two_row = turned[0:1, :], turned[1:2, :]
    cot = cot_ref[...]
    for e in range(experts):
        at = iota_f((cap, count), 0) + float(e * cap)
        pick = jnp.where((at == one_row) | (at == two_row), 1.0, 0.0).astype(BF16)
        sent_ref[e // 2, e % 2] = mm(pick, cot).astype(BF16)


class Groups:
    def __init__(self, devices):
        bits = devices.bit_length() - 1
        mid = (bits - 1) // 2
        self.near = [1]
        self.mid = self.masks(1, mid)
        self.far = self.masks(1 + mid, bits - 1 - mid)
        self.devices = devices

    @staticmethod
    def masks(low, width):
        return [m << low for m in range(1 << width)]

    def owners(self):
        return [[n | b | c for c in self.far] for n in (0, 1) for b in self.mid]

    def swap(self, value, mask):
        return lax.ppermute(value, BOTH, [(i, i ^ mask) for i in range(self.devices)])

    def gather_far(self, shard):
        return jnp.concatenate([shard] + [self.swap(shard, m) for m in self.far[1:]], axis=0)

    def gather_near(self, far):
        mid = [far] + [self.swap(far, m) for m in self.mid[1:]]
        return mid + [self.swap(block, 1) for block in mid]


def place_blocks(owners, me, block_refs, full_ref):
    if len(block_refs) == 1:
        full_ref[...] = block_refs[0][...]
        return
    for block_ref, masks in zip(block_refs, owners):
        rows = block_ref.shape[0] // len(masks)
        for i, mask in enumerate(masks):
            at = pl.multiple_of((me ^ mask) * rows, rows)
            full_ref[pl.ds(at, rows), :] = block_ref[i * rows : (i + 1) * rows, :]


def take_blocks(owners, me, full_ref, keep_ref, send_ref):
    half = len(owners) // 2
    for n, out_ref in ((0, keep_ref), (1, send_ref)):
        for b, masks in enumerate(owners[n * half : (n + 1) * half]):
            rows = full_ref.shape[0] // (len(owners) * len(masks))
            for i, mask in enumerate(masks):
                at = pl.multiple_of((me ^ mask) * rows, rows)
                to = (b * len(masks) + i) * rows
                out_ref[to : to + rows, :] = full_ref[pl.ds(at, rows), :].astype(out_ref.dtype)


def add_kernel(parts, keep_ref, *refs):
    got, outs = refs[: len(refs) - parts], refs[len(refs) - parts :]
    rows = outs[0].shape[0]
    for i, out_ref in enumerate(outs):
        span = slice(i * rows, (i + 1) * rows)
        total = keep_ref[span, :]
        for ref in got:
            total = total + ref[span, :].astype(F32)
        out_ref[...] = total.astype(out_ref.dtype)


def add_parts(keep, got, parts):
    rows, columns = keep.shape
    outs = [shape((rows // parts, columns), F32 if i == 0 else BF16) for i in range(parts)]
    return call(functools.partial(add_kernel, parts), outs, [], [keep] + got, rows * columns * len(got))


def sum_to_owner(groups, keep, send, first):
    blocks = add_parts(keep, [groups.swap(send, 1)], len(groups.mid))
    got = [groups.swap(b, m) for b, m in zip(blocks[1:], groups.mid[1:])]
    blocks = add_parts(after(blocks[0], first), got, len(groups.far))
    return blocks[:1] + [groups.swap(b, m) for b, m in zip(blocks[1:], groups.far[1:])]


def split_kernel(cfg, *refs):
    terms, outs = refs[:-7], refs[-7:]
    rows, width = outs[0].shape[0], outs[1].shape[1]

    def total(start, stop):
        value = terms[0][:, start:stop]
        for ref in terms[1:]:
            value = value + ref[:, start:stop].astype(F32)
        return value

    outs[0][...] = total(0, 3 * width)
    outs[1][...] = total(3 * width, 4 * width)
    outs[2][...] = total(4 * width, 4 * width + cfg.gate_columns)
    tile = 4 * width + cfg.gate_columns // LANES * LANES
    lane = cfg.gate_columns % LANES
    turned = jnp.transpose(total(tile, tile + LANES))
    for i in range(4):
        outs[3 + i][...] = turned[lane + i : lane + i + 1, :]


def gain_rows(full_ref, start, gate_columns):
    tile = start + gate_columns // LANES * LANES
    lane = gate_columns % LANES
    turned = jnp.transpose(full_ref[:, tile : tile + LANES].astype(F32))
    return [turned[lane + i : lane + i + 1, :] for i in range(4)]


def forward_kernel(
    cfg, me_ref, side_ref, rows_ref, tokens_ref, *refs
):
    blocks = refs[: cfg.blocks]
    outs = refs[cfg.blocks :]
    full_ref, proj_ref, heads_ref, lse_ref, hidden_ref, gates_ref = outs[:6]
    half_experts = cfg.experts // 2
    even_ref, odd_refs = outs[6], outs[7 : 7 + half_experts]
    bias_ref, routed_ref = outs[7 + half_experts :]
    count, width = tokens_ref.shape
    me = me_ref[0]
    place_blocks(cfg.owners, me, blocks, full_ref)
    gain_one, bias_one, gain_two, bias_two = gain_rows(full_ref, 4 * width, cfg.gate_columns)
    chunk = 128
    for c in range(count // chunk):
        span = slice(c * chunk, (c + 1) * chunk)
        unit, _ = norm_parts(tokens_ref[span, :].astype(F32))
        routed_ref[span, :] = (unit * gain_one + bias_one).astype(BF16)
        bias_ref[span, :] = jnp.where(
            side_ref[span, 4:5] == rows_ref[4:5, :], 0.0, NEG_FILL
        )
    proj_ref[...] = mm(routed_ref[...], full_ref[:, : 3 * width]).astype(BF16)
    lse_ref[...] = jnp.zeros_like(lse_ref)
    lane = iota((1, LANES), 1)
    scale = HEAD_DIM ** (-0.5)
    block = 256

    def slab(i, carry):
        off = pl.multiple_of(i * LANES, LANES)
        keys = proj_ref[:, pl.ds(width + off, LANES)]
        values = proj_ref[:, pl.ds(2 * width + off, LANES)]
        halves = []
        for half in (0, 1):
            mine = jnp.where(lane // HEAD_DIM == half, 1.0, 0.0).astype(BF16)
            halves.append((keys * mine, values * mine))
        for r in range(count // block):
            span = slice(r * block, (r + 1) * block)
            queries = proj_ref[span, pl.ds(off, LANES)]
            total = jnp.zeros((block, LANES), F32)
            logs = lse_ref[span, :]
            for half, (key_half, value_half) in enumerate(halves):
                scores = contract_last(queries, key_half) * scale + bias_ref[span, :]
                highest = jnp.max(scores, axis=1, keepdims=True)
                expo = jnp.exp(scores - highest)
                sums = lane_sum(expo)
                probs = (expo * (1.0 / sums)).astype(BF16)
                total = total + mm(probs, value_half)
                logs = jnp.where(lane == 2 * i + half, highest + jnp.log(sums), logs)
            heads_ref[span, pl.ds(off, LANES)] = total.astype(BF16)
            lse_ref[span, :] = logs
        return carry

    lax.fori_loop(0, width // LANES, slab, 0)
    for c in range(count // chunk):
        span = slice(c * chunk, (c + 1) * chunk)
        attended = mm(heads_ref[span, :], full_ref[:, 3 * width : 4 * width])
        hidden = tokens_ref[span, :].astype(F32) + attended
        hidden_ref[span, :] = hidden
        unit, _ = norm_parts(hidden)
        routed = (unit * gain_two + bias_two).astype(BF16)
        routed_ref[span, :] = routed
        logits = mm(routed, full_ref[:, 4 * width :])
        column = iota_f(logits.shape, 1)
        one = lane_sum(jnp.where(column == side_ref[span, 2:3], logits, 0.0))
        two = lane_sum(jnp.where(column == side_ref[span, 3:4], logits, 0.0))
        top = jnp.maximum(one, two)
        expo_one, expo_two = jnp.exp(one - top), jnp.exp(two - top)
        both = expo_one + expo_two
        gates_ref[span, :] = jnp.where(
            lane == 0, expo_one / both, jnp.where(lane == 1, expo_two / both, 0.0)
        )
    cap = cfg.cap
    mine = me // cfg.hidden
    routed = routed_ref[...]
    gate_lanes = round_up(cap, LANES)
    for k in range(cfg.experts):
        base = ((mine ^ k) * cap).astype(F32)
        at = iota_f((cap, count), 0) + base
        pick = (at == rows_ref[0:1, :]) | (at == rows_ref[1:2, :])
        send_ref = pick_ref(mine, k, even_ref, odd_refs)
        send_ref[0:cap, :] = mm(jnp.where(pick, 1.0, 0.0).astype(BF16), routed).astype(BF16)
        slot = iota_f((count, gate_lanes), 1) + base
        row = row_sum(
            jnp.where(slot == side_ref[:, 0:1], gates_ref[:, 0:1], 0.0)
            + jnp.where(slot == side_ref[:, 1:2], gates_ref[:, 1:2], 0.0)
        )
        put_split(send_ref, cap, row)


def pick_ref(mine, k, even_ref, odd_refs):
    return odd_refs[k // 2] if k % 2 else even_ref.at[(mine ^ k) // 2]


def put_split(ref, cap, row):
    extra = ref.shape[0] - cap
    high = row.astype(BF16).astype(F32)
    down = iota((extra, row.shape[1]), 0)
    both = jnp.where(down == 0, high, jnp.where(down == 1, row - high, 0.0))
    ref[cap:, :] = jnp.zeros((extra, ref.shape[1]), BF16)
    ref[cap:, 0 : row.shape[1]] = both.astype(BF16)


def take_split(ref, cap, lanes):
    both = ref[cap:, 0:lanes].astype(F32)
    return both[0:1, :] + both[1:2, :]


def expert_kernel(cfg, odd, me_ref, *refs):
    h, cap, n = cfg.hidden, cfg.cap, cfg.experts // 2
    many = n if odd else 1
    ks = range(odd, 2 * n, 2)
    cot_ref, refs = refs[0], refs[1:]
    row_refs, refs = refs[:many], refs[many:]
    in_refs, out_refs, refs = refs[:h], refs[h : 2 * h], refs[2 * h :]
    if odd:
        before_ref, refs = refs[0], refs[1:]
    result_ref, back_refs, refs = refs[0], refs[1 : 1 + many], refs[1 + many :]
    pairs_all, act_refs, pre_refs = refs[0], refs[1 : 1 + h], refs[1 + h : 1 + 2 * h]
    rows_all, result_sum, back_sum, weights_all, act_all, pre_all, in_sems, out_sems = refs[1 + 2 * h :]
    loads = []
    for i, ref in enumerate(in_turn(in_refs, out_refs)):
        held = weights_all.at[i, : ref.shape[0], : ref.shape[1]]
        loads.append(pltpu.make_async_copy(ref, held, in_sems.at[i]))
        loads[-1].start()
    stores = []
    total, width = rows_all.shape
    mine = me_ref[0] // h
    gate_lanes = round_up(cap, LANES)
    eye = iota((cap, gate_lanes), 0) == iota((cap, gate_lanes), 1)

    def cot(k):
        source = (mine ^ k) // 2
        return (cot_ref[source] if odd else cot_ref[source, mine % 2]).astype(F32)

    for i, k in enumerate(ks):
        span = slice(i * cap, (i + 1) * cap)
        row_ref = pick_ref(mine, k, row_refs[0], row_refs)
        rows_all[span, :] = row_ref[0:cap, :]
        gate = lane_sum(jnp.where(eye, take_split(row_ref, cap, gate_lanes), 0.0))
        pairs_all[span, :] = (gate * cot(k)).astype(BF16)
    tile = 384
    root = 0.7978845608028654
    cubic = 0.044715
    for b in range(h):
        loads[2 * b].wait()
        loads[2 * b + 1].wait()
        units = act_all.shape[2]
        w_in, w_out = weights_all.at[2 * b, :, :units], weights_all.at[2 * b + 1, :units, :]

        for m in range(total // tile):
            span = slice(m * tile, (m + 1) * tile)
            pre = mm(rows_all[span, :], w_in[...])
            square = pre * pre
            bent = jnp.tanh(pre * (root + (root * cubic) * square))
            upper = 0.5 + 0.5 * bent
            act = pre * upper
            slope = upper + act * (1.0 - upper) * (2.0 * root + (6.0 * root * cubic) * square)
            act_low = act.astype(BF16)
            act_all[b, span, :] = act_low
            act_grad = contract_last(pairs_all[span, :], w_out[...])
            pre_grad = (act_grad * slope).astype(BF16)
            pre_all[b, span, :] = pre_grad
            result = mm(act_low, w_out[...])
            back = contract_last(pre_grad, w_in[...])
            if b == 0:
                result_sum[span, :] = result
                back_sum[span, :] = back
            else:
                result_sum[span, :] += result
                back_sum[span, :] += back
        for i, pair in enumerate(((act_all, act_refs), (pre_all, pre_refs))):
            copy = pltpu.make_async_copy(pair[0].at[b], pair[1][b], out_sems.at[2 * b + i])
            copy.start()
            stores.append(copy)
    if odd:
        for i in range(n):
            result_ref[mine ^ (2 * i)] = before_ref[i]
    for i, k in enumerate(ks):
        span = slice(i * cap, (i + 1) * cap)
        result = result_sum[span, :].astype(BF16)
        result_ref[mine ^ k if odd else i] = result
        back_ref = pick_ref(mine, k, back_refs[0], back_refs)
        back_ref[0:cap, :] = back_sum[span, :].astype(BF16)
        dots = lane_sum(cot(k) * result.astype(F32))
        put_split(back_ref, cap, row_sum(jnp.where(eye, dots, 0.0)))
    for copy in stores:
        copy.wait()


def expert_part(cfg, odd, me, cot, rows, weights, before):
    n, h = cfg.experts // 2, cfg.hidden
    width, units = cot.shape[-1], weights[0].shape[1]
    slots = n * cfg.cap
    many = len(rows)
    outs = call(
        functools.partial(expert_kernel, cfg, odd),
        [shape((2 * n if odd else n, cfg.cap, width), BF16)]
        + [shape(r.shape, BF16) for r in rows]
        + [shape((slots, width), BF16)]
        + [shape((slots, units), BF16)] * (2 * h),
        [pltpu.VMEM((slots, width), BF16)]
        + [pltpu.VMEM((slots, width), F32)] * 2
        + [pltpu.VMEM((2 * h, max(width, units), max(width, units)), BF16)]
        + [pltpu.VMEM((h, slots, units), BF16)] * 2
        + [pltpu.SemaphoreType.DMA((2 * h,))] * 2,
        [me, cot] + rows + weights + before,
        8 * slots * width * units * h,
        smem=(0,),
        far_in=range(2 + many, 2 + many + 2 * h),
        far_out=range(2 + many, 2 + many + 2 * h),
    )
    return outs[0], outs[1 : 1 + many], outs[1 + many], outs[2 + many : 2 + many + h], outs[2 + many + h :]


def weight_kernel(cfg, parts, first, me_ref, *refs):
    n = cfg.experts
    if first:
        even_ref, odd_refs = refs[0], refs[1 : 1 + n // 2]
        pair_refs, refs = refs[1 + n // 2 : 3 + n // 2], refs[3 + n // 2 :]
    else:
        turned_refs, refs = refs[:2], refs[2:]
    pre_refs, act_refs, refs = refs[: 2 * parts], refs[2 * parts : 4 * parts], refs[4 * parts :]
    if first:
        turned_refs, refs = refs[:2], refs[2:]
    out_refs = refs[:parts]
    rows_turned, pairs_turned = turned_refs
    width, total = rows_turned.shape
    if first:
        rows_all = refs[parts]
        cap, half = cfg.cap, total // 2
        for i in range(n):
            k = 2 * i if i < n // 2 else 2 * i - n + 1
            row_ref = pick_ref(me_ref[0] // cfg.hidden, k, even_ref, odd_refs)
            rows_all[i * cap : (i + 1) * cap, :] = row_ref[0:cap, :]
        rows_turned[...] = jnp.transpose(rows_all[...])
        pairs_turned[:, :half] = jnp.transpose(pair_refs[0][...])
        pairs_turned[:, half:] = jnp.transpose(pair_refs[1][...])
    half = total // 2
    for p in range(parts):
        for turned, half_refs, at in ((rows_turned, pre_refs, 0), (pairs_turned, act_refs, width)):
            value = mm(turned[:, :half], half_refs[2 * p][...])
            value = value + mm(turned[:, half:], half_refs[2 * p + 1][...])
            out_refs[p][at : at + width, :] = value.astype(out_refs[p].dtype)


def turn_add_kernel(*refs):
    terms, (sum_in, sum_out) = refs[:-2], refs[-2:]
    width = sum_in.shape[0]
    total = terms[0][...]
    for ref in terms[1:]:
        total = total + ref[...].astype(F32)
    sum_in[...] = total[:width, :]
    sum_out[...] = jnp.transpose(total[width:, :])


def backward_kernel(cfg, me_ref, side_ref, hidden_ref, gates_ref, cot_ref, heads_ref, full_ref, *refs):
    n, cap = cfg.experts, cfg.cap
    even_ref, odd_refs, refs = refs[0], refs[1 : 1 + n // 2], refs[1 + n // 2 :]
    hidden_grad_ref, heads_grad_ref, dense_ref, routed_sum, routed_ref, logits_ref = refs
    count, width = hidden_ref.shape
    me = me_ref[0]
    mine = me // cfg.hidden
    gain_one, bias_one, gain_two, bias_two = gain_rows(full_ref, 4 * width, cfg.gate_columns)
    gate_lanes = round_up(cap, LANES)
    one, two = side_ref[:, 0:1], side_ref[:, 1:2]
    dot_one = jnp.zeros((count, 1), F32)
    dot_two = jnp.zeros((count, 1), F32)
    for k in range(n):
        base = ((mine ^ k) * cap).astype(F32)
        slot = iota_f((count, cap), 1) + base
        pick = jnp.where((slot == one) | (slot == two), 1.0, 0.0).astype(BF16)
        back_ref = pick_ref(mine, k, even_ref, odd_refs)
        part = mm(pick, back_ref[0:cap, :])
        if k == 0:
            routed_sum[...] = part
        else:
            routed_sum[...] += part
        lane_at = iota_f((count, gate_lanes), 1)
        slot = jnp.where(lane_at < cap, lane_at + base, -1.0)
        dots = take_split(back_ref, cap, gate_lanes)
        dot_one = dot_one + lane_sum(jnp.where(slot == one, dots, 0.0))
        dot_two = dot_two + lane_sum(jnp.where(slot == two, dots, 0.0))
    gate_one, gate_two = gates_ref[:, 0:1], gates_ref[:, 1:2]
    shared = gate_one * dot_one + gate_two * dot_two
    chosen_one = gate_one * (dot_one - shared)
    chosen_two = gate_two * (dot_two - shared)
    gate_full = full_ref[:, 4 * width :]
    chunk = 128
    gain_sum = jnp.zeros((1, width), F32)
    bias_sum = jnp.zeros((1, width), F32)
    for c in range(count // chunk):
        span = slice(c * chunk, (c + 1) * chunk)
        column = iota_f((chunk, cfg.gate_lanes), 1)
        logits = jnp.where(column == side_ref[span, 2:3], chosen_one[span], 0.0) + jnp.where(
            column == side_ref[span, 3:4], chosen_two[span], 0.0
        )
        logits = logits.astype(BF16)
        logits_ref[span, :] = logits
        routed_grad = routed_sum[span, :] + contract_last(logits, gate_full)
        unit, inverse = norm_parts(hidden_ref[span, :])
        routed_ref[span, :] = (unit * gain_two + bias_two).astype(BF16)
        gain_sum = gain_sum + row_sum(routed_grad * unit)
        bias_sum = bias_sum + row_sum(routed_grad)
        hidden_grad = cot_ref[span, :].astype(F32) + norm_back(unit, inverse, gain_two, routed_grad)
        hidden_grad_ref[span, :] = hidden_grad
        low = hidden_grad.astype(BF16)
        routed_sum[span, :] = hidden_grad
        heads_grad_ref[span, :] = contract_last(low, full_ref[:, 3 * width : 4 * width]).astype(BF16)
    dense_ref[:, 0:width] = contract_first(heads_ref[...], routed_sum[...].astype(BF16))
    dense_ref[:, width:] = contract_first(routed_ref[...], logits_ref[...])
    tile = width + cfg.gate_columns // LANES * LANES
    lane = cfg.gate_columns % LANES
    dense_ref[:, tile : tile + LANES] += rows_to_lanes(gain_sum, bias_sum, lane + 2)


def rows_to_lanes(first, second, lane):
    down = iota((LANES, first.shape[1]), 0)
    return jnp.transpose(jnp.where(down == lane, first, jnp.where(down == lane + 1, second, 0.0)))


def put_dense(cfg, me, dense_ref, outs):
    if len(outs) == 1:
        outs[0][...] = dense_ref[...]
    else:
        take_blocks(cfg.owners, me, dense_ref, *outs)


def attention_back_kernel(
    cfg, me_ref, side_ref, rows_ref, tokens_ref, proj_ref, lse_ref, heads_grad_ref, hidden_grad_ref, first_ref, full_ref, *refs
):
    grad_ref = refs[0]
    dense = refs[1 : len(refs) - 4]
    bias_ref, low_ref, qkv_ref, dense_ref = refs[len(refs) - 4 :]
    count, width = tokens_ref.shape
    me = me_ref[0]
    gain_one, bias_one, gain_two, bias_two = gain_rows(full_ref, 4 * width, cfg.gate_columns)
    chunk = 128
    for c in range(count // chunk):
        span = slice(c * chunk, (c + 1) * chunk)
        unit, _ = norm_parts(tokens_ref[span, :].astype(F32))
        low_ref[span, :] = (unit * gain_one + bias_one).astype(BF16)
        bias_ref[span, :] = jnp.where(
            side_ref[span, 4:5] == rows_ref[4:5, :], 0.0, NEG_FILL
        )
    lane = iota((1, LANES), 1)
    scale = HEAD_DIM ** (-0.5)

    def slab(i, carry):
        off = pl.multiple_of(i * LANES, LANES)
        queries = proj_ref[:, pl.ds(off, LANES)]
        keys = proj_ref[:, pl.ds(width + off, LANES)]
        values = proj_ref[:, pl.ds(2 * width + off, LANES)]
        grads = heads_grad_ref[:, pl.ds(off, LANES)]
        query_grad = jnp.zeros((count, LANES), F32)
        key_grad = jnp.zeros((count, LANES), F32)
        value_grad = jnp.zeros((count, LANES), F32)
        for half in (0, 1):
            mine = jnp.where(lane // HEAD_DIM == half, 1.0, 0.0).astype(BF16)
            query_half, key_half, grads_half = queries * mine, keys * mine, grads * mine
            logs = lane_sum(jnp.where(lane == 2 * i + half, lse_ref[...], 0.0))
            probs = jnp.exp(contract_last(queries, key_half) * scale + bias_ref[...] - logs)
            prob_grad = contract_last(grads_half, values)
            row_dot = lane_sum(probs * prob_grad)
            score_grad = (probs * (prob_grad - row_dot)).astype(BF16)
            value_grad = value_grad + contract_first(probs.astype(BF16), grads_half)
            query_grad = query_grad + mm(score_grad, key_half)
            key_grad = key_grad + contract_first(score_grad, query_half)
        qkv_ref[:, pl.ds(off, LANES)] = (query_grad * scale).astype(BF16)
        qkv_ref[:, pl.ds(width + off, LANES)] = (key_grad * scale).astype(BF16)
        qkv_ref[:, pl.ds(2 * width + off, LANES)] = value_grad.astype(BF16)
        return carry

    lax.fori_loop(0, width // LANES, slab, 0)
    dense_ref[:, : 3 * width] = contract_first(low_ref[...], qkv_ref[...])
    gain_sum = jnp.zeros((1, width), F32)
    bias_sum = jnp.zeros((1, width), F32)
    for c in range(count // chunk):
        span = slice(c * chunk, (c + 1) * chunk)
        normed_grad = contract_last(qkv_ref[span, :], full_ref[:, : 3 * width])
        unit, inverse = norm_parts(tokens_ref[span, :].astype(F32))
        gain_sum = gain_sum + row_sum(normed_grad * unit)
        bias_sum = bias_sum + row_sum(normed_grad)
        grad_ref[span, :] = hidden_grad_ref[span, :] + norm_back(unit, inverse, gain_one, normed_grad)
    dense_ref[:, 3 * width :] = first_ref[...]
    tile = 4 * width + cfg.gate_columns // LANES * LANES
    lane = cfg.gate_columns % LANES
    dense_ref[:, tile : tile + LANES] += rows_to_lanes(gain_sum, bias_sum, lane)
    put_dense(cfg, me, dense_ref, dense)


def output_kernel(cfg, side_ref, hidden_ref, gates_ref, result_ref, out_ref):
    cap = cfg.cap
    count = hidden_ref.shape[0]
    total_one = jnp.zeros(hidden_ref.shape, F32)
    total_two = jnp.zeros(hidden_ref.shape, F32)
    for e in range(cfg.experts):
        slot = iota_f((count, cap), 1) + float(e * cap)
        pick_one = jnp.where(slot == side_ref[:, 0:1], 1.0, 0.0).astype(BF16)
        pick_two = jnp.where(slot == side_ref[:, 1:2], 1.0, 0.0).astype(BF16)
        total_one = total_one + mm(pick_one, result_ref[e])
        total_two = total_two + mm(pick_two, result_ref[e])
    mixed = gates_ref[:, 0:1] * total_one + gates_ref[:, 1:2] * total_two
    out_ref[...] = (hidden_ref[...] + mixed).astype(BF16)


class Config:
    pass


def after(value, other):
    return lax.optimization_barrier((value, other))[0]


def apart(always, part, *args):
    given = jax.eval_shape(part, *args)

    def never(*_):
        return jax.tree.map(lambda s: jnp.zeros(s.shape, s.dtype), given)

    return lax.cond(always, part, never, *args)


def swap_hidden(value, mask):
    size = lax.axis_size("hidden")
    return lax.ppermute(value, "hidden", [(i, i ^ mask) for i in range(size)])


def swap_expert(value, mask):
    size = lax.axis_size("expert")
    return lax.ppermute(value, "expert", [(i, i ^ mask) for i in range(size)])


def gather_rest(own):
    blocks = [own]
    bit = 2
    while bit < lax.axis_size("hidden"):
        blocks += [swap_hidden(block, bit) for block in blocks]
        bit *= 2
    return blocks


def gather_core(half):
    return [swap_hidden(block, 1) for block in half]


def in_turn(first, second):
    return [block for pair in zip(first, second) for block in pair]


def sum_hidden(blocks):
    size = len(blocks)
    held = {i: [b] for i, b in enumerate(blocks)}
    bit = 1
    while bit < size:
        low = {i: v for i, v in held.items() if not i & bit}
        for i in low:
            terms = held[i ^ bit]
            value = terms[0]
            for term in terms[1:]:
                value = (value.astype(F32) + term.astype(F32)).astype(BF16)
            low[i] = low[i] + [swap_hidden(value, bit)]
        held = low
        bit *= 2
    return held[0], value


def body(
    tokens,
    lengths,
    task_ids,
    routes,
    w_qkv,
    w_attn_out,
    w_gate,
    ln1_gain,
    ln1_bias,
    ln2_gain,
    ln2_bias,
    w_in,
    w_out,
    cotangent,
):
    count, width = tokens.shape
    cfg = Config()
    cfg.experts = lax.axis_size("expert")
    cfg.hidden = lax.axis_size("hidden")
    experts, hidden = cfg.experts, cfg.hidden
    cfg.cap = cap = (3 * count * routes.shape[1] + 2 * experts - 1) // (2 * experts)
    cfg.gate_columns = w_gate.shape[1]
    cfg.gate_lanes = round_up(cfg.gate_columns + 4, LANES)
    devices = experts * hidden
    groups = Groups(devices)
    shard_rows = w_qkv.shape[0]
    staged = shard_rows % 16 == 0
    cfg.owners = groups.owners()
    me = (lax.axis_index("expert") * hidden + lax.axis_index("hidden")).astype(jnp.int32)[None]
    extra = 16
    units = w_in.shape[2]
    slots = experts * cap
    wide = 4 * width + cfg.gate_lanes
    one_dot = 2 * count * width * width

    packed = jnp.concatenate(
        [w_qkv, w_attn_out, w_gate]
        + [v[:, None] for v in (ln1_gain, ln1_bias, ln2_gain, ln2_bias)]
        + [jnp.zeros((shard_rows, cfg.gate_lanes - cfg.gate_columns - 4), BF16)],
        axis=1,
    )
    always = lengths[0, 0] > 0

    def first_part(packed, own_in, lengths, task_ids, routes, cotangent):
        far = groups.gather_far(packed) if staged else packed
        in_half = gather_rest(own_in)
        made = call(
            functools.partial(prep_kernel, cfg),
            [
                shape((count, LANES), F32),
                shape((8, count), F32),
                shape((experts // 2, 2, cap, width), BF16),
            ],
            [],
            [lengths, task_ids, routes, cotangent],
            3 * one_dot,
        )
        return far, in_half, made

    dense_far, in_half, (side, rows, sent_cot) = apart(
        always, first_part, packed, w_in[0], lengths, task_ids, routes, cotangent
    )
    if staged:
        dense_blocks = groups.gather_near(dense_far)
        reached = dense_blocks[1 : len(groups.mid)]
    else:
        dense_blocks = [lax.all_gather(packed, BOTH, axis=0, tiled=True)]
        reached = dense_blocks[0]
    cfg.blocks = len(dense_blocks)
    parity = [list(range(i, experts, 2)) for i in (0, 1)]

    def exchange_even(value):
        return lax.all_to_all(
            value, "expert", split_axis=0, concat_axis=0, axis_index_groups=parity, tiled=True
        )

    def exchange_odd(values):
        return [swap_expert(value, 2 * i + 1) for i, value in enumerate(values)]

    cot_even = exchange_even(sent_cot)
    other = 1 - lax.axis_index("expert") % 2
    cot_odd = lax.dynamic_index_in_dim(cot_even, other, 1, keepdims=False)
    out_half = gather_rest(after(w_out[0], reached))

    outs = call(
        functools.partial(forward_kernel, cfg),
        [
            shape((width, wide), BF16),
            shape((count, 3 * width), BF16),
            shape((count, width), BF16),
            shape((count, LANES), F32),
            shape((count, width), F32),
            shape((count, LANES), F32),
        ]
        + [shape((experts // 2, cap + extra, width), BF16)]
        + [shape((cap + extra, width), BF16)] * (experts // 2),
        [pltpu.VMEM((count, count), F32), pltpu.VMEM((count, width), BF16)],
        [me, side, rows, tokens] + dense_blocks,
        12 * one_dot,
        smem=(0,),
    )
    full, proj, heads, lse, hidden_one, gates = outs[:6]
    send_rows = outs[6:]
    def even_part(even_send, odd_send, cot_even, cot_odd, in_half, out_half):
        more_in, more_out = gather_core(in_half), gather_core(out_half)
        blocks = in_turn(in_half, more_in) + in_turn(out_half, more_out)
        even_rows = exchange_even(even_send)
        odd_rows = exchange_odd(odd_send)
        cot_odd = swap_expert(cot_odd, 1)
        out = expert_part(cfg, 0, me, cot_even, [even_rows], blocks, [])
        return even_rows, odd_rows, cot_odd, more_in, more_out, out

    def odd_part(even_send, odd_rows, cot_odd, blocks, before):
        even_back = exchange_even(even_send)
        return even_back, expert_part(cfg, 1, me, cot_odd, odd_rows, blocks, [before])

    def weight_part(odd_send, even_rows, odd_rows, even_out, odd_out):
        odd_back = exchange_odd(odd_send)
        grads, turned = {}, []
        for odd in (1, 0):
            picked = [b for b in range(hidden) if b % 2 == odd]
            pre = [o[2][b] for b in picked for o in (even_out, odd_out)]
            act = [o[1][b] for b in picked for o in (even_out, odd_out)]
            lead = [even_rows] + odd_rows + [even_out[0], odd_out[0]] if odd else turned
            outs = call(
                functools.partial(weight_kernel, cfg, len(picked), bool(odd)),
                [shape((width, slots), BF16)] * (2 * odd)
                + [shape((2 * width, units), BF16 if b else F32) for b in picked],
                [pltpu.VMEM((slots, width), BF16)] * odd,
                [me] + lead + pre + act,
                4 * slots * width * units * len(picked),
                smem=(0,),
            )
            if odd:
                turned, outs = outs[:2], outs[2:]
            grads.update(zip(picked, outs))
        return odd_back, [grads[b] for b in range(hidden)]

    even_rows, odd_rows, cot_odd, more_in, more_out, even_out = apart(
        always, even_part, send_rows[0], send_rows[1:], cot_even, cot_odd, in_half, out_half
    )
    weight_blocks = in_turn(in_half, more_in) + in_turn(out_half, more_out)
    even_back, odd_out = apart(
        always, odd_part, even_out[1][0], odd_rows, cot_odd, weight_blocks, even_out[0]
    )
    result = odd_out[0]
    odd_back, grads = apart(
        always, weight_part, odd_out[1], even_rows, odd_rows, even_out[2:], odd_out[2:]
    )
    back = [even_back] + odd_back
    terms, last_sent = sum_hidden(grads)
    returned = lax.all_to_all(
        after(result, back), "expert", split_axis=0, concat_axis=0, tiled=True
    )
    outs = call(
        functools.partial(backward_kernel, cfg),
        [
            shape((count, width), F32),
            shape((count, width), BF16),
            shape((width, width + cfg.gate_lanes), F32),
        ],
        [
            pltpu.VMEM((count, width), F32),
            pltpu.VMEM((count, width), BF16),
            pltpu.VMEM((count, cfg.gate_lanes), BF16),
        ],
        [me, side, hidden_one, gates, cotangent, heads, full] + back,
        7 * one_dot,
        smem=(0,),
    )
    hidden_grad, heads_grad, dense_one = after(outs, last_sent)

    if staged:
        dense_shapes = [shape((width // 2, wide), F32), shape((width // 2, wide), BF16)]
    else:
        dense_shapes = [shape((width, wide), F32)]
    outs = call(
        functools.partial(attention_back_kernel, cfg),
        [shape((count, width), F32)] + dense_shapes,
        [
            pltpu.VMEM((count, count), F32),
            pltpu.VMEM((count, width), BF16),
            pltpu.VMEM((count, 3 * width), BF16),
            pltpu.VMEM((width, wide), F32),
        ],
        [me, side, rows, tokens, proj, lse, heads_grad, hidden_grad, dense_one, full],
        12 * one_dot,
        smem=(0,),
    )
    outs = after(outs, terms)
    grad_tokens = outs[0]
    grad_in, grad_out = call(
        turn_add_kernel,
        [shape((width, units), F32), shape((units, width), F32)],
        [],
        terms,
        4 * width * units,
    )

    layer_out = call(
        functools.partial(output_kernel, cfg),
        shape((count, width), BF16),
        [],
        [side, hidden_one, gates, returned],
        6 * one_dot,
    )
    if staged:
        dense_terms = sum_to_owner(groups, *outs[1:], (layer_out, grad_in))
    else:
        dense_terms = [lax.psum_scatter(outs[1], BOTH, scatter_dimension=0, tiled=True)]
    dense_outs = call(
        functools.partial(split_kernel, cfg),
        [shape((shard_rows, c), F32) for c in (3 * width, width, cfg.gate_columns)]
        + [shape((1, shard_rows), F32)] * 4,
        [],
        dense_terms,
        shard_rows * wide,
    )

    return (
        layer_out,
        grad_tokens,
        *dense_outs[:3],
        *[v.reshape(shard_rows) for v in dense_outs[3:]],
        grad_in[None],
        grad_out[None],
    )


def solution(mesh):
    split = P(BOTH, None)
    vector = P(BOTH)
    placed = (split,) * 7 + (vector,) * 4 + (P("expert", None, "hidden"), P("expert", "hidden", None), split)
    return jax.shard_map(
        body,
        mesh=mesh,
        in_specs=placed,
        out_specs=(split,) * 5
        + (vector,) * 4
        + (P("expert", None, "hidden"), P("expert", "hidden", None)),
        check_vma=False,
    )
```

```python
import functools

import jax
import jax.numpy as jnp
from jax import lax
from jax.experimental import pallas as pl
from jax.experimental.pallas import tpu as pltpu
from jax.sharding import PartitionSpec as P

HEADS = 8
HEAD_DIM = 64
EPS = 1e-05
NEG_FILL = -1e30
LANES = 128
BOTH = ("expert", "hidden")
F32 = jnp.float32
BF16 = jnp.bfloat16
VMEM_LIMIT = 56 * 1024 * 1024
SMALL_LIMIT = 8 * 1024 * 1024


def mm(left, right):
    return jnp.dot(left, right, preferred_element_type=F32)


def contract_last(left, right):
    return lax.dot_general(left, right, (((1,), (1,)), ((), ())), preferred_element_type=F32)


def contract_first(left, right):
    return lax.dot_general(left, right, (((0,), (0,)), ((), ())), preferred_element_type=F32)


def iota(shape, axis):
    return lax.broadcasted_iota(jnp.int32, shape, axis)


def iota_f(shape, axis):
    return iota(shape, axis).astype(F32)


def lane_sum(values):
    return jnp.sum(values, axis=1, keepdims=True)


def row_sum(values):
    return jnp.sum(values, axis=0, keepdims=True)


def norm_parts(values):
    middle = jnp.mean(values, axis=-1, keepdims=True)
    centred = values - middle
    spread = jnp.mean(centred * centred, axis=-1, keepdims=True)
    inverse = lax.rsqrt(spread + EPS)
    return centred * inverse, inverse


def norm_back(unit, inverse, gain, grad):
    scaled = grad * gain
    mean_one = jnp.mean(scaled, axis=-1, keepdims=True)
    mean_two = jnp.mean(scaled * unit, axis=-1, keepdims=True)
    return inverse * (scaled - mean_one - unit * mean_two)


def round_up(value, step):
    return (value + step - 1) // step * step


def call(kernel, outs, scratch, args, flops, smem=(), far_in=(), far_out=(), limit=VMEM_LIMIT):
    def spec(at):
        space = pltpu.SMEM if at in smem else pl.ANY if at in far_in else pltpu.VMEM
        return pl.BlockSpec(memory_space=space)

    def out_spec(at):
        return pl.BlockSpec(memory_space=pl.ANY if at in far_out else pltpu.VMEM)

    touched = sum(a.size * a.dtype.itemsize for a in args) + sum(
        o.size * o.dtype.itemsize for o in jax.tree.leaves(outs)
    )
    got = pl.pallas_call(
        kernel,
        out_shape=outs,
        in_specs=[spec(at) for at in range(len(args))],
        out_specs=[out_spec(at) for at in range(len(outs))] if isinstance(outs, list) else out_spec(0),
        scratch_shapes=scratch,
        compiler_params=pltpu.CompilerParams(vmem_limit_bytes=limit),
        cost_estimate=pl.CostEstimate(flops=1, bytes_accessed=1, transcendentals=0),
    )(*args)
    return list(got) if isinstance(outs, list) else got


def shape(dims, dtype):
    return jax.ShapeDtypeStruct(dims, dtype)


def slot_targets(cfg, routes_ref):
    count, experts = routes_ref.shape[0], cfg.experts
    routes = routes_ref[...].astype(F32)
    first, second = routes[:, 0:1], routes[:, 1:2]
    lane_e = iota_f((count, experts), 1)
    hot_one = jnp.where(lane_e == first, 1.0, 0.0)
    hot_two = jnp.where(lane_e == second, 1.0, 0.0)
    before = jnp.where(iota((count, count), 1) < iota((count, count), 0), 1.0, 0.0).astype(BF16)
    earlier = mm(before, (hot_one + hot_two).astype(BF16))
    target_one = first * cfg.cap + lane_sum(earlier * hot_one)
    target_two = second * cfg.cap + lane_sum(earlier * hot_two)
    return first, second, target_one, target_two


def prep_kernel(cfg, lens_ref, tasks_ref, routes_ref, cot_ref, side_ref, rows_ref, sent_ref):
    experts, cap = cfg.experts, cfg.cap
    count = routes_ref.shape[0]
    sents = lens_ref.shape[1]
    lens = lens_ref[...].astype(F32)
    tasks = tasks_ref[...].astype(F32)
    down, across = iota((sents, sents), 0), iota((sents, sents), 1)
    ends_col = lane_sum(jnp.where(across <= down, lens, 0.0))
    ends_row = row_sum(jnp.where(across == down, ends_col, 0.0))
    passed = jnp.where(iota_f((count, sents), 0) >= ends_row, 1.0, 0.0)
    sentence = lane_sum(passed)
    task = lane_sum(jnp.where(iota_f((count, sents), 1) == sentence, tasks, 0.0))
    lane = iota((count, LANES), 1)
    first, second, target_one, target_two = slot_targets(cfg, routes_ref)
    side = jnp.where(lane == 0, target_one, 0.0)
    side = jnp.where(lane == 1, target_two, side)
    side = jnp.where(lane == 2, task * experts + first, side)
    side = jnp.where(lane == 3, task * experts + second, side)
    side = jnp.where(lane == 4, sentence, side)
    side = jnp.where(lane == 5, first, side)
    side = jnp.where(lane == 6, second, side)
    side_ref[...] = side
    turned = jnp.transpose(side)
    rows_ref[...] = turned[0:8, :]
    one_row, two_row = turned[0:1, :], turned[1:2, :]
    cot = cot_ref[...]
    for e in range(experts):
        at = iota_f((cap, count), 0) + float(e * cap)
        pick = jnp.where((at == one_row) | (at == two_row), 1.0, 0.0).astype(BF16)
        sent_ref[e // 2, e % 2] = mm(pick, cot).astype(BF16)


class Groups:
    def __init__(self, devices):
        bits = devices.bit_length() - 1
        mid = (bits - 1) // 2
        self.near = [1]
        self.mid = self.masks(1, mid)
        self.far = self.masks(1 + mid, bits - 1 - mid)
        self.devices = devices

    @staticmethod
    def masks(low, width):
        return [m << low for m in range(1 << width)]

    def owners(self):
        return [[n | b | c for c in self.far] for n in (0, 1) for b in self.mid]

    def swap(self, value, mask):
        return lax.ppermute(value, BOTH, [(i, i ^ mask) for i in range(self.devices)])

    def gather_far(self, shard):
        return jnp.concatenate([shard] + [self.swap(shard, m) for m in self.far[1:]], axis=0)

    def gather_near(self, far):
        mid = [far] + [self.swap(far, m) for m in self.mid[1:]]
        return mid + [self.swap(block, 1) for block in mid]


def add_kernel(parts, keep_ref, *refs):
    got, outs = refs[: len(refs) - parts], refs[len(refs) - parts :]
    rows = outs[0].shape[0]
    for i, out_ref in enumerate(outs):
        span = slice(i * rows, (i + 1) * rows)
        total = keep_ref[span, :].astype(F32)
        for ref in got:
            total = total + ref[span, :].astype(F32)
        out_ref[...] = total.astype(out_ref.dtype)


def add_parts(keep, got, parts):
    rows, columns = keep.shape
    outs = [shape((rows // parts, columns), F32 if i == 0 else BF16) for i in range(parts)]
    return call(
        functools.partial(add_kernel, parts), outs, [], [keep] + got, rows * columns * len(got), limit=SMALL_LIMIT
    )


def split_kernel(cfg, *refs):
    terms, outs = refs[:-7], refs[-7:]
    rows, width = outs[0].shape[0], outs[1].shape[1]

    def total(start, stop):
        value = terms[0][:, start:stop]
        for ref in terms[1:]:
            value = value + ref[:, start:stop].astype(F32)
        return value

    outs[0][...] = total(0, 3 * width)
    outs[1][...] = total(3 * width, 4 * width)
    outs[2][...] = total(4 * width, 4 * width + cfg.gate_columns)
    tile = 4 * width + cfg.gate_columns // LANES * LANES
    lane = cfg.gate_columns % LANES
    turned = jnp.transpose(total(tile, tile + LANES))
    for i in range(4):
        outs[3 + i][...] = turned[lane + i : lane + i + 1, :]


def gain_rows(full_ref, start, gate_columns):
    tile = start + gate_columns // LANES * LANES
    lane = gate_columns % LANES
    turned = jnp.transpose(full_ref[:, tile : tile + LANES].astype(F32))
    return [turned[lane + i : lane + i + 1, :] for i in range(4)]


def forward_kernel(cfg, me_ref, side_ref, rows_ref, tokens_ref, *refs):
    n, cap = cfg.experts, cfg.cap
    blocks, refs = refs[: cfg.blocks], refs[cfg.blocks :]
    outs, refs = refs[:6], refs[6:]
    even_out, odd_outs, refs = refs[0], refs[1 : 1 + n // 2], refs[1 + n // 2 :]
    full_ref, proj_ref, heads_ref, turned_ref, hidden_ref, gates_ref, send_all = refs[:7]
    bias_ref, routed_ref, lse_ref, in_sems, out_sems = refs[7:]
    count, width = tokens_ref.shape
    me = me_ref[0]
    mine = me // cfg.hidden
    loads, stores = Copies(in_sems), Copies(out_sems)
    if len(blocks) == 1:
        loads.start(blocks[0], full_ref)
    else:
        for block_ref, masks in zip(blocks, cfg.owners):
            rows = block_ref.shape[0] // len(masks)
            for i, mask in enumerate(masks):
                at = pl.multiple_of((me ^ mask) * rows, rows)
                loads.start(block_ref.at[i * rows : (i + 1) * rows], full_ref.at[pl.ds(at, rows)])
    chunk = 128
    for c in range(count // chunk):
        span = slice(c * chunk, (c + 1) * chunk)
        bias_ref[span, :] = jnp.where(side_ref[span, 4:5] == rows_ref[4:5, :], 0.0, NEG_FILL)
    loads.finish()
    stores.start(full_ref, outs[0])
    gain_one, bias_one, gain_two, bias_two = gain_rows(full_ref, 4 * width, cfg.gate_columns)
    for c in range(count // chunk):
        span = slice(c * chunk, (c + 1) * chunk)
        unit, _ = norm_parts(tokens_ref[span, :].astype(F32))
        routed_ref[span, :] = (unit * gain_one + bias_one).astype(BF16)
    proj_ref[...] = mm(routed_ref[...], full_ref[:, : 3 * width]).astype(BF16)
    stores.start(proj_ref, outs[1])
    lse_ref[...] = jnp.zeros_like(lse_ref)
    lane = iota((1, LANES), 1)
    scale = HEAD_DIM ** (-0.5)
    block = 256

    def slab(i, carry):
        off = pl.multiple_of(i * LANES, LANES)
        keys = proj_ref[:, pl.ds(width + off, LANES)]
        values = proj_ref[:, pl.ds(2 * width + off, LANES)]
        halves = []
        for half in (0, 1):
            mine = jnp.where(lane // HEAD_DIM == half, 1.0, 0.0).astype(BF16)
            halves.append((keys * mine, values * mine))
        for r in range(count // block):
            span = slice(r * block, (r + 1) * block)
            queries = proj_ref[span, pl.ds(off, LANES)]
            total = jnp.zeros((block, LANES), F32)
            logs = lse_ref[span, :]
            for half, (key_half, value_half) in enumerate(halves):
                scores = contract_last(queries, key_half) * scale + bias_ref[span, :]
                highest = jnp.max(scores, axis=1, keepdims=True)
                expo = jnp.exp(scores - highest)
                sums = lane_sum(expo)
                probs = (expo * (1.0 / sums)).astype(BF16)
                total = total + mm(probs, value_half)
                logs = jnp.where(lane == 2 * i + half, highest + jnp.log(sums), logs)
            heads_ref[span, pl.ds(off, LANES)] = total.astype(BF16)
            lse_ref[span, :] = logs
        return carry

    lax.fori_loop(0, width // LANES, slab, 0)
    stores.start(heads_ref, outs[2])
    turned_ref[...] = jnp.transpose(lse_ref[...])[:HEADS, :]
    stores.start(turned_ref, outs[3])
    for c in range(count // chunk):
        span = slice(c * chunk, (c + 1) * chunk)
        attended = mm(heads_ref[span, :], full_ref[:, 3 * width : 4 * width])
        hidden = tokens_ref[span, :].astype(F32) + attended
        hidden_ref[span, :] = hidden
        unit, _ = norm_parts(hidden)
        routed = (unit * gain_two + bias_two).astype(BF16)
        routed_ref[span, :] = routed
        logits = mm(routed, full_ref[:, 4 * width :])
        column = iota_f(logits.shape, 1)
        one = lane_sum(jnp.where(column == side_ref[span, 2:3], logits, 0.0))
        two = lane_sum(jnp.where(column == side_ref[span, 3:4], logits, 0.0))
        top = jnp.maximum(one, two)
        expo_one, expo_two = jnp.exp(one - top), jnp.exp(two - top)
        both = expo_one + expo_two
        gates_ref[span, :] = jnp.where(
            lane == 0, expo_one / both, jnp.where(lane == 1, expo_two / both, 0.0)
        )
    stores.start(hidden_ref, outs[4])
    stores.start(gates_ref, outs[5])
    routed = routed_ref[...]
    gate_lanes = round_up(cap, LANES)
    for k in range(n):
        base = ((mine ^ k) * cap).astype(F32)
        at = iota_f((cap, count), 0) + base
        pick = (at == rows_ref[0:1, :]) | (at == rows_ref[1:2, :])
        send_all[k, 0:cap, :] = mm(jnp.where(pick, 1.0, 0.0).astype(BF16), routed).astype(BF16)
        slot = iota_f((count, gate_lanes), 1) + base
        row = row_sum(
            jnp.where(slot == side_ref[:, 0:1], gates_ref[:, 0:1], 0.0)
            + jnp.where(slot == side_ref[:, 1:2], gates_ref[:, 1:2], 0.0)
        )
        put_split(send_all.at[k], cap, row)
        stores.start(send_all.at[k], pick_ref(mine, k, even_out, odd_outs))
    stores.finish()


def pick_ref(mine, k, even_ref, odd_refs):
    return odd_refs[k // 2] if k % 2 else even_ref.at[(mine ^ k) // 2]


def put_split(ref, cap, row):
    extra = ref.shape[0] - cap
    high = row.astype(BF16).astype(F32)
    down = iota((extra, row.shape[1]), 0)
    both = jnp.where(down == 0, high, jnp.where(down == 1, row - high, 0.0))
    ref[cap:, :] = jnp.zeros((extra, ref.shape[1]), BF16)
    ref[cap:, 0 : row.shape[1]] = both.astype(BF16)


def take_split(ref, cap, lanes):
    both = ref[cap:, 0:lanes].astype(F32)
    return both[0:1, :] + both[1:2, :]


def gelu_parts(pre):
    root = 0.7978845608028654
    cubic = 0.044715
    square = pre * pre
    upper = 0.5 + 0.5 * jnp.tanh(pre * (root + (root * cubic) * square))
    act = pre * upper
    return act, upper + act * (1.0 - upper) * (2.0 * root + (6.0 * root * cubic) * square)


class Copies:
    def __init__(self, sems):
        self.sems, self.count, self.open = sems, 0, []

    def start(self, source, target, kept=True):
        copy = pltpu.make_async_copy(source, target, self.sems.at[self.count])
        self.count += 1
        copy.start()
        if kept:
            self.open.append(copy)
        return copy

    def finish(self):
        for copy in self.open:
            copy.wait()


def expert_kernel(cfg, odd, me_ref, *refs):
    h, cap, n = cfg.hidden, cfg.cap, cfg.experts // 2
    many = n if odd else 1
    cot_ref, refs = refs[0], refs[1:]
    row_refs, refs = refs[:many], refs[many:]
    in_refs, out_refs, refs = refs[:h], refs[h : 2 * h], refs[2 * h :]
    if odd:
        before_ref, refs = refs[0], refs[1:]
    result_ref, back_refs, refs = refs[0], refs[1 : 1 + many], refs[1 + many :]
    pairs_ref, refs = refs[0], refs[1:]
    rows_all, cot_all, pairs_all, result_all, back_all, before_all, extra_in, extra_out = refs[:8]
    result_sum, back_sum, weights_all, in_sems, out_sems = refs[8:]
    total, width = rows_all.shape
    extra = extra_in.shape[1]
    mine = me_ref[0] // h
    loads, stores = Copies(in_sems), Copies(out_sems)
    ks = list(range(odd, 2 * n, 2))
    tiles = 2
    per = n // tiles
    tile = per * cap
    row_loads, weight_loads = [], []

    def load_rows(m):
        for i in range(m * per, (m + 1) * per):
            span = slice(i * cap, (i + 1) * cap)
            source = (mine ^ ks[i]) // 2
            row_ref = pick_ref(mine, ks[i], row_refs[0], row_refs)
            from_ref = cot_ref.at[source] if odd else cot_ref.at[source, mine % 2]
            row_loads.append(
                (
                    loads.start(row_ref.at[0:cap], rows_all.at[span], False),
                    loads.start(row_ref.at[cap : cap + extra], extra_in.at[i], False),
                    loads.start(from_ref, cot_all.at[span], False),
                )
            )

    load_rows(0)
    for i, ref in enumerate(in_turn(in_refs, out_refs)):
        held = weights_all.at[i, : ref.shape[0], : ref.shape[1]]
        weight_loads.append(loads.start(ref, held, False))
    for m in range(1, tiles):
        load_rows(m)
    if odd:
        before_loads = [loads.start(before_ref.at[i], before_all.at[i], False) for i in range(n)]
    gate_lanes = round_up(cap, LANES)
    eye = iota((cap, gate_lanes), 0) == iota((cap, gate_lanes), 1)
    units = in_refs[0].shape[1]
    gates = {}
    for m in range(tiles):
        span = slice(m * tile, (m + 1) * tile)
        for i in range(m * per, (m + 1) * per):
            for copy in row_loads[i]:
                copy.wait()
            rows = slice(i * cap, (i + 1) * cap)
            gates[i] = lane_sum(jnp.where(eye, take_split(extra_in.at[i], 0, gate_lanes), 0.0))
            pairs_all[rows, :] = (gates[i] * cot_all[rows, :].astype(F32)).astype(BF16)
        stores.start(pairs_all.at[span], pairs_ref.at[span])
        for b in range(h):
            if m == 0:
                weight_loads[2 * b].wait()
                weight_loads[2 * b + 1].wait()
            w_in, w_out = weights_all.at[2 * b, :, :units], weights_all.at[2 * b + 1, :units, :]
            act, slope = gelu_parts(mm(rows_all[span, :], w_in[...]))
            act_low = act.astype(BF16)
            act_grad = contract_last(pairs_all[span, :], w_out[...])
            pre_grad = (act_grad * slope).astype(BF16)
            result = mm(act_low, w_out[...])
            back = contract_last(pre_grad, w_in[...])
            if b == 0:
                result_sum[...] = result
                back_sum[...] = back
            elif b < h - 1:
                result_sum[...] += result
                back_sum[...] += back
            else:
                result_sum[...] += result
                back_all[span, :] = (back_sum[...] + back).astype(BF16)
        if odd and m == 0:
            for i in range(n):
                before_loads[i].wait()
                stores.start(before_all.at[i], result_ref.at[mine ^ (2 * i)])
        for i in range(m * per, (m + 1) * per):
            rows, k = slice(i * cap, (i + 1) * cap), ks[i]
            back_ref = pick_ref(mine, k, back_refs[0], back_refs)
            stores.start(back_all.at[rows], back_ref.at[0:cap])
            result = result_sum[(i - m * per) * cap : (i - m * per + 1) * cap, :]
            result_all[rows, :] = (gates[i] * result).astype(BF16)
            stores.start(result_all.at[rows], result_ref.at[mine ^ k if odd else i])
            dots = lane_sum(cot_all[rows, :].astype(F32) * result)
            put_split(extra_out.at[i], 0, row_sum(jnp.where(eye, dots, 0.0)))
            stores.start(extra_out.at[i], back_ref.at[cap : cap + extra])
    stores.finish()


def expert_part(cfg, odd, me, cot, rows, weights, before):
    n, h, cap, extra = cfg.experts // 2, cfg.hidden, cfg.cap, 16
    width, units = cot.shape[-1], weights[0].shape[1]
    slots = n * cap
    many = len(rows)
    side = max(width, units)
    args = [me, cot] + rows + weights + before
    outs = (
        [shape((2 * n if odd else n, cap, width), BF16)]
        + [shape(r.shape, BF16) for r in rows]
        + [shape((slots, width), BF16)]
    )
    outs = call(
        functools.partial(expert_kernel, cfg, odd),
        outs,
        [pltpu.VMEM((slots, width), BF16)] * 5
        + [pltpu.VMEM((n, cap, width), BF16)]
        + [pltpu.VMEM((n, extra, width), BF16)] * 2
        + [pltpu.VMEM((slots // 2, width), F32)] * 2
        + [pltpu.VMEM((2 * h, side, side), BF16)]
        + [pltpu.SemaphoreType.DMA((4 * n + 2 * h,)), pltpu.SemaphoreType.DMA((4 * n + 2,))],
        args,
        8 * slots * width * units * h,
        smem=(0,),
        far_in=range(1, len(args)),
        far_out=range(len(outs)),
    )
    return outs[0], outs[1 : 1 + many], outs[1 + many]


def weight_kernel(cfg, parts, me_ref, *refs):
    n, cap = cfg.experts, cfg.cap
    even_ref, odd_refs, refs = refs[0], refs[1 : 1 + n // 2], refs[1 + n // 2 :]
    pair_refs, in_refs, out_refs, refs = refs[:2], refs[2 : 2 + parts], refs[2 + parts : 2 + 2 * parts], refs[2 + 2 * parts :]
    grad_refs, refs = refs[:parts], refs[parts:]
    grads_all, refs = refs[:parts], refs[parts:]
    rows_all, pairs_all, rows_turned, pairs_turned, act_all, pre_all, weights_all, in_sems, out_sems = refs
    total, width = rows_all.shape
    half = total // 2
    units = act_all.shape[1]
    mine = me_ref[0] // cfg.hidden
    loads, stores = Copies(in_sems), Copies(out_sems)
    waits = {0: [], 1: []}
    weight_loads = []
    for odd in (0, 1):
        for i in range(n // 2):
            k = 2 * i + odd
            span = slice(odd * half + i * cap, odd * half + (i + 1) * cap)
            row_ref = pick_ref(mine, k, even_ref, odd_refs)
            waits[odd].append(loads.start(row_ref.at[0:cap], rows_all.at[span], False))
        span = slice(odd * half, (odd + 1) * half)
        waits[odd].append(loads.start(pair_refs[odd], pairs_all.at[span], False))
        if not odd:
            for i, ref in enumerate(in_turn(in_refs, out_refs)):
                held = weights_all.at[i, : ref.shape[0], : ref.shape[1]]
                weight_loads.append(loads.start(ref, held, False))
    tile = half // 2
    for p in range(parts):
        weight_loads[2 * p].wait()
        weight_loads[2 * p + 1].wait()
        w_in, w_out = weights_all.at[2 * p, :, :units], weights_all.at[2 * p + 1, :units, :]
        for m in range(4):
            if p == 0 and m % 2 == 0:
                for copy in waits[m // 2]:
                    copy.wait()
                span = slice(m // 2 * half, (m // 2 + 1) * half)
                rows_turned[:, span] = jnp.transpose(rows_all[span, :])
                pairs_turned[:, span] = jnp.transpose(pairs_all[span, :])
            span = slice(m * tile, (m + 1) * tile)
            act, slope = gelu_parts(mm(rows_all[span, :], w_in[...]))
            act_all[span, :] = act.astype(BF16)
            act_grad = contract_last(pairs_all[span, :], w_out[...])
            pre_all[span, :] = (act_grad * slope).astype(BF16)
        kept = grads_all[p]
        kept[:width, :] = mm(rows_turned[...], pre_all[...]).astype(kept.dtype)
        kept[width:, :] = mm(pairs_turned[...], act_all[...]).astype(kept.dtype)
        stores.start(kept, grad_refs[p])
    stores.finish()


def weight_part(cfg, picked, me, even_rows, odd_rows, pairs, ins, outs):
    width, units = ins[0].shape
    slots, parts = cfg.experts * cfg.cap, len(picked)
    args = [me, even_rows] + odd_rows + pairs + [ins[b] for b in picked] + [outs[b] for b in picked]
    kinds = [BF16 if b else F32 for b in picked]
    side = max(width, units)
    return call(
        functools.partial(weight_kernel, cfg, parts),
        [shape((2 * width, units), kind) for kind in kinds],
        [pltpu.VMEM((2 * width, units), kind) for kind in kinds]
        + [pltpu.VMEM((slots, width), BF16)] * 2
        + [pltpu.VMEM((width, slots), BF16)] * 2
        + [pltpu.VMEM((slots, units), BF16)] * 2
        + [pltpu.VMEM((2 * parts, side, side), BF16)]
        + [pltpu.SemaphoreType.DMA((cfg.experts + 2 + 2 * parts,)), pltpu.SemaphoreType.DMA((parts,))],
        args,
        8 * slots * width * units * parts,
        smem=(0,),
        far_in=range(1, len(args)),
        far_out=range(parts),
    )


def turn_add_kernel(*refs):
    terms, (sum_in, sum_out) = refs[:-2], refs[-2:]
    width = sum_in.shape[0]
    total = terms[0][...]
    for ref in terms[1:]:
        total = total + ref[...].astype(F32)
    sum_in[...] = total[:width, :]
    sum_out[...] = jnp.transpose(total[width:, :])


def rows_to_lanes(first, second, lane):
    down = iota((LANES, first.shape[1]), 0)
    return jnp.transpose(jnp.where(down == lane, first, jnp.where(down == lane + 1, second, 0.0)))


def backward_kernel(cfg, me_ref, side_ref, rows_ref, gates_ref, lse_ref, *refs):
    n, cap = cfg.experts, cfg.cap
    even_ref, odd_refs, refs = refs[0], refs[1 : 1 + n // 2], refs[1 + n // 2 :]
    hidden_in, cot_in, heads_in, tokens_in, proj_in, full_in, refs = *refs[:6], refs[6:]
    grad_ref, dense_outs, refs = refs[0], refs[1 : 1 + cfg.dense_outs], refs[1 + cfg.dense_outs :]
    back_all, extra_all, hidden_ref, cot_ref, heads_ref, tokens_ref, proj_ref, full_ref = refs[:8]
    routed_sum, routed_ref, logits_ref, low_ref, heads_grad_ref, bias_ref, qkv_ref = refs[8:15]
    turned_ref, dense_ref, grad_all, in_sems, out_sems = refs[15:]
    count, width = hidden_ref.shape
    extra = extra_all.shape[1]
    me = me_ref[0]
    mine = me // cfg.hidden
    loads, stores = Copies(in_sems), Copies(out_sems)
    back_loads = []
    for k in range(n):
        ref = pick_ref(mine, k, even_ref, odd_refs)
        span = slice(k * cap, (k + 1) * cap)
        back_loads.append(loads.start(ref.at[0:cap], back_all.at[span], False))
        back_loads.append(loads.start(ref.at[cap : cap + extra], extra_all.at[k], False))
    hidden_load = loads.start(hidden_in, hidden_ref, False)
    right = slice(3 * width, full_ref.shape[1])
    left = slice(0, 3 * width)
    right_load = loads.start(full_in.at[:, right], full_ref.at[:, right], False)
    cot_load = loads.start(cot_in, cot_ref, False)
    heads_load = loads.start(heads_in, heads_ref, False)
    proj_load = loads.start(proj_in, proj_ref, False)
    tokens_load = loads.start(tokens_in, tokens_ref, False)
    left_load = loads.start(full_in.at[:, left], full_ref.at[:, left], False)

    def relative(at):
        expert = side_ref[:, 5 + at : 6 + at]
        turned = (expert.astype(jnp.int32) ^ mine).astype(F32)
        return side_ref[:, at : at + 1] + (turned - expert) * cap

    one, two = relative(0), relative(1)
    slot = iota_f((count, n * cap), 1)
    pick = jnp.where((slot == one) | (slot == two), 1.0, 0.0).astype(BF16)
    chunk = 128
    for c in range(count // chunk):
        span = slice(c * chunk, (c + 1) * chunk)
        bias_ref[span, :] = jnp.where(side_ref[span, 4:5] == rows_ref[4:5, :], 0.0, NEG_FILL)
    for copy in back_loads:
        copy.wait()
    routed_sum[...] = mm(pick, back_all[...])
    gate_lanes = round_up(cap, LANES)
    dots_one = jnp.zeros((count, gate_lanes), F32)
    dots_two = jnp.zeros((count, gate_lanes), F32)
    lane_at = iota_f((count, gate_lanes), 1)
    for k in range(n):
        slot = jnp.where(lane_at < cap, lane_at + float(k * cap), -1.0)
        dots = take_split(extra_all.at[k], 0, gate_lanes)
        dots_one = dots_one + jnp.where(slot == one, dots, 0.0)
        dots_two = dots_two + jnp.where(slot == two, dots, 0.0)
    dot_one, dot_two = lane_sum(dots_one), lane_sum(dots_two)
    gate_one, gate_two = gates_ref[:, 0:1], gates_ref[:, 1:2]
    shared = gate_one * dot_one + gate_two * dot_two
    chosen_one = gate_one * (dot_one - shared)
    chosen_two = gate_two * (dot_two - shared)
    hidden_load.wait()
    right_load.wait()
    cot_load.wait()
    gain_one, bias_one, gain_two, bias_two = gain_rows(full_ref, 4 * width, cfg.gate_columns)
    gain_sum = jnp.zeros((1, width), F32)
    bias_sum = jnp.zeros((1, width), F32)
    for c in range(count // chunk):
        span = slice(c * chunk, (c + 1) * chunk)
        column = iota_f((chunk, cfg.gate_lanes), 1)
        logits = jnp.where(column == side_ref[span, 2:3], chosen_one[span], 0.0) + jnp.where(
            column == side_ref[span, 3:4], chosen_two[span], 0.0
        )
        logits = logits.astype(BF16)
        logits_ref[span, :] = logits
        routed_grad = routed_sum[span, :] + contract_last(logits, full_ref[:, 4 * width :])
        unit, inverse = norm_parts(hidden_ref[span, :])
        routed_ref[span, :] = (unit * gain_two + bias_two).astype(BF16)
        gain_sum = gain_sum + row_sum(routed_grad * unit)
        bias_sum = bias_sum + row_sum(routed_grad)
        hidden_grad = cot_ref[span, :].astype(F32) + norm_back(unit, inverse, gain_two, routed_grad)
        routed_sum[span, :] = hidden_grad
        low = hidden_grad.astype(BF16)
        low_ref[span, :] = low
        heads_grad_ref[span, :] = contract_last(low, full_ref[:, 3 * width : 4 * width]).astype(BF16)
    heads_load.wait()
    kind = dense_ref.dtype
    dense_ref[:, 3 * width : 4 * width] = contract_first(heads_ref[...], low_ref[...]).astype(kind)
    dense_ref[:, 4 * width :] = contract_first(routed_ref[...], logits_ref[...]).astype(kind)
    tile = 4 * width + cfg.gate_columns // LANES * LANES
    lane = cfg.gate_columns % LANES
    tile = slice(tile, tile + LANES)
    dense_ref[:, tile] += rows_to_lanes(gain_sum, bias_sum, lane + 2).astype(kind)
    proj_load.wait()
    lane_row = iota((1, LANES), 1)
    scale = HEAD_DIM ** (-0.5)
    block = 256

    def slab(i, carry):
        off = pl.multiple_of(i * LANES, LANES)
        queries = proj_ref[:, pl.ds(off, LANES)] * jnp.asarray(scale, BF16)
        keys = proj_ref[:, pl.ds(width + off, LANES)]
        values = proj_ref[:, pl.ds(2 * width + off, LANES)]
        grads = heads_grad_ref[:, pl.ds(off, LANES)]
        query_grad = [jnp.zeros((block, LANES), F32)] * (count // block)
        key_grad = jnp.zeros((count, LANES), F32)
        value_grad = jnp.zeros((count, LANES), F32)
        for half in (0, 1):
            part = jnp.where(lane_row // HEAD_DIM == half, 1.0, 0.0).astype(BF16)
            query_half, key_half, grads_half = queries * part, keys * part, grads * part
            logs = lse_ref[pl.ds(2 * i + half, 1), :]
            for q in range(count // block):
                span = slice(q * block, (q + 1) * block)
                scores = contract_last(key_half, queries[span]) + bias_ref[:, span] - logs[:, span]
                probs = jnp.exp(scores)
                prob_grad = contract_last(values, grads_half[span])
                score_grad = (probs * (prob_grad - row_sum(probs * prob_grad))).astype(BF16)
                value_grad = value_grad + mm(probs.astype(BF16), grads_half[span])
                key_grad = key_grad + mm(score_grad, query_half[span])
                query_grad[q] = query_grad[q] + contract_first(score_grad, key_half)
        for q in range(count // block):
            qkv_ref[q * block : (q + 1) * block, pl.ds(off, LANES)] = (query_grad[q] * scale).astype(BF16)
        qkv_ref[:, pl.ds(width + off, LANES)] = key_grad.astype(BF16)
        qkv_ref[:, pl.ds(2 * width + off, LANES)] = value_grad.astype(BF16)
        return carry

    lax.fori_loop(0, width // LANES, slab, 0)
    tokens_load.wait()
    left_load.wait()
    gain_sum = jnp.zeros((1, width), F32)
    bias_sum = jnp.zeros((1, width), F32)
    for c in range(count // chunk):
        span = slice(c * chunk, (c + 1) * chunk)
        normed_grad = contract_last(qkv_ref[span, :], full_ref[:, left])
        unit, inverse = norm_parts(tokens_ref[span, :].astype(F32))
        low_ref[span, :] = (unit * gain_one + bias_one).astype(BF16)
        gain_sum = gain_sum + row_sum(normed_grad * unit)
        bias_sum = bias_sum + row_sum(normed_grad)
        grad_all[span, :] = routed_sum[span, :] + norm_back(unit, inverse, gain_one, normed_grad)
        stores.start(grad_all.at[span], grad_ref.at[span])
    turned_ref[...] = jnp.transpose(low_ref[...])
    dense_ref[:, tile] += rows_to_lanes(gain_sum, bias_sum, lane).astype(kind)
    owners = [mask for masks in cfg.owners for mask in masks]
    rows = width // len(owners)
    for c in range(width // chunk):
        span = slice(c * chunk, (c + 1) * chunk)
        dense_ref[span, left] = mm(turned_ref[span, :], qkv_ref[...]).astype(kind)
    if len(dense_outs) == 1:
        stores.start(dense_ref, dense_outs[0])
    else:
        for at, mask in enumerate(owners):
            half = at * 2 // len(owners)
            to = (at - half * len(owners) // 2) * rows
            source = pl.multiple_of((me ^ mask) * rows, rows)
            stores.start(dense_ref.at[pl.ds(source, rows)], dense_outs[half].at[to : to + rows])
    stores.finish()


def output_kernel(cfg, side_ref, hidden_ref, result_ref, out_ref):
    count, width = hidden_ref.shape
    slot = iota_f((count, cfg.experts * cfg.cap), 1)
    pick = (slot == side_ref[:, 0:1]) | (slot == side_ref[:, 1:2])
    mixed = mm(jnp.where(pick, 1.0, 0.0).astype(BF16), result_ref[...])
    out_ref[...] = (hidden_ref[...] + mixed).astype(BF16)


class Config:
    pass


def after(value, other):
    return lax.optimization_barrier((value, other))[0]


def apart(always, part, *args):
    given = jax.eval_shape(part, *args)

    def never(*_):
        return jax.tree.map(lambda s: jnp.zeros(s.shape, s.dtype), given)

    return lax.cond(always, part, never, *args)


def swap_hidden(value, mask):
    size = lax.axis_size("hidden")
    return lax.ppermute(value, "hidden", [(i, i ^ mask) for i in range(size)])


def swap_expert(value, mask):
    size = lax.axis_size("expert")
    return lax.ppermute(value, "expert", [(i, i ^ mask) for i in range(size)])


def gather_rest(own):
    blocks = [own]
    bit = 2
    while bit < lax.axis_size("hidden"):
        blocks += [swap_hidden(block, bit) for block in blocks]
        bit *= 2
    return blocks


def gather_core(half):
    return [swap_hidden(block, 1) for block in half]


def in_turn(first, second):
    return [block for pair in zip(first, second) for block in pair]


def sum_rest(blocks):
    held = {i + 2: [b] for i, b in enumerate(blocks)}
    low = {i: v + [swap_hidden(held[i + 1][0], 1)] for i, v in held.items() if not i & 1}
    held = {0: [], **low}
    bit = 2
    while bit < len(blocks) + 2:
        low = {i: v for i, v in held.items() if not i & bit}
        for i in low:
            value = functools.reduce(jnp.add, held[i ^ bit])
            if 2 * bit == len(blocks) + 2:
                return low[0], value
            low[i] = low[i] + [swap_hidden(value, bit)]
        held = low
        bit *= 2


def body(
    tokens,
    lengths,
    task_ids,
    routes,
    w_qkv,
    w_attn_out,
    w_gate,
    ln1_gain,
    ln1_bias,
    ln2_gain,
    ln2_bias,
    w_in,
    w_out,
    cotangent,
):
    count, width = tokens.shape
    cfg = Config()
    cfg.experts = lax.axis_size("expert")
    cfg.hidden = lax.axis_size("hidden")
    experts, hidden = cfg.experts, cfg.hidden
    cfg.cap = cap = (3 * count * routes.shape[1] + 2 * experts - 1) // (2 * experts)
    cfg.gate_columns = w_gate.shape[1]
    cfg.gate_lanes = round_up(cfg.gate_columns + 4, LANES)
    devices = experts * hidden
    groups = Groups(devices)
    shard_rows = w_qkv.shape[0]
    staged = shard_rows % 16 == 0
    cfg.owners = groups.owners()
    me = (lax.axis_index("expert") * hidden + lax.axis_index("hidden")).astype(jnp.int32)[None]
    extra = 16
    units = w_in.shape[2]
    slots = experts * cap
    wide = 4 * width + cfg.gate_lanes
    one_dot = 2 * count * width * width

    packed = jnp.concatenate(
        [w_qkv, w_attn_out, w_gate]
        + [v[:, None] for v in (ln1_gain, ln1_bias, ln2_gain, ln2_bias)]
        + [jnp.zeros((shard_rows, cfg.gate_lanes - cfg.gate_columns - 4), BF16)],
        axis=1,
    )
    always = lengths[0, 0] > 0

    def first_part(packed, own_in, lengths, task_ids, routes, cotangent):
        far = groups.gather_far(packed) if staged else packed
        in_half = gather_rest(own_in)
        made = call(
            functools.partial(prep_kernel, cfg),
            [
                shape((count, LANES), F32),
                shape((8, count), F32),
                shape((experts // 2, 2, cap, width), BF16),
            ],
            [],
            [lengths, task_ids, routes, cotangent],
            3 * one_dot,
        )
        return far, in_half, made

    dense_far, in_half, (side, rows, sent_cot) = apart(
        always, first_part, packed, w_in[0], lengths, task_ids, routes, cotangent
    )
    if staged:
        dense_blocks = groups.gather_near(dense_far)
        reached = dense_blocks[1 : len(groups.mid)]
    else:
        dense_blocks = [lax.all_gather(packed, BOTH, axis=0, tiled=True)]
        reached = dense_blocks[0]
    cfg.blocks = len(dense_blocks)
    parity = [list(range(i, experts, 2)) for i in (0, 1)]

    def exchange_even(value):
        return lax.all_to_all(
            value, "expert", split_axis=0, concat_axis=0, axis_index_groups=parity, tiled=True
        )

    def exchange_odd(values):
        return [swap_expert(value, 2 * i + 1) for i, value in enumerate(values)]

    cot_even = exchange_even(sent_cot)
    other = 1 - lax.axis_index("expert") % 2
    cot_odd = lax.dynamic_index_in_dim(cot_even, other, 1, keepdims=False)
    out_half = gather_rest(after(w_out[0], reached))

    outs = call(
        functools.partial(forward_kernel, cfg),
        [
            shape((width, wide), BF16),
            shape((count, 3 * width), BF16),
            shape((count, width), BF16),
            shape((HEADS, count), F32),
            shape((count, width), F32),
            shape((count, LANES), F32),
        ]
        + [shape((experts // 2, cap + extra, width), BF16)]
        + [shape((cap + extra, width), BF16)] * (experts // 2),
        [
            pltpu.VMEM((width, wide), BF16),
            pltpu.VMEM((count, 3 * width), BF16),
            pltpu.VMEM((count, width), BF16),
            pltpu.VMEM((HEADS, count), F32),
            pltpu.VMEM((count, width), F32),
            pltpu.VMEM((count, LANES), F32),
            pltpu.VMEM((experts, cap + extra, width), BF16),
            pltpu.VMEM((count, count), F32),
            pltpu.VMEM((count, width), BF16),
            pltpu.VMEM((count, LANES), F32),
            pltpu.SemaphoreType.DMA((devices,)),
            pltpu.SemaphoreType.DMA((6 + experts,)),
        ],
        [me, side, rows, tokens] + dense_blocks,
        12 * one_dot,
        smem=(0,),
        far_in=range(4, 4 + cfg.blocks),
        far_out=range(7 + experts // 2),
    )
    full, proj, heads, lse, hidden_one, gates = outs[:6]
    send_rows = outs[6:]
    def even_part(even_send, odd_send, cot_even, cot_odd, in_half, out_half):
        more_in, more_out = gather_core(in_half), gather_core(out_half)
        blocks = in_turn(in_half, more_in) + in_turn(out_half, more_out)
        even_rows = exchange_even(even_send)
        odd_rows = exchange_odd(odd_send)
        cot_odd = swap_expert(cot_odd, 1)
        out = expert_part(cfg, 0, me, cot_even, [even_rows], blocks, [])
        return even_rows, odd_rows, cot_odd, more_in, more_out, out

    def odd_part(even_send, even_rows, odd_rows, cot_odd, in_blocks, out_blocks, before, even_pairs):
        even_back = exchange_even(even_send)
        blocks = in_blocks + out_blocks
        result, sends, pairs = expert_part(cfg, 1, me, cot_odd, odd_rows, blocks, [before])
        odd_back = exchange_odd(sends)
        picked = [b for b in range(hidden) if b > 1]
        pairs = [even_pairs, pairs]
        grads = weight_part(cfg, picked, me, even_rows, odd_rows, pairs, in_blocks, out_blocks)
        return [even_back] + odd_back, result, pairs[1], grads

    def own_weights(even_rows, odd_rows, pairs, in_blocks, out_blocks):
        return weight_part(cfg, [0, 1], me, even_rows, odd_rows, pairs, in_blocks, out_blocks)

    even_rows, odd_rows, cot_odd, more_in, more_out, even_out = apart(
        always, even_part, send_rows[0], send_rows[1:], cot_even, cot_odd, in_half, out_half
    )
    in_blocks, out_blocks = in_turn(in_half, more_in), in_turn(out_half, more_out)
    back, result, odd_pairs, far_grads = apart(
        always,
        odd_part,
        even_out[1][0],
        even_rows,
        odd_rows,
        cot_odd,
        in_blocks,
        out_blocks,
        even_out[0],
        even_out[2],
    )
    pairs = [even_out[2], odd_pairs]
    held, value = sum_rest(far_grads)
    back = after(back, value)
    returned = lax.all_to_all(
        after(result, back), "expert", split_axis=0, concat_axis=0, tiled=True
    )
    if staged:
        dense_shapes = [shape((width // 2, wide), BF16)] * 2
    else:
        dense_shapes = [shape((width, wide), F32)]
    cfg.dense_outs = len(dense_shapes)

    def back_part(value, back):
        args = [me, side, rows, gates, lse] + back + [hidden_one, cotangent, heads, tokens, proj, full]
        outs = call(
            functools.partial(backward_kernel, cfg),
            [shape((count, width), F32)] + dense_shapes,
            [
                pltpu.VMEM((slots, width), BF16),
                pltpu.VMEM((experts, extra, width), BF16),
                pltpu.VMEM((count, width), F32),
                pltpu.VMEM((count, width), BF16),
                pltpu.VMEM((count, width), BF16),
                pltpu.VMEM((count, width), BF16),
                pltpu.VMEM((count, 3 * width), BF16),
                pltpu.VMEM((width, wide), BF16),
                pltpu.VMEM((count, width), F32),
                pltpu.VMEM((count, width), BF16),
                pltpu.VMEM((count, cfg.gate_lanes), BF16),
                pltpu.VMEM((count, width), BF16),
                pltpu.VMEM((count, width), BF16),
                pltpu.VMEM((count, count), F32),
                pltpu.VMEM((count, 3 * width), BF16),
                pltpu.VMEM((width, count), BF16),
                pltpu.VMEM((width, wide), dense_shapes[0].dtype),
                pltpu.VMEM((count, width), F32),
                pltpu.SemaphoreType.DMA((2 * experts + 7,)),
                pltpu.SemaphoreType.DMA((4 + devices,)),
            ],
            args,
            19 * one_dot,
            smem=(0,),
            far_in=range(5, len(args)),
            far_out=range(1 + len(dense_shapes)),
        )
        return swap_hidden(value, hidden // 2), outs

    last, outs = apart(always, back_part, value, back)
    reached = held + [last]
    grad_tokens = outs[0]

    def last_weights(blocks):
        got = [groups.swap(b, m) for b, m in zip(blocks[1:], groups.mid[1:])]
        return got, own_weights(even_rows, odd_rows, pairs, in_blocks, out_blocks)

    def last_sums(blocks, own, more, reached, returned):
        layer_out = call(
            functools.partial(output_kernel, cfg),
            shape((count, width), BF16),
            [],
            [side, hidden_one, returned.reshape(slots, width)],
            6 * one_dot,
        )
        got = [groups.swap(b, m) for b, m in zip(blocks[1:], groups.far[1:])]
        terms = [own, swap_hidden(more, 1)] + reached
        grad_in, grad_out = call(
            turn_add_kernel,
            [shape((width, units), F32), shape((units, width), F32)],
            [],
            terms,
            4 * width * units,
            limit=2 * SMALL_LIMIT,
        )
        return got, grad_in, grad_out, layer_out

    blocks = [None]
    if staged:
        blocks = add_parts(outs[1], [groups.swap(outs[2], 1)], len(groups.mid))
    got, (own, more) = apart(always, last_weights, blocks)
    if staged:
        blocks = add_parts(blocks[0], got, len(groups.far))
    got, grad_in, grad_out, layer_out = apart(
        always, last_sums, blocks, own, more, reached, returned
    )
    if staged:
        dense_terms = blocks[:1] + got
    else:
        dense_terms = [lax.psum_scatter(outs[1], BOTH, scatter_dimension=0, tiled=True)]
    dense_outs = call(
        functools.partial(split_kernel, cfg),
        [shape((shard_rows, c), F32) for c in (3 * width, width, cfg.gate_columns)]
        + [shape((1, shard_rows), F32)] * 4,
        [],
        dense_terms,
        shard_rows * wide,
        limit=SMALL_LIMIT,
    )

    return (
        layer_out,
        grad_tokens,
        *dense_outs[:3],
        *[v.reshape(shard_rows) for v in dense_outs[3:]],
        grad_in[None],
        grad_out[None],
    )


def solution(mesh):
    split = P(BOTH, None)
    vector = P(BOTH)
    placed = (split,) * 7 + (vector,) * 4 + (P("expert", None, "hidden"), P("expert", "hidden", None), split)
    return jax.shard_map(
        body,
        mesh=mesh,
        in_specs=placed,
        out_specs=(split,) * 5
        + (vector,) * 4
        + (P("expert", None, "hidden"), P("expert", "hidden", None)),
        check_vma=False,
    )
```

```python
import functools

import jax
import jax.numpy as jnp
from jax import lax
from jax.experimental import pallas as pl
from jax.experimental.pallas import tpu as pltpu
from jax.sharding import PartitionSpec as P

HEADS = 8
HEAD_DIM = 64
EPS = 1e-05
NEG_FILL = -1e30
LANES = 128
BOTH = ("expert", "hidden")
F32 = jnp.float32
BF16 = jnp.bfloat16
VMEM_LIMIT = 56 * 1024 * 1024
SMALL_LIMIT = 8 * 1024 * 1024


def mm(left, right):
    return jnp.dot(left, right, preferred_element_type=F32)


def contract_last(left, right):
    return lax.dot_general(left, right, (((1,), (1,)), ((), ())), preferred_element_type=F32)


def contract_first(left, right):
    return lax.dot_general(left, right, (((0,), (0,)), ((), ())), preferred_element_type=F32)


def iota(shape, axis):
    return lax.broadcasted_iota(jnp.int32, shape, axis)


def iota_f(shape, axis):
    return iota(shape, axis).astype(F32)


def lane_sum(values):
    return jnp.sum(values, axis=1, keepdims=True)


def row_sum(values):
    return jnp.sum(values, axis=0, keepdims=True)


def norm_parts(values):
    middle = jnp.mean(values, axis=-1, keepdims=True)
    centred = values - middle
    spread = jnp.mean(centred * centred, axis=-1, keepdims=True)
    inverse = lax.rsqrt(spread + EPS)
    return centred * inverse, inverse


def norm_back(unit, inverse, gain, grad):
    scaled = grad * gain
    mean_one = jnp.mean(scaled, axis=-1, keepdims=True)
    mean_two = jnp.mean(scaled * unit, axis=-1, keepdims=True)
    return inverse * (scaled - mean_one - unit * mean_two)


def round_up(value, step):
    return (value + step - 1) // step * step


def call(kernel, outs, scratch, args, flops, smem=(), far_in=(), far_out=(), limit=VMEM_LIMIT):
    def spec(at):
        space = pltpu.SMEM if at in smem else pl.ANY if at in far_in else pltpu.VMEM
        return pl.BlockSpec(memory_space=space)

    def out_spec(at):
        return pl.BlockSpec(memory_space=pl.ANY if at in far_out else pltpu.VMEM)

    touched = sum(a.size * a.dtype.itemsize for a in args) + sum(
        o.size * o.dtype.itemsize for o in jax.tree.leaves(outs)
    )
    got = pl.pallas_call(
        kernel,
        out_shape=outs,
        in_specs=[spec(at) for at in range(len(args))],
        out_specs=[out_spec(at) for at in range(len(outs))] if isinstance(outs, list) else out_spec(0),
        scratch_shapes=scratch,
        compiler_params=pltpu.CompilerParams(vmem_limit_bytes=limit),
        cost_estimate=pl.CostEstimate(flops=1, bytes_accessed=1, transcendentals=0),
    )(*args)
    return list(got) if isinstance(outs, list) else got


def shape(dims, dtype):
    return jax.ShapeDtypeStruct(dims, dtype)


def slot_targets(cfg, routes_ref):
    count, experts = routes_ref.shape[1], cfg.experts
    both = jnp.zeros((8, count), F32)
    for at in (0, 1):
        both = jnp.where(iota((8, count), 0) == at, routes_ref[at : at + 1, :].astype(F32), both)
    routes = jnp.transpose(both)
    first, second = routes[:, 0:1], routes[:, 1:2]
    lane_e = iota_f((count, experts), 1)
    hot_one = jnp.where(lane_e == first, 1.0, 0.0)
    hot_two = jnp.where(lane_e == second, 1.0, 0.0)
    before = jnp.where(iota((count, count), 1) < iota((count, count), 0), 1.0, 0.0).astype(BF16)
    earlier = mm(before, (hot_one + hot_two).astype(BF16))
    target_one = first * cfg.cap + lane_sum(earlier * hot_one)
    target_two = second * cfg.cap + lane_sum(earlier * hot_two)
    return first, second, target_one, target_two


def prep_kernel(cfg, lens_ref, tasks_ref, routes_ref, cot_ref, side_ref, rows_ref, sent_ref):
    experts, cap = cfg.experts, cfg.cap
    count = routes_ref.shape[1]
    sents = lens_ref.shape[1]
    lens = lens_ref[...].astype(F32)
    tasks = tasks_ref[...].astype(F32)
    down, across = iota((sents, sents), 0), iota((sents, sents), 1)
    ends_col = lane_sum(jnp.where(across <= down, lens, 0.0))
    ends_row = row_sum(jnp.where(across == down, ends_col, 0.0))
    passed = jnp.where(iota_f((count, sents), 0) >= ends_row, 1.0, 0.0)
    sentence = lane_sum(passed)
    task = lane_sum(jnp.where(iota_f((count, sents), 1) == sentence, tasks, 0.0))
    lane = iota((count, LANES), 1)
    first, second, target_one, target_two = slot_targets(cfg, routes_ref)
    side = jnp.where(lane == 0, target_one, 0.0)
    side = jnp.where(lane == 1, target_two, side)
    side = jnp.where(lane == 2, task * experts + first, side)
    side = jnp.where(lane == 3, task * experts + second, side)
    side = jnp.where(lane == 4, sentence, side)
    side = jnp.where(lane == 5, first, side)
    side = jnp.where(lane == 6, second, side)
    side_ref[...] = side
    turned = jnp.transpose(side)
    rows_ref[...] = turned[0:8, :]
    one_row, two_row = turned[0:1, :], turned[1:2, :]
    cot = cot_ref[...]
    for e in range(experts):
        at = iota_f((cap, count), 0) + float(e * cap)
        pick = jnp.where((at == one_row) | (at == two_row), 1.0, 0.0).astype(BF16)
        sent_ref[e // 2, e % 2] = mm(pick, cot).astype(BF16)


def pack_kernel(qkv_ref, attn_ref, gate_ref, vectors_ref, out_ref):
    rows = out_ref.shape[0]
    at = 0
    for ref in (qkv_ref, attn_ref):
        out_ref[:, at : at + ref.shape[1]] = ref[...]
        at += ref.shape[1]
    columns = gate_ref.shape[1]
    lanes = out_ref.shape[1] - at
    tile = columns // LANES * LANES
    out_ref[:, at : at + columns] = gate_ref[...]
    eye = iota((rows, rows), 0) == iota((rows, rows), 1)
    vectors = vectors_ref[...].astype(F32)
    lane = iota((rows, lanes - tile), 1)
    last = out_ref[:, at + tile :].astype(F32)
    last = jnp.where(lane < columns - tile, last, 0.0)
    for i in range(4):
        column = lane_sum(jnp.where(eye, vectors[i : i + 1, :], 0.0))
        last = jnp.where(lane == columns - tile + i, column, last)
    out_ref[:, at + tile :] = last.astype(BF16)


class Groups:
    def __init__(self, devices):
        bits = devices.bit_length() - 1
        mid = (bits - 1) // 2
        self.near = [1]
        self.mid = self.masks(1, mid)
        self.far = self.masks(1 + mid, bits - 1 - mid)
        self.devices = devices

    @staticmethod
    def masks(low, width):
        return [m << low for m in range(1 << width)]

    def owners(self):
        return [[n | b | c for c in self.far] for n in (0, 1) for b in self.mid]

    def swap(self, value, mask):
        return lax.ppermute(value, BOTH, [(i, i ^ mask) for i in range(self.devices)])

    def gather_far(self, shard):
        return jnp.concatenate([shard] + [self.swap(shard, m) for m in self.far[1:]], axis=0)

    def gather_near(self, far):
        mid = [far] + [self.swap(far, m) for m in self.mid[1:]]
        return mid + [self.swap(block, 1) for block in mid]


def add_kernel(parts, keep_ref, *refs):
    got, outs = refs[: len(refs) - parts], refs[len(refs) - parts :]
    rows = outs[0].shape[0]
    for i, out_ref in enumerate(outs):
        span = slice(i * rows, (i + 1) * rows)
        total = keep_ref[span, :].astype(F32)
        for ref in got:
            total = total + ref[span, :].astype(F32)
        out_ref[...] = total.astype(out_ref.dtype)


def add_parts(keep, got, parts):
    rows, columns = keep.shape
    outs = [shape((rows // parts, columns), F32 if i == 0 else BF16) for i in range(parts)]
    return call(
        functools.partial(add_kernel, parts), outs, [], [keep] + got, rows * columns * len(got), limit=SMALL_LIMIT
    )


def split_kernel(cfg, *refs):
    terms, outs = refs[:-7], refs[-7:]
    rows, width = outs[0].shape[0], outs[1].shape[1]

    def total(start, stop):
        value = terms[0][:, start:stop]
        for ref in terms[1:]:
            value = value + ref[:, start:stop].astype(F32)
        return value

    outs[0][...] = total(0, 3 * width)
    outs[1][...] = total(3 * width, 4 * width)
    outs[2][...] = total(4 * width, 4 * width + cfg.gate_columns)
    tile = 4 * width + cfg.gate_columns // LANES * LANES
    lane = cfg.gate_columns % LANES
    turned = jnp.transpose(total(tile, tile + LANES))
    for i in range(4):
        outs[3 + i][...] = turned[lane + i : lane + i + 1, :]


def gain_rows(full_ref, start, gate_columns):
    tile = start + gate_columns // LANES * LANES
    lane = gate_columns % LANES
    turned = jnp.transpose(full_ref[:, tile : tile + LANES].astype(F32))
    return [turned[lane + i : lane + i + 1, :] for i in range(4)]


def forward_kernel(cfg, me_ref, side_ref, rows_ref, tokens_ref, *refs):
    n, cap = cfg.experts, cfg.cap
    blocks, refs = refs[: cfg.blocks], refs[cfg.blocks :]
    outs, refs = refs[:6], refs[6:]
    even_out, odd_outs, refs = refs[0], refs[1 : 1 + n // 2], refs[1 + n // 2 :]
    full_ref, proj_ref, heads_ref, turned_ref, hidden_ref, gates_ref, send_all = refs[:7]
    bias_ref, routed_ref, lse_ref, in_sems, out_sems = refs[7:]
    count, width = tokens_ref.shape
    me = me_ref[0]
    mine = me // cfg.hidden
    loads, stores = Copies(in_sems), Copies(out_sems)
    if len(blocks) == 1:
        loads.start(blocks[0], full_ref)
    else:
        for block_ref, masks in zip(blocks, cfg.owners):
            rows = block_ref.shape[0] // len(masks)
            for i, mask in enumerate(masks):
                at = pl.multiple_of((me ^ mask) * rows, rows)
                loads.start(block_ref.at[i * rows : (i + 1) * rows], full_ref.at[pl.ds(at, rows)])
    chunk = 128
    for c in range(count // chunk):
        span = slice(c * chunk, (c + 1) * chunk)
        bias_ref[span, :] = jnp.where(side_ref[span, 4:5] == rows_ref[4:5, :], 0.0, NEG_FILL)
    loads.finish()
    stores.start(full_ref, outs[0])
    gain_one, bias_one, gain_two, bias_two = gain_rows(full_ref, 4 * width, cfg.gate_columns)
    for c in range(count // chunk):
        span = slice(c * chunk, (c + 1) * chunk)
        unit, _ = norm_parts(tokens_ref[span, :].astype(F32))
        routed_ref[span, :] = (unit * gain_one + bias_one).astype(BF16)
    proj_ref[...] = mm(routed_ref[...], full_ref[:, : 3 * width]).astype(BF16)
    stores.start(proj_ref, outs[1])
    lse_ref[...] = jnp.zeros_like(lse_ref)
    lane = iota((1, LANES), 1)
    scale = HEAD_DIM ** (-0.5)
    block = 256

    def slab(i, carry):
        off = pl.multiple_of(i * LANES, LANES)
        keys = proj_ref[:, pl.ds(width + off, LANES)]
        values = proj_ref[:, pl.ds(2 * width + off, LANES)]
        halves = []
        for half in (0, 1):
            mine = jnp.where(lane // HEAD_DIM == half, 1.0, 0.0).astype(BF16)
            halves.append((keys * mine, values * mine))
        for r in range(count // block):
            span = slice(r * block, (r + 1) * block)
            queries = proj_ref[span, pl.ds(off, LANES)]
            total = jnp.zeros((block, LANES), F32)
            logs = lse_ref[span, :]
            for half, (key_half, value_half) in enumerate(halves):
                scores = contract_last(queries, key_half) * scale + bias_ref[span, :]
                highest = jnp.max(scores, axis=1, keepdims=True)
                expo = jnp.exp(scores - highest)
                sums = lane_sum(expo)
                probs = (expo * (1.0 / sums)).astype(BF16)
                total = total + mm(probs, value_half)
                logs = jnp.where(lane == 2 * i + half, highest + jnp.log(sums), logs)
            heads_ref[span, pl.ds(off, LANES)] = total.astype(BF16)
            lse_ref[span, :] = logs
        return carry

    lax.fori_loop(0, width // LANES, slab, 0)
    stores.start(heads_ref, outs[2])
    turned_ref[...] = jnp.transpose(lse_ref[...])[:HEADS, :]
    stores.start(turned_ref, outs[3])
    for c in range(count // chunk):
        span = slice(c * chunk, (c + 1) * chunk)
        attended = mm(heads_ref[span, :], full_ref[:, 3 * width : 4 * width])
        hidden = tokens_ref[span, :].astype(F32) + attended
        hidden_ref[span, :] = hidden
        unit, _ = norm_parts(hidden)
        routed = (unit * gain_two + bias_two).astype(BF16)
        routed_ref[span, :] = routed
        logits = mm(routed, full_ref[:, 4 * width :])
        column = iota_f(logits.shape, 1)
        one = lane_sum(jnp.where(column == side_ref[span, 2:3], logits, 0.0))
        two = lane_sum(jnp.where(column == side_ref[span, 3:4], logits, 0.0))
        top = jnp.maximum(one, two)
        expo_one, expo_two = jnp.exp(one - top), jnp.exp(two - top)
        both = expo_one + expo_two
        gates_ref[span, :] = jnp.where(
            lane == 0, expo_one / both, jnp.where(lane == 1, expo_two / both, 0.0)
        )
    stores.start(hidden_ref, outs[4])
    stores.start(gates_ref, outs[5])
    routed = routed_ref[...]
    gate_lanes = round_up(cap, LANES)
    for k in range(n):
        base = ((mine ^ k) * cap).astype(F32)
        at = iota_f((cap, count), 0) + base
        pick = (at == rows_ref[0:1, :]) | (at == rows_ref[1:2, :])
        send_all[k, 0:cap, :] = mm(jnp.where(pick, 1.0, 0.0).astype(BF16), routed).astype(BF16)
        slot = iota_f((count, gate_lanes), 1) + base
        row = row_sum(
            jnp.where(slot == side_ref[:, 0:1], gates_ref[:, 0:1], 0.0)
            + jnp.where(slot == side_ref[:, 1:2], gates_ref[:, 1:2], 0.0)
        )
        put_split(send_all.at[k], cap, row)
        stores.start(send_all.at[k], pick_ref(mine, k, even_out, odd_outs))
    stores.finish()


def pick_ref(mine, k, even_ref, odd_refs):
    return odd_refs[k // 2] if k % 2 else even_ref.at[(mine ^ k) // 2]


def put_split(ref, cap, row):
    extra = ref.shape[0] - cap
    high = row.astype(BF16).astype(F32)
    down = iota((extra, row.shape[1]), 0)
    both = jnp.where(down == 0, high, jnp.where(down == 1, row - high, 0.0))
    ref[cap:, :] = jnp.zeros((extra, ref.shape[1]), BF16)
    ref[cap:, 0 : row.shape[1]] = both.astype(BF16)


def take_split(ref, cap, lanes):
    both = ref[cap:, 0:lanes].astype(F32)
    return both[0:1, :] + both[1:2, :]


def gelu_parts(pre):
    root = 0.7978845608028654
    cubic = 0.044715
    square = pre * pre
    upper = 0.5 + 0.5 * jnp.tanh(pre * (root + (root * cubic) * square))
    act = pre * upper
    return act, upper + act * (1.0 - upper) * (2.0 * root + (6.0 * root * cubic) * square)


class Copies:
    def __init__(self, sems):
        self.sems, self.count, self.open = sems, 0, []

    def start(self, source, target, kept=True):
        copy = pltpu.make_async_copy(source, target, self.sems.at[self.count])
        self.count += 1
        copy.start()
        if kept:
            self.open.append(copy)
        return copy

    def finish(self):
        for copy in self.open:
            copy.wait()


def expert_kernel(cfg, odd, me_ref, *refs):
    h, cap, n = cfg.hidden, cfg.cap, cfg.experts // 2
    many = n if odd else 1
    cot_ref, refs = refs[0], refs[1:]
    row_refs, refs = refs[:many], refs[many:]
    in_refs, out_refs, refs = refs[:h], refs[h : 2 * h], refs[2 * h :]
    if odd:
        before_ref, refs = refs[0], refs[1:]
    result_ref, back_refs, refs = refs[0], refs[1 : 1 + many], refs[1 + many :]
    pairs_ref, refs = refs[0], refs[1:]
    rows_all, cot_all, pairs_all, result_all, back_all, before_all, extra_in, extra_out = refs[:8]
    result_sum, back_sum, weights_all, in_sems, out_sems = refs[8:]
    total, width = rows_all.shape
    extra = extra_in.shape[1]
    mine = me_ref[0] // h
    loads, stores = Copies(in_sems), Copies(out_sems)
    ks = list(range(odd, 2 * n, 2))
    tiles = 2
    per = n // tiles
    tile = per * cap
    row_loads, weight_loads = [], []

    def load_rows(m):
        for i in range(m * per, (m + 1) * per):
            span = slice(i * cap, (i + 1) * cap)
            source = (mine ^ ks[i]) // 2
            row_ref = pick_ref(mine, ks[i], row_refs[0], row_refs)
            from_ref = cot_ref.at[source] if odd else cot_ref.at[source, mine % 2]
            row_loads.append(
                (
                    loads.start(row_ref.at[0:cap], rows_all.at[span], False),
                    loads.start(row_ref.at[cap : cap + extra], extra_in.at[i], False),
                    loads.start(from_ref, cot_all.at[span], False),
                )
            )

    load_rows(0)
    for i, ref in enumerate(in_turn(in_refs, out_refs)):
        held = weights_all.at[i, : ref.shape[0], : ref.shape[1]]
        weight_loads.append(loads.start(ref, held, False))
    for m in range(1, tiles):
        load_rows(m)
    if odd:
        before_loads = [loads.start(before_ref.at[i], before_all.at[i], False) for i in range(n)]
    gate_lanes = round_up(cap, LANES)
    eye = iota((cap, gate_lanes), 0) == iota((cap, gate_lanes), 1)
    units = in_refs[0].shape[1]
    gates = {}
    for m in range(tiles):
        span = slice(m * tile, (m + 1) * tile)
        for i in range(m * per, (m + 1) * per):
            for copy in row_loads[i]:
                copy.wait()
            rows = slice(i * cap, (i + 1) * cap)
            gates[i] = lane_sum(jnp.where(eye, take_split(extra_in.at[i], 0, gate_lanes), 0.0))
            pairs_all[rows, :] = (gates[i] * cot_all[rows, :].astype(F32)).astype(BF16)
        stores.start(pairs_all.at[span], pairs_ref.at[span])
        for b in range(h):
            if m == 0:
                weight_loads[2 * b].wait()
                weight_loads[2 * b + 1].wait()
            w_in, w_out = weights_all.at[2 * b, :, :units], weights_all.at[2 * b + 1, :units, :]
            act, slope = gelu_parts(mm(rows_all[span, :], w_in[...]))
            act_low = act.astype(BF16)
            act_grad = contract_last(pairs_all[span, :], w_out[...])
            pre_grad = (act_grad * slope).astype(BF16)
            result = mm(act_low, w_out[...])
            back = contract_last(pre_grad, w_in[...])
            if b == 0:
                result_sum[...] = result
                back_sum[...] = back
            elif b < h - 1:
                result_sum[...] += result
                back_sum[...] += back
            else:
                result_sum[...] += result
                back_all[span, :] = (back_sum[...] + back).astype(BF16)
        if odd and m == 0:
            for i in range(n):
                before_loads[i].wait()
                stores.start(before_all.at[i], result_ref.at[mine ^ (2 * i)])
        for i in range(m * per, (m + 1) * per):
            rows, k = slice(i * cap, (i + 1) * cap), ks[i]
            back_ref = pick_ref(mine, k, back_refs[0], back_refs)
            stores.start(back_all.at[rows], back_ref.at[0:cap])
            result = result_sum[(i - m * per) * cap : (i - m * per + 1) * cap, :]
            result_all[rows, :] = (gates[i] * result).astype(BF16)
            stores.start(result_all.at[rows], result_ref.at[mine ^ k if odd else i])
            dots = lane_sum(cot_all[rows, :].astype(F32) * result)
            put_split(extra_out.at[i], 0, row_sum(jnp.where(eye, dots, 0.0)))
            stores.start(extra_out.at[i], back_ref.at[cap : cap + extra])
    stores.finish()


def expert_part(cfg, odd, me, cot, rows, weights, before):
    n, h, cap, extra = cfg.experts // 2, cfg.hidden, cfg.cap, 16
    width, units = cot.shape[-1], weights[0].shape[1]
    slots = n * cap
    many = len(rows)
    side = max(width, units)
    args = [me, cot] + rows + weights + before
    outs = (
        [shape((2 * n if odd else n, cap, width), BF16)]
        + [shape(r.shape, BF16) for r in rows]
        + [shape((slots, width), BF16)]
    )
    outs = call(
        functools.partial(expert_kernel, cfg, odd),
        outs,
        [pltpu.VMEM((slots, width), BF16)] * 5
        + [pltpu.VMEM((n, cap, width), BF16)]
        + [pltpu.VMEM((n, extra, width), BF16)] * 2
        + [pltpu.VMEM((slots // 2, width), F32)] * 2
        + [pltpu.VMEM((2 * h, side, side), BF16)]
        + [pltpu.SemaphoreType.DMA((4 * n + 2 * h,)), pltpu.SemaphoreType.DMA((4 * n + 2,))],
        args,
        8 * slots * width * units * h,
        smem=(0,),
        far_in=range(1, len(args)),
        far_out=range(len(outs)),
    )
    return outs[0], outs[1 : 1 + many], outs[1 + many]


def weight_kernel(cfg, parts, me_ref, *refs):
    n, cap = cfg.experts, cfg.cap
    even_ref, odd_refs, refs = refs[0], refs[1 : 1 + n // 2], refs[1 + n // 2 :]
    pair_refs, in_refs, out_refs, refs = refs[:2], refs[2 : 2 + parts], refs[2 + parts : 2 + 2 * parts], refs[2 + 2 * parts :]
    grad_refs, refs = refs[:parts], refs[parts:]
    grads_all, refs = refs[:parts], refs[parts:]
    rows_all, pairs_all, rows_turned, pairs_turned, act_all, pre_all, weights_all, in_sems, out_sems = refs
    total, width = rows_all.shape
    half = total // 2
    units = act_all.shape[1]
    mine = me_ref[0] // cfg.hidden
    loads, stores = Copies(in_sems), Copies(out_sems)
    waits = {0: [], 1: []}
    weight_loads = []
    for odd in (0, 1):
        for i in range(n // 2):
            k = 2 * i + odd
            span = slice(odd * half + i * cap, odd * half + (i + 1) * cap)
            row_ref = pick_ref(mine, k, even_ref, odd_refs)
            waits[odd].append(loads.start(row_ref.at[0:cap], rows_all.at[span], False))
        span = slice(odd * half, (odd + 1) * half)
        waits[odd].append(loads.start(pair_refs[odd], pairs_all.at[span], False))
        if not odd:
            for i, ref in enumerate(in_turn(in_refs, out_refs)):
                held = weights_all.at[i, : ref.shape[0], : ref.shape[1]]
                weight_loads.append(loads.start(ref, held, False))
    tile = half // 2
    for p in range(parts):
        weight_loads[2 * p].wait()
        weight_loads[2 * p + 1].wait()
        w_in, w_out = weights_all.at[2 * p, :, :units], weights_all.at[2 * p + 1, :units, :]
        for m in range(4):
            if p == 0 and m % 2 == 0:
                for copy in waits[m // 2]:
                    copy.wait()
                span = slice(m // 2 * half, (m // 2 + 1) * half)
                rows_turned[:, span] = jnp.transpose(rows_all[span, :])
                pairs_turned[:, span] = jnp.transpose(pairs_all[span, :])
            span = slice(m * tile, (m + 1) * tile)
            act, slope = gelu_parts(mm(rows_all[span, :], w_in[...]))
            act_all[span, :] = act.astype(BF16)
            act_grad = contract_last(pairs_all[span, :], w_out[...])
            pre_all[span, :] = (act_grad * slope).astype(BF16)
        kept = grads_all[p]
        kept[:width, :] = mm(rows_turned[...], pre_all[...]).astype(kept.dtype)
        kept[width:, :] = mm(pairs_turned[...], act_all[...]).astype(kept.dtype)
        stores.start(kept, grad_refs[p])
    stores.finish()


def weight_part(cfg, picked, me, even_rows, odd_rows, pairs, ins, outs):
    width, units = ins[0].shape
    slots, parts = cfg.experts * cfg.cap, len(picked)
    args = [me, even_rows] + odd_rows + pairs + [ins[b] for b in picked] + [outs[b] for b in picked]
    kinds = [BF16 if b else F32 for b in picked]
    side = max(width, units)
    return call(
        functools.partial(weight_kernel, cfg, parts),
        [shape((2 * width, units), kind) for kind in kinds],
        [pltpu.VMEM((2 * width, units), kind) for kind in kinds]
        + [pltpu.VMEM((slots, width), BF16)] * 2
        + [pltpu.VMEM((width, slots), BF16)] * 2
        + [pltpu.VMEM((slots, units), BF16)] * 2
        + [pltpu.VMEM((2 * parts, side, side), BF16)]
        + [pltpu.SemaphoreType.DMA((cfg.experts + 2 + 2 * parts,)), pltpu.SemaphoreType.DMA((parts,))],
        args,
        8 * slots * width * units * parts,
        smem=(0,),
        far_in=range(1, len(args)),
        far_out=range(parts),
    )


def turn_add_kernel(*refs):
    terms, (sum_in, sum_out) = refs[:-2], refs[-2:]
    width = sum_in.shape[0]
    total = terms[0][...]
    for ref in terms[1:]:
        total = total + ref[...].astype(F32)
    sum_in[...] = total[:width, :]
    sum_out[...] = jnp.transpose(total[width:, :])


def rows_to_lanes(first, second, lane):
    down = iota((LANES, first.shape[1]), 0)
    return jnp.transpose(jnp.where(down == lane, first, jnp.where(down == lane + 1, second, 0.0)))


def backward_kernel(cfg, me_ref, side_ref, rows_ref, gates_ref, lse_ref, *refs):
    n, cap = cfg.experts, cfg.cap
    even_ref, odd_refs, refs = refs[0], refs[1 : 1 + n // 2], refs[1 + n // 2 :]
    hidden_in, cot_in, heads_in, tokens_in, proj_in, full_in, refs = *refs[:6], refs[6:]
    grad_ref, dense_outs, refs = refs[0], refs[1 : 1 + cfg.dense_outs], refs[1 + cfg.dense_outs :]
    back_all, extra_all, hidden_ref, cot_ref, heads_ref, tokens_ref, proj_ref, full_ref = refs[:8]
    routed_sum, routed_ref, logits_ref, low_ref, heads_grad_ref, bias_ref, qkv_ref = refs[8:15]
    turned_ref, dense_ref, grad_all, in_sems, out_sems = refs[15:]
    count, width = hidden_ref.shape
    extra = extra_all.shape[1]
    me = me_ref[0]
    mine = me // cfg.hidden
    loads, stores = Copies(in_sems), Copies(out_sems)
    back_loads = []
    for k in range(n):
        ref = pick_ref(mine, k, even_ref, odd_refs)
        span = slice(k * cap, (k + 1) * cap)
        back_loads.append(loads.start(ref.at[0:cap], back_all.at[span], False))
        back_loads.append(loads.start(ref.at[cap : cap + extra], extra_all.at[k], False))
    hidden_load = loads.start(hidden_in, hidden_ref, False)
    right = slice(3 * width, full_ref.shape[1])
    left = slice(0, 3 * width)
    right_load = loads.start(full_in.at[:, right], full_ref.at[:, right], False)
    cot_load = loads.start(cot_in, cot_ref, False)
    heads_load = loads.start(heads_in, heads_ref, False)
    proj_load = loads.start(proj_in, proj_ref, False)
    tokens_load = loads.start(tokens_in, tokens_ref, False)
    left_load = loads.start(full_in.at[:, left], full_ref.at[:, left], False)

    def relative(at):
        expert = side_ref[:, 5 + at : 6 + at]
        turned = (expert.astype(jnp.int32) ^ mine).astype(F32)
        return side_ref[:, at : at + 1] + (turned - expert) * cap

    one, two = relative(0), relative(1)
    slot = iota_f((count, n * cap), 1)
    pick = jnp.where((slot == one) | (slot == two), 1.0, 0.0).astype(BF16)
    chunk = 128
    for c in range(count // chunk):
        span = slice(c * chunk, (c + 1) * chunk)
        bias_ref[span, :] = jnp.where(side_ref[span, 4:5] == rows_ref[4:5, :], 0.0, NEG_FILL)
    for copy in back_loads:
        copy.wait()
    routed_sum[...] = mm(pick, back_all[...])
    gate_lanes = round_up(cap, LANES)
    dots_one = jnp.zeros((count, gate_lanes), F32)
    dots_two = jnp.zeros((count, gate_lanes), F32)
    lane_at = iota_f((count, gate_lanes), 1)
    for k in range(n):
        slot = jnp.where(lane_at < cap, lane_at + float(k * cap), -1.0)
        dots = take_split(extra_all.at[k], 0, gate_lanes)
        dots_one = dots_one + jnp.where(slot == one, dots, 0.0)
        dots_two = dots_two + jnp.where(slot == two, dots, 0.0)
    dot_one, dot_two = lane_sum(dots_one), lane_sum(dots_two)
    gate_one, gate_two = gates_ref[:, 0:1], gates_ref[:, 1:2]
    shared = gate_one * dot_one + gate_two * dot_two
    chosen_one = gate_one * (dot_one - shared)
    chosen_two = gate_two * (dot_two - shared)
    hidden_load.wait()
    right_load.wait()
    cot_load.wait()
    gain_one, bias_one, gain_two, bias_two = gain_rows(full_ref, 4 * width, cfg.gate_columns)
    gain_sum = jnp.zeros((1, width), F32)
    bias_sum = jnp.zeros((1, width), F32)
    for c in range(count // chunk):
        span = slice(c * chunk, (c + 1) * chunk)
        column = iota_f((chunk, cfg.gate_lanes), 1)
        logits = jnp.where(column == side_ref[span, 2:3], chosen_one[span], 0.0) + jnp.where(
            column == side_ref[span, 3:4], chosen_two[span], 0.0
        )
        logits = logits.astype(BF16)
        logits_ref[span, :] = logits
        routed_grad = routed_sum[span, :] + contract_last(logits, full_ref[:, 4 * width :])
        unit, inverse = norm_parts(hidden_ref[span, :])
        routed_ref[span, :] = (unit * gain_two + bias_two).astype(BF16)
        gain_sum = gain_sum + row_sum(routed_grad * unit)
        bias_sum = bias_sum + row_sum(routed_grad)
        hidden_grad = cot_ref[span, :].astype(F32) + norm_back(unit, inverse, gain_two, routed_grad)
        routed_sum[span, :] = hidden_grad
        low = hidden_grad.astype(BF16)
        low_ref[span, :] = low
        heads_grad_ref[span, :] = contract_last(low, full_ref[:, 3 * width : 4 * width]).astype(BF16)
    heads_load.wait()
    kind = dense_ref.dtype
    dense_ref[:, 3 * width : 4 * width] = contract_first(heads_ref[...], low_ref[...]).astype(kind)
    dense_ref[:, 4 * width :] = contract_first(routed_ref[...], logits_ref[...]).astype(kind)
    tile = 4 * width + cfg.gate_columns // LANES * LANES
    lane = cfg.gate_columns % LANES
    tile = slice(tile, tile + LANES)
    dense_ref[:, tile] += rows_to_lanes(gain_sum, bias_sum, lane + 2).astype(kind)
    proj_load.wait()
    lane_row = iota((1, LANES), 1)
    scale = HEAD_DIM ** (-0.5)
    block = 256

    def slab(i, carry):
        off = pl.multiple_of(i * LANES, LANES)
        queries = proj_ref[:, pl.ds(off, LANES)] * jnp.asarray(scale, BF16)
        keys = proj_ref[:, pl.ds(width + off, LANES)]
        values = proj_ref[:, pl.ds(2 * width + off, LANES)]
        grads = heads_grad_ref[:, pl.ds(off, LANES)]
        query_grad = [jnp.zeros((block, LANES), F32)] * (count // block)
        key_grad = jnp.zeros((count, LANES), F32)
        value_grad = jnp.zeros((count, LANES), F32)
        for half in (0, 1):
            part = jnp.where(lane_row // HEAD_DIM == half, 1.0, 0.0).astype(BF16)
            query_half, key_half, grads_half = queries * part, keys * part, grads * part
            logs = lse_ref[pl.ds(2 * i + half, 1), :]
            for q in range(count // block):
                span = slice(q * block, (q + 1) * block)
                scores = contract_last(key_half, queries[span]) + bias_ref[:, span] - logs[:, span]
                probs = jnp.exp(scores)
                prob_grad = contract_last(values, grads_half[span])
                score_grad = (probs * (prob_grad - row_sum(probs * prob_grad))).astype(BF16)
                value_grad = value_grad + mm(probs.astype(BF16), grads_half[span])
                key_grad = key_grad + mm(score_grad, query_half[span])
                query_grad[q] = query_grad[q] + contract_first(score_grad, key_half)
        for q in range(count // block):
            qkv_ref[q * block : (q + 1) * block, pl.ds(off, LANES)] = (query_grad[q] * scale).astype(BF16)
        qkv_ref[:, pl.ds(width + off, LANES)] = key_grad.astype(BF16)
        qkv_ref[:, pl.ds(2 * width + off, LANES)] = value_grad.astype(BF16)
        return carry

    lax.fori_loop(0, width // LANES, slab, 0)
    tokens_load.wait()
    left_load.wait()
    gain_sum = jnp.zeros((1, width), F32)
    bias_sum = jnp.zeros((1, width), F32)
    for c in range(count // chunk):
        span = slice(c * chunk, (c + 1) * chunk)
        normed_grad = contract_last(qkv_ref[span, :], full_ref[:, left])
        unit, inverse = norm_parts(tokens_ref[span, :].astype(F32))
        low_ref[span, :] = (unit * gain_one + bias_one).astype(BF16)
        gain_sum = gain_sum + row_sum(normed_grad * unit)
        bias_sum = bias_sum + row_sum(normed_grad)
        grad_all[span, :] = routed_sum[span, :] + norm_back(unit, inverse, gain_one, normed_grad)
        stores.start(grad_all.at[span], grad_ref.at[span])
    turned_ref[...] = jnp.transpose(low_ref[...])
    dense_ref[:, tile] += rows_to_lanes(gain_sum, bias_sum, lane).astype(kind)
    owners = [mask for masks in cfg.owners for mask in masks]
    rows = width // len(owners)
    for c in range(width // chunk):
        span = slice(c * chunk, (c + 1) * chunk)
        dense_ref[span, left] = mm(turned_ref[span, :], qkv_ref[...]).astype(kind)
    if len(dense_outs) == 1:
        stores.start(dense_ref, dense_outs[0])
    else:
        for at, mask in enumerate(owners):
            half = at * 2 // len(owners)
            to = (at - half * len(owners) // 2) * rows
            source = pl.multiple_of((me ^ mask) * rows, rows)
            stores.start(dense_ref.at[pl.ds(source, rows)], dense_outs[half].at[to : to + rows])
    stores.finish()


def output_kernel(cfg, side_ref, hidden_ref, result_ref, out_ref):
    count, width = hidden_ref.shape
    slot = iota_f((count, cfg.experts * cfg.cap), 1)
    pick = (slot == side_ref[:, 0:1]) | (slot == side_ref[:, 1:2])
    mixed = mm(jnp.where(pick, 1.0, 0.0).astype(BF16), result_ref[...])
    out_ref[...] = (hidden_ref[...] + mixed).astype(BF16)


class Config:
    pass


def after(value, other):
    return lax.optimization_barrier((value, other))[0]


def apart(always, part, *args):
    given = jax.eval_shape(part, *args)

    def never(*_):
        return jax.tree.map(lambda s: jnp.zeros(s.shape, s.dtype), given)

    return lax.cond(always, part, never, *args)


def swap_hidden(value, mask):
    size = lax.axis_size("hidden")
    return lax.ppermute(value, "hidden", [(i, i ^ mask) for i in range(size)])


def swap_expert(value, mask):
    size = lax.axis_size("expert")
    return lax.ppermute(value, "expert", [(i, i ^ mask) for i in range(size)])


def gather_rest(own):
    blocks = [own]
    bit = 2
    while bit < lax.axis_size("hidden"):
        blocks += [swap_hidden(block, bit) for block in blocks]
        bit *= 2
    return blocks


def gather_core(half):
    return [swap_hidden(block, 1) for block in half]


def in_turn(first, second):
    return [block for pair in zip(first, second) for block in pair]


def sum_rest(blocks):
    held = {i + 2: [b] for i, b in enumerate(blocks)}
    low = {i: v + [swap_hidden(held[i + 1][0], 1)] for i, v in held.items() if not i & 1}
    held = {0: [], **low}
    bit = 2
    while bit < len(blocks) + 2:
        low = {i: v for i, v in held.items() if not i & bit}
        for i in low:
            value = functools.reduce(jnp.add, held[i ^ bit])
            if 2 * bit == len(blocks) + 2:
                return low[0], value
            low[i] = low[i] + [swap_hidden(value, bit)]
        held = low
        bit *= 2


def body(
    tokens,
    lengths,
    task_ids,
    routes,
    w_qkv,
    w_attn_out,
    w_gate,
    ln1_gain,
    ln1_bias,
    ln2_gain,
    ln2_bias,
    w_in,
    w_out,
    cotangent,
):
    count, width = tokens.shape
    cfg = Config()
    cfg.experts = lax.axis_size("expert")
    cfg.hidden = lax.axis_size("hidden")
    experts, hidden = cfg.experts, cfg.hidden
    cfg.cap = cap = (3 * count * routes.shape[1] + 2 * experts - 1) // (2 * experts)
    cfg.gate_columns = w_gate.shape[1]
    cfg.gate_lanes = round_up(cfg.gate_columns + 4, LANES)
    devices = experts * hidden
    groups = Groups(devices)
    shard_rows = w_qkv.shape[0]
    staged = shard_rows % 16 == 0
    cfg.owners = groups.owners()
    me = (lax.axis_index("expert") * hidden + lax.axis_index("hidden")).astype(jnp.int32)[None]
    extra = 16
    units = w_in.shape[2]
    slots = experts * cap
    wide = 4 * width + cfg.gate_lanes
    one_dot = 2 * count * width * width

    packed = call(
        pack_kernel,
        shape((shard_rows, wide), BF16),
        [],
        [w_qkv, w_attn_out, w_gate, jnp.stack([ln1_gain, ln1_bias, ln2_gain, ln2_bias])],
        1,
    )
    always = lengths[0, 0] > 0

    def first_part(packed, lengths, task_ids, routes, cotangent):
        far = groups.gather_far(packed) if staged else packed
        made = call(
            functools.partial(prep_kernel, cfg),
            [
                shape((count, LANES), F32),
                shape((8, count), F32),
                shape((experts // 2, 2, cap, width), BF16),
            ],
            [],
            [lengths, task_ids, routes, cotangent],
            3 * one_dot,
        )
        return far, made

    dense_far, (side, rows, sent_cot) = apart(
        always, first_part, packed, lengths, task_ids, routes.T, cotangent
    )
    if staged:
        dense_blocks = groups.gather_near(dense_far)
        reached = dense_blocks[1 : len(groups.mid)]
    else:
        dense_blocks = [lax.all_gather(packed, BOTH, axis=0, tiled=True)]
        reached = dense_blocks[0]
    cfg.blocks = len(dense_blocks)
    parity = [list(range(i, experts, 2)) for i in (0, 1)]

    def exchange_even(value):
        return lax.all_to_all(
            value, "expert", split_axis=0, concat_axis=0, axis_index_groups=parity, tiled=True
        )

    def exchange_odd(values):
        return [swap_expert(value, 2 * i + 1) for i, value in enumerate(values)]

    cot_even = exchange_even(sent_cot)
    other = 1 - lax.axis_index("expert") % 2
    cot_odd = lax.dynamic_index_in_dim(cot_even, other, 1, keepdims=False)
    in_half = gather_rest(after(w_in[0], reached))

    outs = call(
        functools.partial(forward_kernel, cfg),
        [
            shape((width, wide), BF16),
            shape((count, 3 * width), BF16),
            shape((count, width), BF16),
            shape((HEADS, count), F32),
            shape((count, width), F32),
            shape((count, LANES), F32),
        ]
        + [shape((experts // 2, cap + extra, width), BF16)]
        + [shape((cap + extra, width), BF16)] * (experts // 2),
        [
            pltpu.VMEM((width, wide), BF16),
            pltpu.VMEM((count, 3 * width), BF16),
            pltpu.VMEM((count, width), BF16),
            pltpu.VMEM((HEADS, count), F32),
            pltpu.VMEM((count, width), F32),
            pltpu.VMEM((count, LANES), F32),
            pltpu.VMEM((experts, cap + extra, width), BF16),
            pltpu.VMEM((count, count), F32),
            pltpu.VMEM((count, width), BF16),
            pltpu.VMEM((count, LANES), F32),
            pltpu.SemaphoreType.DMA((devices,)),
            pltpu.SemaphoreType.DMA((6 + experts,)),
        ],
        [me, side, rows, tokens] + dense_blocks,
        12 * one_dot,
        smem=(0,),
        far_in=range(4, 4 + cfg.blocks),
        far_out=range(7 + experts // 2),
    )
    full, proj, heads, lse, hidden_one, gates = outs[:6]
    send_rows = outs[6:]
    def even_part(even_send, odd_send, cot_even, cot_odd, in_half, own_out):
        out_half = gather_rest(own_out)
        more_in, more_out = gather_core(in_half), gather_core(out_half)
        blocks = in_turn(in_half, more_in) + in_turn(out_half, more_out)
        even_rows = exchange_even(even_send)
        odd_rows = exchange_odd(odd_send)
        cot_odd = swap_expert(cot_odd, 1)
        out = expert_part(cfg, 0, me, cot_even, [even_rows], blocks, [])
        return even_rows, odd_rows, cot_odd, more_in, out_half[1:], more_out, out

    def odd_part(even_send, even_rows, odd_rows, cot_odd, in_blocks, out_blocks, before, even_pairs):
        even_back = exchange_even(even_send)
        blocks = in_blocks + out_blocks
        result, sends, pairs = expert_part(cfg, 1, me, cot_odd, odd_rows, blocks, [before])
        odd_back = exchange_odd(sends)
        sums = apart(always, far_weights, even_rows, odd_rows, [even_pairs, pairs], in_blocks, out_blocks)
        return [even_back] + odd_back, result, pairs, *sums

    def far_weights(even_rows, odd_rows, pairs, in_blocks, out_blocks):
        picked = [b for b in range(hidden) if b > 1]
        return sum_rest(
            weight_part(cfg, picked, me, even_rows, odd_rows, pairs, in_blocks, out_blocks)
        )

    def own_weights(even_rows, odd_rows, pairs, in_blocks, out_blocks):
        return weight_part(cfg, [0, 1], me, even_rows, odd_rows, pairs, in_blocks, out_blocks)

    even_rows, odd_rows, cot_odd, more_in, rest_out, more_out, even_out = apart(
        always, even_part, send_rows[0], send_rows[1:], cot_even, cot_odd, in_half, w_out[0]
    )
    out_half = [w_out[0]] + rest_out
    in_blocks, out_blocks = in_turn(in_half, more_in), in_turn(out_half, more_out)
    back, result, odd_pairs, held, value = apart(
        always,
        odd_part,
        even_out[1][0],
        even_rows,
        odd_rows,
        cot_odd,
        in_blocks,
        out_blocks,
        even_out[0],
        even_out[2],
    )
    pairs = [even_out[2], odd_pairs]
    returned = lax.all_to_all(
        after(result, back), "expert", split_axis=0, concat_axis=0, tiled=True
    )
    if staged:
        dense_shapes = [shape((width // 2, wide), BF16)] * 2
    else:
        dense_shapes = [shape((width, wide), F32)]
    cfg.dense_outs = len(dense_shapes)

    def back_part(value, back):
        args = [me, side, rows, gates, lse] + back + [hidden_one, cotangent, heads, tokens, proj, full]
        outs = call(
            functools.partial(backward_kernel, cfg),
            [shape((count, width), F32)] + dense_shapes,
            [
                pltpu.VMEM((slots, width), BF16),
                pltpu.VMEM((experts, extra, width), BF16),
                pltpu.VMEM((count, width), F32),
                pltpu.VMEM((count, width), BF16),
                pltpu.VMEM((count, width), BF16),
                pltpu.VMEM((count, width), BF16),
                pltpu.VMEM((count, 3 * width), BF16),
                pltpu.VMEM((width, wide), BF16),
                pltpu.VMEM((count, width), F32),
                pltpu.VMEM((count, width), BF16),
                pltpu.VMEM((count, cfg.gate_lanes), BF16),
                pltpu.VMEM((count, width), BF16),
                pltpu.VMEM((count, width), BF16),
                pltpu.VMEM((count, count), F32),
                pltpu.VMEM((count, 3 * width), BF16),
                pltpu.VMEM((width, count), BF16),
                pltpu.VMEM((width, wide), dense_shapes[0].dtype),
                pltpu.VMEM((count, width), F32),
                pltpu.SemaphoreType.DMA((2 * experts + 7,)),
                pltpu.SemaphoreType.DMA((4 + devices,)),
            ],
            args,
            19 * one_dot,
            smem=(0,),
            far_in=range(5, len(args)),
            far_out=range(1 + len(dense_shapes)),
        )
        return swap_hidden(value, hidden // 2), outs

    last, outs = apart(always, back_part, value, back)
    reached = held + [last]
    grad_tokens = outs[0]

    def last_weights(blocks):
        got = [groups.swap(b, m) for b, m in zip(blocks[1:], groups.mid[1:])]
        return got, own_weights(even_rows, odd_rows, pairs, in_blocks, out_blocks)

    def last_sums(blocks, own, more, reached, returned):
        layer_out = call(
            functools.partial(output_kernel, cfg),
            shape((count, width), BF16),
            [],
            [side, hidden_one, returned.reshape(slots, width)],
            6 * one_dot,
        )
        got = [groups.swap(b, m) for b, m in zip(blocks[1:], groups.far[1:])]
        terms = [own, swap_hidden(more, 1)] + reached
        grad_in, grad_out = call(
            turn_add_kernel,
            [shape((width, units), F32), shape((units, width), F32)],
            [],
            terms,
            4 * width * units,
            limit=2 * SMALL_LIMIT,
        )
        return got, grad_in, grad_out, layer_out

    blocks = [None]
    if staged:
        blocks = add_parts(outs[1], [groups.swap(outs[2], 1)], len(groups.mid))
    got, (own, more) = apart(always, last_weights, blocks)
    if staged:
        blocks = add_parts(blocks[0], got, len(groups.far))
    got, grad_in, grad_out, layer_out = apart(
        always, last_sums, blocks, own, more, reached, returned
    )
    if staged:
        dense_terms = blocks[:1] + got
    else:
        dense_terms = [lax.psum_scatter(outs[1], BOTH, scatter_dimension=0, tiled=True)]
    dense_outs = call(
        functools.partial(split_kernel, cfg),
        [shape((shard_rows, c), F32) for c in (3 * width, width, cfg.gate_columns)]
        + [shape((1, shard_rows), F32)] * 4,
        [],
        dense_terms,
        shard_rows * wide,
        limit=SMALL_LIMIT,
    )

    return (
        layer_out,
        grad_tokens,
        *dense_outs[:3],
        *[v.reshape(shard_rows) for v in dense_outs[3:]],
        grad_in[None],
        grad_out[None],
    )


def solution(mesh):
    split = P(BOTH, None)
    vector = P(BOTH)
    placed = (split,) * 7 + (vector,) * 4 + (P("expert", None, "hidden"), P("expert", "hidden", None), split)
    return jax.shard_map(
        body,
        mesh=mesh,
        in_specs=placed,
        out_specs=(split,) * 5
        + (vector,) * 4
        + (P("expert", None, "hidden"), P("expert", "hidden", None)),
        check_vma=False,
    )
```

```python
import functools

import jax
import jax.numpy as jnp
from jax import lax
from jax.experimental import pallas as pl
from jax.experimental.pallas import tpu as pltpu
from jax.sharding import PartitionSpec as P

HEADS = 8
HEAD_DIM = 64
EPS = 1e-05
NEG_FILL = -1e30
LANES = 128
BOTH = ("expert", "hidden")
F32 = jnp.float32
BF16 = jnp.bfloat16
VMEM_LIMIT = 56 * 1024 * 1024
SMALL_LIMIT = 8 * 1024 * 1024


def mm(left, right):
    return jnp.dot(left, right, preferred_element_type=F32)


def contract_last(left, right):
    return lax.dot_general(left, right, (((1,), (1,)), ((), ())), preferred_element_type=F32)


def contract_first(left, right):
    return lax.dot_general(left, right, (((0,), (0,)), ((), ())), preferred_element_type=F32)


def iota(shape, axis):
    return lax.broadcasted_iota(jnp.int32, shape, axis)


def iota_f(shape, axis):
    return iota(shape, axis).astype(F32)


def lane_sum(values):
    return jnp.sum(values, axis=1, keepdims=True)


def row_sum(values):
    return jnp.sum(values, axis=0, keepdims=True)


def norm_parts(values):
    middle = jnp.mean(values, axis=-1, keepdims=True)
    centred = values - middle
    spread = jnp.mean(centred * centred, axis=-1, keepdims=True)
    inverse = lax.rsqrt(spread + EPS)
    return centred * inverse, inverse


def norm_back(unit, inverse, gain, grad):
    scaled = grad * gain
    mean_one = jnp.mean(scaled, axis=-1, keepdims=True)
    mean_two = jnp.mean(scaled * unit, axis=-1, keepdims=True)
    return inverse * (scaled - mean_one - unit * mean_two)


def round_up(value, step):
    return (value + step - 1) // step * step


def call(kernel, outs, scratch, args, flops, smem=(), far_in=(), far_out=(), limit=VMEM_LIMIT):
    def spec(at):
        space = pltpu.SMEM if at in smem else pl.ANY if at in far_in else pltpu.VMEM
        return pl.BlockSpec(memory_space=space)

    def out_spec(at):
        return pl.BlockSpec(memory_space=pl.ANY if at in far_out else pltpu.VMEM)

    touched = sum(a.size * a.dtype.itemsize for a in args) + sum(
        o.size * o.dtype.itemsize for o in jax.tree.leaves(outs)
    )
    got = pl.pallas_call(
        kernel,
        out_shape=outs,
        in_specs=[spec(at) for at in range(len(args))],
        out_specs=[out_spec(at) for at in range(len(outs))] if isinstance(outs, list) else out_spec(0),
        scratch_shapes=scratch,
        compiler_params=pltpu.CompilerParams(vmem_limit_bytes=limit),
        cost_estimate=pl.CostEstimate(flops=1, bytes_accessed=1, transcendentals=0),
    )(*args)
    return list(got) if isinstance(outs, list) else got


def shape(dims, dtype):
    return jax.ShapeDtypeStruct(dims, dtype)


def slot_targets(cfg, routes_ref):
    count, experts = routes_ref.shape[1], cfg.experts
    both = jnp.zeros((8, count), F32)
    for at in (0, 1):
        both = jnp.where(iota((8, count), 0) == at, routes_ref[at : at + 1, :].astype(F32), both)
    routes = jnp.transpose(both)
    first, second = routes[:, 0:1], routes[:, 1:2]
    lane_e = iota_f((count, experts), 1)
    hot_one = jnp.where(lane_e == first, 1.0, 0.0)
    hot_two = jnp.where(lane_e == second, 1.0, 0.0)
    before = jnp.where(iota((count, count), 1) < iota((count, count), 0), 1.0, 0.0).astype(BF16)
    earlier = mm(before, (hot_one + hot_two).astype(BF16))
    target_one = first * cfg.cap + lane_sum(earlier * hot_one)
    target_two = second * cfg.cap + lane_sum(earlier * hot_two)
    return first, second, target_one, target_two


def prep_kernel(cfg, lens_ref, tasks_ref, routes_ref, cot_in, side_out, rows_out, sent_out, *scratch):
    experts, cap = cfg.experts, cfg.cap
    cot_ref, side_ref, rows_ref, sent_ref, in_sems, out_sems = scratch
    loads, stores = Copies(in_sems), Copies(out_sems)
    loads.start(cot_in, cot_ref)
    count = routes_ref.shape[1]
    sents = lens_ref.shape[1]
    lens = lens_ref[...].astype(F32)
    tasks = tasks_ref[...].astype(F32)
    down, across = iota((sents, sents), 0), iota((sents, sents), 1)
    ends_col = lane_sum(jnp.where(across <= down, lens, 0.0))
    ends_row = row_sum(jnp.where(across == down, ends_col, 0.0))
    passed = jnp.where(iota_f((count, sents), 0) >= ends_row, 1.0, 0.0)
    sentence = lane_sum(passed)
    task = lane_sum(jnp.where(iota_f((count, sents), 1) == sentence, tasks, 0.0))
    lane = iota((count, LANES), 1)
    first, second, target_one, target_two = slot_targets(cfg, routes_ref)
    side = jnp.where(lane == 0, target_one, 0.0)
    side = jnp.where(lane == 1, target_two, side)
    side = jnp.where(lane == 2, task * experts + first, side)
    side = jnp.where(lane == 3, task * experts + second, side)
    side = jnp.where(lane == 4, sentence, side)
    side = jnp.where(lane == 5, first, side)
    side = jnp.where(lane == 6, second, side)
    side_ref[...] = side
    stores.start(side_ref, side_out)
    turned = jnp.transpose(side)
    rows_ref[...] = turned[0:8, :]
    stores.start(rows_ref, rows_out)
    one_row, two_row = turned[0:1, :], turned[1:2, :]
    loads.finish()
    cot = cot_ref[...]
    for e in range(experts):
        at = iota_f((cap, count), 0) + float(e * cap)
        pick = jnp.where((at == one_row) | (at == two_row), 1.0, 0.0).astype(BF16)
        sent_ref[e // 2, e % 2] = mm(pick, cot).astype(BF16)
        stores.start(sent_ref.at[e // 2, e % 2], sent_out.at[e // 2, e % 2])
    stores.finish()


def pack_kernel(qkv_ref, attn_ref, gate_ref, *refs):
    vector_refs, out_ref = refs[:4], refs[4]
    rows = out_ref.shape[0]
    at = 0
    for ref in (qkv_ref, attn_ref):
        out_ref[:, at : at + ref.shape[1]] = ref[...]
        at += ref.shape[1]
    columns = gate_ref.shape[1]
    lanes = out_ref.shape[1] - at
    tile = columns // LANES * LANES
    out_ref[:, at : at + columns] = gate_ref[...]
    eye = iota((rows, rows), 0) == iota((rows, rows), 1)
    lane = iota((rows, lanes - tile), 1)
    last = out_ref[:, at + tile :].astype(F32)
    last = jnp.where(lane < columns - tile, last, 0.0)
    for i in range(4):
        column = lane_sum(jnp.where(eye, vector_refs[i][...].astype(F32), 0.0))
        last = jnp.where(lane == columns - tile + i, column, last)
    out_ref[:, at + tile :] = last.astype(BF16)


class Groups:
    def __init__(self, devices):
        bits = devices.bit_length() - 1
        mid = (bits - 1) // 2
        self.near = [1]
        self.mid = self.masks(1, mid)
        self.far = self.masks(1 + mid, bits - 1 - mid)
        self.devices = devices

    @staticmethod
    def masks(low, width):
        return [m << low for m in range(1 << width)]

    def owners(self):
        return [[n | b | c for c in self.far] for n in (0, 1) for b in self.mid]

    def swap(self, value, mask):
        return lax.ppermute(value, BOTH, [(i, i ^ mask) for i in range(self.devices)])

    def gather_far(self, shard):
        return jnp.concatenate([shard] + [self.swap(shard, m) for m in self.far[1:]], axis=0)

    def gather_near(self, far):
        mid = [far] + [self.swap(far, m) for m in self.mid[1:]]
        return mid + [self.swap(block, 1) for block in mid]


def add_kernel(parts, keep_ref, *refs):
    got, outs = refs[: len(refs) - parts], refs[len(refs) - parts :]
    rows = outs[0].shape[0]
    for i, out_ref in enumerate(outs):
        span = slice(i * rows, (i + 1) * rows)
        total = keep_ref[span, :].astype(F32)
        for ref in got:
            total = total + ref[span, :].astype(F32)
        out_ref[...] = total.astype(out_ref.dtype)


def add_parts(keep, got, parts):
    rows, columns = keep.shape
    outs = [shape((rows // parts, columns), F32 if i == 0 else BF16) for i in range(parts)]
    return call(
        functools.partial(add_kernel, parts), outs, [], [keep] + got, rows * columns * len(got), limit=SMALL_LIMIT
    )


def split_kernel(cfg, *refs):
    terms, outs = refs[:-7], refs[-7:]
    rows, width = outs[0].shape[0], outs[1].shape[1]

    def total(start, stop):
        value = terms[0][:, start:stop]
        for ref in terms[1:]:
            value = value + ref[:, start:stop].astype(F32)
        return value

    outs[0][...] = total(0, 3 * width)
    outs[1][...] = total(3 * width, 4 * width)
    outs[2][...] = total(4 * width, 4 * width + cfg.gate_columns)
    tile = 4 * width + cfg.gate_columns // LANES * LANES
    lane = cfg.gate_columns % LANES
    turned = jnp.transpose(total(tile, tile + LANES))
    for i in range(4):
        outs[3 + i][...] = turned[lane + i : lane + i + 1, :]


def gain_rows(full_ref, start, gate_columns):
    tile = start + gate_columns // LANES * LANES
    lane = gate_columns % LANES
    turned = jnp.transpose(full_ref[:, tile : tile + LANES].astype(F32))
    return [turned[lane + i : lane + i + 1, :] for i in range(4)]


def forward_kernel(cfg, me_ref, side_ref, rows_ref, tokens_ref, *refs):
    n, cap = cfg.experts, cfg.cap
    blocks, refs = refs[: cfg.blocks], refs[cfg.blocks :]
    outs, refs = refs[:6], refs[6:]
    even_out, odd_outs, refs = refs[0], refs[1 : 1 + n // 2], refs[1 + n // 2 :]
    full_ref, proj_ref, heads_ref, turned_ref, hidden_ref, gates_ref, send_all = refs[:7]
    rows_all, pick_ref_all, bias_ref, routed_ref, lse_ref, in_sems, out_sems = refs[7:]
    count, width = tokens_ref.shape
    me = me_ref[0]
    mine = me // cfg.hidden
    loads, stores = Copies(in_sems), Copies(out_sems)
    if len(blocks) == 1:
        loads.start(blocks[0], full_ref)
    else:
        for block_ref, masks in zip(blocks, cfg.owners):
            rows = block_ref.shape[0] // len(masks)
            for i, mask in enumerate(masks):
                at = pl.multiple_of((me ^ mask) * rows, rows)
                loads.start(block_ref.at[i * rows : (i + 1) * rows], full_ref.at[pl.ds(at, rows)])
    chunk = 512
    for c in range(count // chunk):
        span = slice(c * chunk, (c + 1) * chunk)
        bias_ref[span, :] = jnp.where(side_ref[span, 4:5] == rows_ref[4:5, :], 0.0, NEG_FILL)
        hidden_ref[span, :], _ = norm_parts(tokens_ref[span, :].astype(F32))
    for k in range(n):
        at = iota_f((cap, count), 0) + ((mine ^ k) * cap).astype(F32)
        pick = (at == rows_ref[0:1, :]) | (at == rows_ref[1:2, :])
        pick_ref_all[k * cap : (k + 1) * cap, :] = jnp.where(pick, 1.0, 0.0).astype(BF16)
    loads.finish()
    stores.start(full_ref, outs[0])
    gain_one, bias_one, gain_two, bias_two = gain_rows(full_ref, 4 * width, cfg.gate_columns)
    for c in range(count // chunk):
        span = slice(c * chunk, (c + 1) * chunk)
        routed_ref[span, :] = (hidden_ref[span, :] * gain_one + bias_one).astype(BF16)
    proj_ref[...] = mm(routed_ref[...], full_ref[:, : 3 * width]).astype(BF16)
    stores.start(proj_ref, outs[1])
    lse_ref[...] = jnp.zeros_like(lse_ref)
    lane = iota((1, LANES), 1)
    scale = HEAD_DIM ** (-0.5)
    block = 256

    def slab(i, carry):
        off = i * LANES
        keys = proj_ref[:, pl.ds(width + off, LANES)]
        values = proj_ref[:, pl.ds(2 * width + off, LANES)]
        halves = []
        for half in (0, 1):
            mine = jnp.where(lane // HEAD_DIM == half, 1.0, 0.0).astype(BF16)
            halves.append((keys * mine, values * mine))
        for r in range(count // block):
            span = slice(r * block, (r + 1) * block)
            queries = proj_ref[span, pl.ds(off, LANES)]
            total = jnp.zeros((block, LANES), F32)
            logs = lse_ref[span, :]
            for half, (key_half, value_half) in enumerate(halves):
                scores = contract_last(queries, key_half) * scale + bias_ref[span, :]
                highest = jnp.max(scores, axis=1, keepdims=True)
                expo = jnp.exp(scores - highest)
                sums = lane_sum(expo)
                probs = (expo * (1.0 / sums)).astype(BF16)
                total = total + mm(probs, value_half)
                logs = jnp.where(lane == 2 * i + half, highest + jnp.log(sums), logs)
            heads_ref[span, pl.ds(off, LANES)] = total.astype(BF16)
            lse_ref[span, :] = logs
        return carry

    for i in range(width // LANES):
        slab(i, 0)
    stores.start(heads_ref, outs[2])
    turned_ref[...] = jnp.transpose(lse_ref[...])[:HEADS, :]
    stores.start(turned_ref, outs[3])
    for c in range(count // chunk):
        span = slice(c * chunk, (c + 1) * chunk)
        attended = mm(heads_ref[span, :], full_ref[:, 3 * width : 4 * width])
        hidden = tokens_ref[span, :].astype(F32) + attended
        hidden_ref[span, :] = hidden
        unit, _ = norm_parts(hidden)
        routed = (unit * gain_two + bias_two).astype(BF16)
        routed_ref[span, :] = routed
        logits = mm(routed, full_ref[:, 4 * width :])
        column = iota_f(logits.shape, 1)
        one = lane_sum(jnp.where(column == side_ref[span, 2:3], logits, 0.0))
        two = lane_sum(jnp.where(column == side_ref[span, 3:4], logits, 0.0))
        top = jnp.maximum(one, two)
        expo_one, expo_two = jnp.exp(one - top), jnp.exp(two - top)
        both = expo_one + expo_two
        gates_ref[span, :] = jnp.where(
            lane == 0, expo_one / both, jnp.where(lane == 1, expo_two / both, 0.0)
        )
    stores.start(hidden_ref, outs[4])
    stores.start(gates_ref, outs[5])
    gate_lanes = round_up(cap, LANES)
    rows_all[...] = mm(pick_ref_all[...], routed_ref[...]).astype(BF16)
    for k in range(n):
        base = ((mine ^ k) * cap).astype(F32)
        out_ref = pick_ref(mine, k, even_out, odd_outs)
        stores.start(rows_all.at[k * cap : (k + 1) * cap], out_ref.at[0:cap])
        slot = iota_f((count, gate_lanes), 1) + base
        row = row_sum(
            jnp.where(slot == side_ref[:, 0:1], gates_ref[:, 0:1], 0.0)
            + jnp.where(slot == side_ref[:, 1:2], gates_ref[:, 1:2], 0.0)
        )
        put_split(send_all.at[k], 0, row)
        stores.start(send_all.at[k], out_ref.at[cap : cap + send_all.shape[1]])
    stores.finish()


def pick_ref(mine, k, even_ref, odd_refs):
    return odd_refs[k // 2] if k % 2 else even_ref.at[(mine ^ k) // 2]


def put_split(ref, cap, row):
    extra = ref.shape[0] - cap
    high = row.astype(BF16).astype(F32)
    down = iota((extra, row.shape[1]), 0)
    both = jnp.where(down == 0, high, jnp.where(down == 1, row - high, 0.0))
    ref[cap:, :] = jnp.zeros((extra, ref.shape[1]), BF16)
    ref[cap:, 0 : row.shape[1]] = both.astype(BF16)


def take_split(ref, cap, lanes):
    both = ref[cap:, 0:lanes].astype(F32)
    return both[0:1, :] + both[1:2, :]


def gelu_parts(pre):
    root = 0.7978845608028654
    cubic = 0.044715
    square = pre * pre
    upper = 0.5 + 0.5 * jnp.tanh(pre * (root + (root * cubic) * square))
    act = pre * upper
    return act, upper + act * (1.0 - upper) * (2.0 * root + (6.0 * root * cubic) * square)


class Copies:
    def __init__(self, sems):
        self.sems, self.count, self.open = sems, 0, []

    def start(self, source, target, kept=True):
        copy = pltpu.make_async_copy(source, target, self.sems.at[self.count])
        self.count += 1
        copy.start()
        if kept:
            self.open.append(copy)
        return copy

    def finish(self):
        for copy in self.open:
            copy.wait()


def expert_kernel(cfg, odd, me_ref, *refs):
    h, cap, n = cfg.hidden, cfg.cap, cfg.experts // 2
    many = n if odd else 1
    cot_ref, refs = refs[0], refs[1:]
    row_refs, refs = refs[:many], refs[many:]
    in_refs, out_refs, refs = refs[:h], refs[h : 2 * h], refs[2 * h :]
    if odd:
        before_ref, refs = refs[0], refs[1:]
    result_ref, back_refs, refs = refs[0], refs[1 : 1 + many], refs[1 + many :]
    pairs_ref, refs = refs[0], refs[1:]
    rows_all, cot_all, pairs_all, result_all, back_all, before_all, extra_in, extra_out = refs[:8]
    result_sum, back_sum, weights_all, in_sems, out_sems = refs[8:]
    total, width = rows_all.shape
    extra = extra_in.shape[1]
    mine = me_ref[0] // h
    loads, stores = Copies(in_sems), Copies(out_sems)
    ks = list(range(odd, 2 * n, 2))
    tiles = 2
    per = n // tiles
    tile = per * cap
    row_loads, weight_loads = [], []

    def load_rows(m):
        for i in range(m * per, (m + 1) * per):
            span = slice(i * cap, (i + 1) * cap)
            source = (mine ^ ks[i]) // 2
            row_ref = pick_ref(mine, ks[i], row_refs[0], row_refs)
            from_ref = cot_ref.at[source] if odd else cot_ref.at[source, mine % 2]
            row_loads.append(
                (
                    loads.start(row_ref.at[0:cap], rows_all.at[span], False),
                    loads.start(row_ref.at[cap : cap + extra], extra_in.at[i], False),
                    loads.start(from_ref, cot_all.at[span], False),
                )
            )

    load_rows(0)
    for i, ref in enumerate(in_turn(in_refs, out_refs)):
        held = weights_all.at[i, : ref.shape[0], : ref.shape[1]]
        weight_loads.append(loads.start(ref, held, False))
    for m in range(1, tiles):
        load_rows(m)
    if odd:
        before_loads = [loads.start(before_ref.at[i], before_all.at[i], False) for i in range(n)]
    gate_lanes = round_up(cap, LANES)
    eye = iota((cap, gate_lanes), 0) == iota((cap, gate_lanes), 1)
    units = in_refs[0].shape[1]
    gates = {}
    for m in range(tiles):
        span = slice(m * tile, (m + 1) * tile)
        for i in range(m * per, (m + 1) * per):
            for copy in row_loads[i]:
                copy.wait()
            rows = slice(i * cap, (i + 1) * cap)
            gates[i] = lane_sum(jnp.where(eye, take_split(extra_in.at[i], 0, gate_lanes), 0.0))
            pairs_all[rows, :] = (gates[i] * cot_all[rows, :].astype(F32)).astype(BF16)
        stores.start(pairs_all.at[span], pairs_ref.at[span])
        for b in range(h):
            if m == 0:
                weight_loads[2 * b].wait()
                weight_loads[2 * b + 1].wait()
            w_in, w_out = weights_all.at[2 * b, :, :units], weights_all.at[2 * b + 1, :units, :]
            act, slope = gelu_parts(mm(rows_all[span, :], w_in[...]))
            act_low = act.astype(BF16)
            act_grad = contract_last(pairs_all[span, :], w_out[...])
            pre_grad = (act_grad * slope).astype(BF16)
            result = mm(act_low, w_out[...])
            back = contract_last(pre_grad, w_in[...])
            if b == 0:
                result_sum[...] = result
                back_sum[...] = back
            elif b < h - 1:
                result_sum[...] += result
                back_sum[...] += back
            else:
                result_sum[...] += result
                back_all[span, :] = (back_sum[...] + back).astype(BF16)
        if odd and m == 0:
            for i in range(n):
                before_loads[i].wait()
                stores.start(before_all.at[i], result_ref.at[mine ^ (2 * i)])
        for i in range(m * per, (m + 1) * per):
            rows, k = slice(i * cap, (i + 1) * cap), ks[i]
            back_ref = pick_ref(mine, k, back_refs[0], back_refs)
            stores.start(back_all.at[rows], back_ref.at[0:cap])
            result = result_sum[(i - m * per) * cap : (i - m * per + 1) * cap, :]
            result_all[rows, :] = (gates[i] * result).astype(BF16)
            stores.start(result_all.at[rows], result_ref.at[mine ^ k if odd else i])
            dots = lane_sum(cot_all[rows, :].astype(F32) * result)
            put_split(extra_out.at[i], 0, row_sum(jnp.where(eye, dots, 0.0)))
            stores.start(extra_out.at[i], back_ref.at[cap : cap + extra])
    stores.finish()


def expert_part(cfg, odd, me, cot, rows, weights, before):
    n, h, cap, extra = cfg.experts // 2, cfg.hidden, cfg.cap, 16
    width, units = cot.shape[-1], weights[0].shape[1]
    slots = n * cap
    many = len(rows)
    side = max(width, units)
    args = [me, cot] + rows + weights + before
    outs = (
        [shape((2 * n if odd else n, cap, width), BF16)]
        + [shape(r.shape, BF16) for r in rows]
        + [shape((slots, width), BF16)]
    )
    outs = call(
        functools.partial(expert_kernel, cfg, odd),
        outs,
        [pltpu.VMEM((slots, width), BF16)] * 5
        + [pltpu.VMEM((n, cap, width), BF16)]
        + [pltpu.VMEM((n, extra, width), BF16)] * 2
        + [pltpu.VMEM((slots // 2, width), F32)] * 2
        + [pltpu.VMEM((2 * h, side, side), BF16)]
        + [pltpu.SemaphoreType.DMA((4 * n + 2 * h,)), pltpu.SemaphoreType.DMA((4 * n + 2,))],
        args,
        8 * slots * width * units * h,
        smem=(0,),
        far_in=range(1, len(args)),
        far_out=range(len(outs)),
    )
    return outs[0], outs[1 : 1 + many], outs[1 + many]


def weight_kernel(cfg, parts, me_ref, *refs):
    n, cap = cfg.experts, cfg.cap
    even_ref, odd_refs, refs = refs[0], refs[1 : 1 + n // 2], refs[1 + n // 2 :]
    pair_refs, in_refs, out_refs, refs = refs[:2], refs[2 : 2 + parts], refs[2 + parts : 2 + 2 * parts], refs[2 + 2 * parts :]
    grad_refs, refs = refs[:parts], refs[parts:]
    grads_all, refs = refs[:parts], refs[parts:]
    rows_all, pairs_all, rows_turned, pairs_turned, act_all, pre_all, weights_all, in_sems, out_sems = refs
    total, width = rows_all.shape
    half = total // 2
    units = act_all.shape[1]
    mine = me_ref[0] // cfg.hidden
    loads, stores = Copies(in_sems), Copies(out_sems)
    waits = {0: [], 1: []}
    weight_loads = []
    for odd in (0, 1):
        for i in range(n // 2):
            k = 2 * i + odd
            span = slice(odd * half + i * cap, odd * half + (i + 1) * cap)
            row_ref = pick_ref(mine, k, even_ref, odd_refs)
            waits[odd].append(loads.start(row_ref.at[0:cap], rows_all.at[span], False))
        span = slice(odd * half, (odd + 1) * half)
        waits[odd].append(loads.start(pair_refs[odd], pairs_all.at[span], False))
        if not odd:
            for i, ref in enumerate(in_turn(in_refs, out_refs)):
                held = weights_all.at[i, : ref.shape[0], : ref.shape[1]]
                weight_loads.append(loads.start(ref, held, False))
    tile = half // 2
    for p in range(parts):
        weight_loads[2 * p].wait()
        weight_loads[2 * p + 1].wait()
        w_in, w_out = weights_all.at[2 * p, :, :units], weights_all.at[2 * p + 1, :units, :]
        for m in range(4):
            if p == 0 and m % 2 == 0:
                for copy in waits[m // 2]:
                    copy.wait()
                span = slice(m // 2 * half, (m // 2 + 1) * half)
                rows_turned[:, span] = jnp.transpose(rows_all[span, :])
                pairs_turned[:, span] = jnp.transpose(pairs_all[span, :])
            span = slice(m * tile, (m + 1) * tile)
            act, slope = gelu_parts(mm(rows_all[span, :], w_in[...]))
            act_all[span, :] = act.astype(BF16)
            act_grad = contract_last(pairs_all[span, :], w_out[...])
            pre_all[span, :] = (act_grad * slope).astype(BF16)
        kept = grads_all[p]
        kept[:width, :] = mm(rows_turned[...], pre_all[...]).astype(kept.dtype)
        kept[width:, :] = mm(pairs_turned[...], act_all[...]).astype(kept.dtype)
        stores.start(kept, grad_refs[p])
    stores.finish()


def weight_part(cfg, picked, me, even_rows, odd_rows, pairs, ins, outs):
    width, units = ins[0].shape
    slots, parts = cfg.experts * cfg.cap, len(picked)
    args = [me, even_rows] + odd_rows + pairs + [ins[b] for b in picked] + [outs[b] for b in picked]
    kinds = [BF16 if b else F32 for b in picked]
    side = max(width, units)
    return call(
        functools.partial(weight_kernel, cfg, parts),
        [shape((2 * width, units), kind) for kind in kinds],
        [pltpu.VMEM((2 * width, units), kind) for kind in kinds]
        + [pltpu.VMEM((slots, width), BF16)] * 2
        + [pltpu.VMEM((width, slots), BF16)] * 2
        + [pltpu.VMEM((slots, units), BF16)] * 2
        + [pltpu.VMEM((2 * parts, side, side), BF16)]
        + [pltpu.SemaphoreType.DMA((cfg.experts + 2 + 2 * parts,)), pltpu.SemaphoreType.DMA((parts,))],
        args,
        8 * slots * width * units * parts,
        smem=(0,),
        far_in=range(1, len(args)),
        far_out=range(parts),
    )


def turn_add_kernel(*refs):
    terms, (sum_in, sum_out) = refs[:-2], refs[-2:]
    width = sum_in.shape[0]
    total = terms[0][...]
    for ref in terms[1:]:
        total = total + ref[...].astype(F32)
    sum_in[...] = total[:width, :]
    sum_out[...] = jnp.transpose(total[width:, :])


def rows_to_lanes(first, second, lane):
    down = iota((LANES, first.shape[1]), 0)
    return jnp.transpose(jnp.where(down == lane, first, jnp.where(down == lane + 1, second, 0.0)))


def backward_kernel(cfg, me_ref, side_ref, rows_ref, gates_ref, lse_ref, *refs):
    n, cap = cfg.experts, cfg.cap
    even_ref, odd_refs, refs = refs[0], refs[1 : 1 + n // 2], refs[1 + n // 2 :]
    hidden_in, cot_in, heads_in, tokens_in, proj_in, full_in, refs = *refs[:6], refs[6:]
    grad_ref, dense_outs, refs = refs[0], refs[1 : 1 + cfg.dense_outs], refs[1 + cfg.dense_outs :]
    back_all, extra_all, hidden_ref, cot_ref, heads_ref, tokens_ref, proj_ref, full_ref = refs[:8]
    routed_sum, routed_ref, logits_ref, low_ref, heads_grad_ref, bias_ref, qkv_ref = refs[8:15]
    turned_ref, dense_ref, grad_all, in_sems, out_sems = refs[15:]
    count, width = hidden_ref.shape
    extra = extra_all.shape[1]
    me = me_ref[0]
    mine = me // cfg.hidden
    loads, stores = Copies(in_sems), Copies(out_sems)
    back_loads = []
    for k in range(n):
        ref = pick_ref(mine, k, even_ref, odd_refs)
        span = slice(k * cap, (k + 1) * cap)
        back_loads.append(loads.start(ref.at[0:cap], back_all.at[span], False))
        back_loads.append(loads.start(ref.at[cap : cap + extra], extra_all.at[k], False))
    hidden_load = loads.start(hidden_in, hidden_ref, False)
    right = slice(3 * width, full_ref.shape[1])
    left = slice(0, 3 * width)
    right_load = loads.start(full_in.at[:, right], full_ref.at[:, right], False)
    cot_load = loads.start(cot_in, cot_ref, False)
    heads_load = loads.start(heads_in, heads_ref, False)
    proj_load = loads.start(proj_in, proj_ref, False)
    tokens_load = loads.start(tokens_in, tokens_ref, False)
    left_load = loads.start(full_in.at[:, left], full_ref.at[:, left], False)

    def relative(at):
        expert = side_ref[:, 5 + at : 6 + at]
        turned = (expert.astype(jnp.int32) ^ mine).astype(F32)
        return side_ref[:, at : at + 1] + (turned - expert) * cap

    one, two = relative(0), relative(1)
    slot = iota_f((count, n * cap), 1)
    pick = jnp.where((slot == one) | (slot == two), 1.0, 0.0).astype(BF16)
    chunk = 512
    for c in range(count // chunk):
        span = slice(c * chunk, (c + 1) * chunk)
        bias_ref[span, :] = jnp.where(side_ref[span, 4:5] == rows_ref[4:5, :], 0.0, NEG_FILL)
    for copy in back_loads:
        copy.wait()
    routed_sum[...] = mm(pick, back_all[...])
    gate_lanes = round_up(cap, LANES)
    dots_one = jnp.zeros((count, gate_lanes), F32)
    dots_two = jnp.zeros((count, gate_lanes), F32)
    lane_at = iota_f((count, gate_lanes), 1)
    for k in range(n):
        slot = jnp.where(lane_at < cap, lane_at + float(k * cap), -1.0)
        dots = take_split(extra_all.at[k], 0, gate_lanes)
        dots_one = dots_one + jnp.where(slot == one, dots, 0.0)
        dots_two = dots_two + jnp.where(slot == two, dots, 0.0)
    dot_one, dot_two = lane_sum(dots_one), lane_sum(dots_two)
    gate_one, gate_two = gates_ref[:, 0:1], gates_ref[:, 1:2]
    shared = gate_one * dot_one + gate_two * dot_two
    chosen_one = gate_one * (dot_one - shared)
    chosen_two = gate_two * (dot_two - shared)
    hidden_load.wait()
    right_load.wait()
    cot_load.wait()
    gain_one, bias_one, gain_two, bias_two = gain_rows(full_ref, 4 * width, cfg.gate_columns)
    gain_sum = jnp.zeros((1, width), F32)
    bias_sum = jnp.zeros((1, width), F32)
    for c in range(count // chunk):
        span = slice(c * chunk, (c + 1) * chunk)
        column = iota_f((chunk, cfg.gate_lanes), 1)
        logits = jnp.where(column == side_ref[span, 2:3], chosen_one[span], 0.0) + jnp.where(
            column == side_ref[span, 3:4], chosen_two[span], 0.0
        )
        logits = logits.astype(BF16)
        logits_ref[span, :] = logits
        routed_grad = routed_sum[span, :] + contract_last(logits, full_ref[:, 4 * width :])
        unit, inverse = norm_parts(hidden_ref[span, :])
        routed_ref[span, :] = (unit * gain_two + bias_two).astype(BF16)
        gain_sum = gain_sum + row_sum(routed_grad * unit)
        bias_sum = bias_sum + row_sum(routed_grad)
        hidden_grad = cot_ref[span, :].astype(F32) + norm_back(unit, inverse, gain_two, routed_grad)
        routed_sum[span, :] = hidden_grad
        low = hidden_grad.astype(BF16)
        low_ref[span, :] = low
        heads_grad_ref[span, :] = contract_last(low, full_ref[:, 3 * width : 4 * width]).astype(BF16)
    heads_load.wait()
    kind = dense_ref.dtype
    dense_ref[:, 3 * width : 4 * width] = contract_first(heads_ref[...], low_ref[...]).astype(kind)
    dense_ref[:, 4 * width :] = contract_first(routed_ref[...], logits_ref[...]).astype(kind)
    tile = 4 * width + cfg.gate_columns // LANES * LANES
    lane = cfg.gate_columns % LANES
    tile = slice(tile, tile + LANES)
    dense_ref[:, tile] += rows_to_lanes(gain_sum, bias_sum, lane + 2).astype(kind)
    proj_load.wait()
    lane_row = iota((1, LANES), 1)
    scale = HEAD_DIM ** (-0.5)
    block = 256

    def slab(i, carry):
        off = pl.multiple_of(i * LANES, LANES)
        queries = proj_ref[:, pl.ds(off, LANES)] * jnp.asarray(scale, BF16)
        keys = proj_ref[:, pl.ds(width + off, LANES)]
        values = proj_ref[:, pl.ds(2 * width + off, LANES)]
        grads = heads_grad_ref[:, pl.ds(off, LANES)]
        query_grad = [jnp.zeros((block, LANES), F32)] * (count // block)
        key_grad = jnp.zeros((count, LANES), F32)
        value_grad = jnp.zeros((count, LANES), F32)
        for half in (0, 1):
            part = jnp.where(lane_row // HEAD_DIM == half, 1.0, 0.0).astype(BF16)
            query_half, key_half, grads_half = queries * part, keys * part, grads * part
            logs = lse_ref[pl.ds(2 * i + half, 1), :]
            for q in range(count // block):
                span = slice(q * block, (q + 1) * block)
                scores = contract_last(key_half, queries[span]) + bias_ref[:, span] - logs[:, span]
                probs = jnp.exp(scores)
                prob_grad = contract_last(values, grads_half[span])
                score_grad = (probs * (prob_grad - row_sum(probs * prob_grad))).astype(BF16)
                value_grad = value_grad + mm(probs.astype(BF16), grads_half[span])
                key_grad = key_grad + mm(score_grad, query_half[span])
                query_grad[q] = query_grad[q] + contract_first(score_grad, key_half)
        for q in range(count // block):
            qkv_ref[q * block : (q + 1) * block, pl.ds(off, LANES)] = (query_grad[q] * scale).astype(BF16)
        qkv_ref[:, pl.ds(width + off, LANES)] = key_grad.astype(BF16)
        qkv_ref[:, pl.ds(2 * width + off, LANES)] = value_grad.astype(BF16)
        return carry

    lax.fori_loop(0, width // LANES, slab, 0)
    tokens_load.wait()
    left_load.wait()
    gain_sum = jnp.zeros((1, width), F32)
    bias_sum = jnp.zeros((1, width), F32)
    for c in range(count // chunk):
        span = slice(c * chunk, (c + 1) * chunk)
        normed_grad = contract_last(qkv_ref[span, :], full_ref[:, left])
        unit, inverse = norm_parts(tokens_ref[span, :].astype(F32))
        low_ref[span, :] = (unit * gain_one + bias_one).astype(BF16)
        gain_sum = gain_sum + row_sum(normed_grad * unit)
        bias_sum = bias_sum + row_sum(normed_grad)
        grad_all[span, :] = routed_sum[span, :] + norm_back(unit, inverse, gain_one, normed_grad)
        stores.start(grad_all.at[span], grad_ref.at[span])
    turned_ref[...] = jnp.transpose(low_ref[...])
    dense_ref[:, tile] += rows_to_lanes(gain_sum, bias_sum, lane).astype(kind)
    owners = [mask for masks in cfg.owners for mask in masks]
    rows = width // len(owners)
    for c in range(width // chunk):
        span = slice(c * chunk, (c + 1) * chunk)
        dense_ref[span, left] = mm(turned_ref[span, :], qkv_ref[...]).astype(kind)
    if len(dense_outs) == 1:
        stores.start(dense_ref, dense_outs[0])
    else:
        for at, mask in enumerate(owners):
            half = at * 2 // len(owners)
            to = (at - half * len(owners) // 2) * rows
            source = pl.multiple_of((me ^ mask) * rows, rows)
            stores.start(dense_ref.at[pl.ds(source, rows)], dense_outs[half].at[to : to + rows])
    stores.finish()


def output_kernel(cfg, side_ref, hidden_ref, result_ref, out_ref):
    count, width = hidden_ref.shape
    slot = iota_f((count, cfg.experts * cfg.cap), 1)
    pick = (slot == side_ref[:, 0:1]) | (slot == side_ref[:, 1:2])
    mixed = mm(jnp.where(pick, 1.0, 0.0).astype(BF16), result_ref[...])
    out_ref[...] = (hidden_ref[...] + mixed).astype(BF16)


class Config:
    pass


def after(value, other):
    return lax.optimization_barrier((value, other))[0]


def apart(always, part, *args):
    given = jax.eval_shape(part, *args)

    def never(*_):
        return jax.tree.map(lambda s: jnp.zeros(s.shape, s.dtype), given)

    return lax.cond(always, part, never, *args)


def swap_hidden(value, mask):
    size = lax.axis_size("hidden")
    return lax.ppermute(value, "hidden", [(i, i ^ mask) for i in range(size)])


def swap_expert(value, mask):
    size = lax.axis_size("expert")
    return lax.ppermute(value, "expert", [(i, i ^ mask) for i in range(size)])


def gather_rest(own):
    blocks = [own]
    bit = 2
    while bit < lax.axis_size("hidden"):
        blocks += [swap_hidden(block, bit) for block in blocks]
        bit *= 2
    return blocks


def gather_core(half):
    return [swap_hidden(block, 1) for block in half]


def in_turn(first, second):
    return [block for pair in zip(first, second) for block in pair]


def sum_rest(blocks):
    held = {i + 2: [b] for i, b in enumerate(blocks)}
    low = {i: v + [swap_hidden(held[i + 1][0], 1)] for i, v in held.items() if not i & 1}
    held = {0: [], **low}
    bit = 2
    while bit < len(blocks) + 2:
        low = {i: v for i, v in held.items() if not i & bit}
        for i in low:
            value = functools.reduce(jnp.add, held[i ^ bit])
            if 2 * bit == len(blocks) + 2:
                return low[0], value
            low[i] = low[i] + [swap_hidden(value, bit)]
        held = low
        bit *= 2


def body(
    tokens,
    lengths,
    task_ids,
    routes,
    w_qkv,
    w_attn_out,
    w_gate,
    ln1_gain,
    ln1_bias,
    ln2_gain,
    ln2_bias,
    w_in,
    w_out,
    cotangent,
):
    count, width = tokens.shape
    cfg = Config()
    cfg.experts = lax.axis_size("expert")
    cfg.hidden = lax.axis_size("hidden")
    experts, hidden = cfg.experts, cfg.hidden
    cfg.cap = cap = (3 * count * routes.shape[1] + 2 * experts - 1) // (2 * experts)
    cfg.gate_columns = w_gate.shape[1]
    cfg.gate_lanes = round_up(cfg.gate_columns + 4, LANES)
    devices = experts * hidden
    groups = Groups(devices)
    shard_rows = w_qkv.shape[0]
    staged = shard_rows % 16 == 0
    cfg.owners = groups.owners()
    me = (lax.axis_index("expert") * hidden + lax.axis_index("hidden")).astype(jnp.int32)[None]
    extra = 16
    units = w_in.shape[2]
    slots = experts * cap
    wide = 4 * width + cfg.gate_lanes
    one_dot = 2 * count * width * width

    packed = call(
        pack_kernel,
        shape((shard_rows, wide), BF16),
        [],
        [w_qkv, w_attn_out, w_gate]
        + [v.reshape(1, shard_rows) for v in (ln1_gain, ln1_bias, ln2_gain, ln2_bias)],
        1,
    )
    always = lengths[0, 0] > 0

    def first_part(packed, lengths, task_ids, routes, cotangent):
        far = groups.gather_far(packed) if staged else packed
        made = call(
            functools.partial(prep_kernel, cfg),
            [
                shape((count, LANES), F32),
                shape((8, count), F32),
                shape((experts // 2, 2, cap, width), BF16),
            ],
            [
                pltpu.VMEM((count, width), BF16),
                pltpu.VMEM((count, LANES), F32),
                pltpu.VMEM((8, count), F32),
                pltpu.VMEM((experts // 2, 2, cap, width), BF16),
                pltpu.SemaphoreType.DMA((1,)),
                pltpu.SemaphoreType.DMA((2 + experts,)),
            ],
            [lengths, task_ids, routes, cotangent],
            3 * one_dot,
            far_in=(3,),
            far_out=(0, 1, 2),
        )
        return far, made

    dense_far, (side, rows, sent_cot) = apart(
        always, first_part, packed, lengths, task_ids, routes.T, cotangent
    )
    if staged:
        dense_blocks = groups.gather_near(dense_far)
        reached = dense_blocks[1 : len(groups.mid)]
    else:
        dense_blocks = [lax.all_gather(packed, BOTH, axis=0, tiled=True)]
        reached = dense_blocks[0]
    cfg.blocks = len(dense_blocks)
    parity = [list(range(i, experts, 2)) for i in (0, 1)]

    def exchange_even(value):
        return lax.all_to_all(
            value, "expert", split_axis=0, concat_axis=0, axis_index_groups=parity, tiled=True
        )

    def exchange_odd(values):
        return [swap_expert(value, 2 * i + 1) for i, value in enumerate(values)]

    cot_even = exchange_even(sent_cot)
    other = 1 - lax.axis_index("expert") % 2
    cot_odd = lax.dynamic_index_in_dim(cot_even, other, 1, keepdims=False)
    in_half = gather_rest(after(w_in[0], reached))

    outs = call(
        functools.partial(forward_kernel, cfg),
        [
            shape((width, wide), BF16),
            shape((count, 3 * width), BF16),
            shape((count, width), BF16),
            shape((HEADS, count), F32),
            shape((count, width), F32),
            shape((count, LANES), F32),
        ]
        + [shape((experts // 2, cap + extra, width), BF16)]
        + [shape((cap + extra, width), BF16)] * (experts // 2),
        [
            pltpu.VMEM((width, wide), BF16),
            pltpu.VMEM((count, 3 * width), BF16),
            pltpu.VMEM((count, width), BF16),
            pltpu.VMEM((HEADS, count), F32),
            pltpu.VMEM((count, width), F32),
            pltpu.VMEM((count, LANES), F32),
            pltpu.VMEM((experts, extra, width), BF16),
            pltpu.VMEM((slots, width), BF16),
            pltpu.VMEM((slots, count), BF16),
            pltpu.VMEM((count, count), F32),
            pltpu.VMEM((count, width), BF16),
            pltpu.VMEM((count, LANES), F32),
            pltpu.SemaphoreType.DMA((devices,)),
            pltpu.SemaphoreType.DMA((6 + 2 * experts,)),
        ],
        [me, side, rows, tokens] + dense_blocks,
        12 * one_dot,
        smem=(0,),
        far_in=range(4, 4 + cfg.blocks),
        far_out=range(7 + experts // 2),
    )
    full, proj, heads, lse, hidden_one, gates = outs[:6]
    send_rows = outs[6:]
    def even_part(even_send, odd_send, cot_even, cot_odd, in_half, own_out):
        out_half = gather_rest(own_out)
        more_in, more_out = gather_core(in_half), gather_core(out_half)
        blocks = in_turn(in_half, more_in) + in_turn(out_half, more_out)
        even_rows = exchange_even(even_send)
        odd_rows = exchange_odd(odd_send)
        cot_odd = swap_expert(cot_odd, 1)
        out = expert_part(cfg, 0, me, cot_even, [even_rows], blocks, [])
        return even_rows, odd_rows, cot_odd, more_in, out_half[1:], more_out, out

    def odd_part(even_send, even_rows, odd_rows, cot_odd, in_blocks, out_blocks, before, even_pairs):
        even_back = exchange_even(even_send)
        blocks = in_blocks + out_blocks
        result, sends, pairs = expert_part(cfg, 1, me, cot_odd, odd_rows, blocks, [before])
        odd_back = exchange_odd(sends)
        sums = apart(always, far_weights, even_rows, odd_rows, [even_pairs, pairs], in_blocks, out_blocks)
        return [even_back] + odd_back, result, pairs, *sums

    def far_weights(even_rows, odd_rows, pairs, in_blocks, out_blocks):
        picked = [b for b in range(hidden) if b > 1]
        return sum_rest(
            weight_part(cfg, picked, me, even_rows, odd_rows, pairs, in_blocks, out_blocks)
        )

    def own_weights(even_rows, odd_rows, pairs, in_blocks, out_blocks):
        return weight_part(cfg, [0, 1], me, even_rows, odd_rows, pairs, in_blocks, out_blocks)

    even_rows, odd_rows, cot_odd, more_in, rest_out, more_out, even_out = apart(
        always, even_part, send_rows[0], send_rows[1:], cot_even, cot_odd, in_half, w_out[0]
    )
    out_half = [w_out[0]] + rest_out
    in_blocks, out_blocks = in_turn(in_half, more_in), in_turn(out_half, more_out)
    back, result, odd_pairs, held, value = apart(
        always,
        odd_part,
        even_out[1][0],
        even_rows,
        odd_rows,
        cot_odd,
        in_blocks,
        out_blocks,
        even_out[0],
        even_out[2],
    )
    pairs = [even_out[2], odd_pairs]
    returned = lax.all_to_all(
        after(result, back), "expert", split_axis=0, concat_axis=0, tiled=True
    )
    if staged:
        dense_shapes = [shape((width // 2, wide), BF16)] * 2
    else:
        dense_shapes = [shape((width, wide), F32)]
    cfg.dense_outs = len(dense_shapes)

    def back_part(value, back):
        args = [me, side, rows, gates, lse] + back + [hidden_one, cotangent, heads, tokens, proj, full]
        outs = call(
            functools.partial(backward_kernel, cfg),
            [shape((count, width), F32)] + dense_shapes,
            [
                pltpu.VMEM((slots, width), BF16),
                pltpu.VMEM((experts, extra, width), BF16),
                pltpu.VMEM((count, width), F32),
                pltpu.VMEM((count, width), BF16),
                pltpu.VMEM((count, width), BF16),
                pltpu.VMEM((count, width), BF16),
                pltpu.VMEM((count, 3 * width), BF16),
                pltpu.VMEM((width, wide), BF16),
                pltpu.VMEM((count, width), F32),
                pltpu.VMEM((count, width), BF16),
                pltpu.VMEM((count, cfg.gate_lanes), BF16),
                pltpu.VMEM((count, width), BF16),
                pltpu.VMEM((count, width), BF16),
                pltpu.VMEM((count, count), F32),
                pltpu.VMEM((count, 3 * width), BF16),
                pltpu.VMEM((width, count), BF16),
                pltpu.VMEM((width, wide), dense_shapes[0].dtype),
                pltpu.VMEM((count, width), F32),
                pltpu.SemaphoreType.DMA((2 * experts + 7,)),
                pltpu.SemaphoreType.DMA((4 + devices,)),
            ],
            args,
            19 * one_dot,
            smem=(0,),
            far_in=range(5, len(args)),
            far_out=range(1 + len(dense_shapes)),
        )
        return swap_hidden(value, hidden // 2), outs

    last, outs = apart(always, back_part, value, back)
    reached = held + [last]
    grad_tokens = outs[0]

    def last_weights(blocks):
        got = [groups.swap(b, m) for b, m in zip(blocks[1:], groups.mid[1:])]
        return got, own_weights(even_rows, odd_rows, pairs, in_blocks, out_blocks)

    def last_sums(blocks, own, more, reached, returned):
        layer_out = call(
            functools.partial(output_kernel, cfg),
            shape((count, width), BF16),
            [],
            [side, hidden_one, returned.reshape(slots, width)],
            6 * one_dot,
        )
        got = [groups.swap(b, m) for b, m in zip(blocks[1:], groups.far[1:])]
        terms = [own, swap_hidden(more, 1)] + reached
        grad_in, grad_out = call(
            turn_add_kernel,
            [shape((width, units), F32), shape((units, width), F32)],
            [],
            terms,
            4 * width * units,
            limit=2 * SMALL_LIMIT,
        )
        return got, grad_in, grad_out, layer_out

    blocks = [None]
    if staged:
        blocks = add_parts(outs[1], [groups.swap(outs[2], 1)], len(groups.mid))
    got, (own, more) = apart(always, last_weights, blocks)
    if staged:
        blocks = add_parts(blocks[0], got, len(groups.far))
    got, grad_in, grad_out, layer_out = apart(
        always, last_sums, blocks, own, more, reached, returned
    )
    if staged:
        dense_terms = blocks[:1] + got
    else:
        dense_terms = [lax.psum_scatter(outs[1], BOTH, scatter_dimension=0, tiled=True)]
    dense_outs = call(
        functools.partial(split_kernel, cfg),
        [shape((shard_rows, c), F32) for c in (3 * width, width, cfg.gate_columns)]
        + [shape((1, shard_rows), F32)] * 4,
        [],
        dense_terms,
        shard_rows * wide,
        limit=SMALL_LIMIT,
    )

    return (
        layer_out,
        grad_tokens,
        *dense_outs[:3],
        *[v.reshape(shard_rows) for v in dense_outs[3:]],
        grad_in[None],
        grad_out[None],
    )


def solution(mesh):
    split = P(BOTH, None)
    vector = P(BOTH)
    placed = (split,) * 7 + (vector,) * 4 + (P("expert", None, "hidden"), P("expert", "hidden", None), split)
    return jax.shard_map(
        body,
        mesh=mesh,
        in_specs=placed,
        out_specs=(split,) * 5
        + (vector,) * 4
        + (P("expert", None, "hidden"), P("expert", "hidden", None)),
        check_vma=False,
    )
```

```python
import functools

import jax
import jax.numpy as jnp
from jax import lax
from jax.experimental import pallas as pl
from jax.experimental.pallas import tpu as pltpu
from jax.sharding import PartitionSpec as P

HEADS = 8
HEAD_DIM = 64
EPS = 1e-05
NEG_FILL = -1e30
LANES = 128
BOTH = ("expert", "hidden")
F32 = jnp.float32
BF16 = jnp.bfloat16
VMEM_LIMIT = 56 * 1024 * 1024
SMALL_LIMIT = 8 * 1024 * 1024


def mm(left, right):
    return jnp.dot(left, right, preferred_element_type=F32)


def contract_last(left, right):
    return lax.dot_general(left, right, (((1,), (1,)), ((), ())), preferred_element_type=F32)


def contract_first(left, right):
    return lax.dot_general(left, right, (((0,), (0,)), ((), ())), preferred_element_type=F32)


def iota(shape, axis):
    return lax.broadcasted_iota(jnp.int32, shape, axis)


def iota_f(shape, axis):
    return iota(shape, axis).astype(F32)


def lane_sum(values):
    return jnp.sum(values, axis=1, keepdims=True)


def row_sum(values):
    return jnp.sum(values, axis=0, keepdims=True)


def norm_parts(values):
    middle = jnp.mean(values, axis=-1, keepdims=True)
    centred = values - middle
    spread = jnp.mean(centred * centred, axis=-1, keepdims=True)
    inverse = lax.rsqrt(spread + EPS)
    return centred * inverse, inverse


def norm_back(unit, inverse, gain, grad):
    scaled = grad * gain
    mean_one = jnp.mean(scaled, axis=-1, keepdims=True)
    mean_two = jnp.mean(scaled * unit, axis=-1, keepdims=True)
    return inverse * (scaled - mean_one - unit * mean_two)


def round_up(value, step):
    return (value + step - 1) // step * step


def call(kernel, outs, scratch, args, flops, smem=(), far_in=(), far_out=(), limit=VMEM_LIMIT):
    def spec(at):
        space = pltpu.SMEM if at in smem else pl.ANY if at in far_in else pltpu.VMEM
        return pl.BlockSpec(memory_space=space)

    def out_spec(at):
        return pl.BlockSpec(memory_space=pl.ANY if at in far_out else pltpu.VMEM)

    touched = sum(a.size * a.dtype.itemsize for a in args) + sum(
        o.size * o.dtype.itemsize for o in jax.tree.leaves(outs)
    )
    got = pl.pallas_call(
        kernel,
        out_shape=outs,
        in_specs=[spec(at) for at in range(len(args))],
        out_specs=[out_spec(at) for at in range(len(outs))] if isinstance(outs, list) else out_spec(0),
        scratch_shapes=scratch,
        compiler_params=pltpu.CompilerParams(vmem_limit_bytes=limit),
        cost_estimate=pl.CostEstimate(flops=1, bytes_accessed=1, transcendentals=0),
    )(*args)
    return list(got) if isinstance(outs, list) else got


def shape(dims, dtype):
    return jax.ShapeDtypeStruct(dims, dtype)


def slot_targets(cfg, routes_ref):
    count, experts = routes_ref.shape[1], cfg.experts
    both = jnp.zeros((8, count), F32)
    for at in (0, 1):
        both = jnp.where(iota((8, count), 0) == at, routes_ref[at : at + 1, :].astype(F32), both)
    routes = jnp.transpose(both)
    first, second = routes[:, 0:1], routes[:, 1:2]
    lane_e = iota_f((count, experts), 1)
    hot_one = jnp.where(lane_e == first, 1.0, 0.0)
    hot_two = jnp.where(lane_e == second, 1.0, 0.0)
    before = jnp.where(iota((count, count), 1) < iota((count, count), 0), 1.0, 0.0).astype(BF16)
    earlier = mm(before, (hot_one + hot_two).astype(BF16))
    target_one = first * cfg.cap + lane_sum(earlier * hot_one)
    target_two = second * cfg.cap + lane_sum(earlier * hot_two)
    return first, second, target_one, target_two


def prep_kernel(cfg, lens_ref, tasks_ref, routes_ref, cot_in, side_out, rows_out, sent_out, *scratch):
    experts, cap = cfg.experts, cfg.cap
    cot_ref, side_ref, rows_ref, sent_ref, in_sems, out_sems = scratch
    loads, stores = Copies(in_sems), Copies(out_sems)
    loads.start(cot_in, cot_ref)
    count = routes_ref.shape[1]
    sents = lens_ref.shape[1]
    lens = lens_ref[...].astype(F32)
    tasks = tasks_ref[...].astype(F32)
    down, across = iota((sents, sents), 0), iota((sents, sents), 1)
    ends_col = lane_sum(jnp.where(across <= down, lens, 0.0))
    ends_row = row_sum(jnp.where(across == down, ends_col, 0.0))
    passed = jnp.where(iota_f((count, sents), 0) >= ends_row, 1.0, 0.0)
    sentence = lane_sum(passed)
    task = lane_sum(jnp.where(iota_f((count, sents), 1) == sentence, tasks, 0.0))
    lane = iota((count, LANES), 1)
    first, second, target_one, target_two = slot_targets(cfg, routes_ref)
    side = jnp.where(lane == 0, target_one, 0.0)
    side = jnp.where(lane == 1, target_two, side)
    side = jnp.where(lane == 2, task * experts + first, side)
    side = jnp.where(lane == 3, task * experts + second, side)
    side = jnp.where(lane == 4, sentence, side)
    side = jnp.where(lane == 5, first, side)
    side = jnp.where(lane == 6, second, side)
    side_ref[...] = side
    stores.start(side_ref, side_out)
    turned = jnp.transpose(side)
    rows_ref[...] = turned[0:8, :]
    stores.start(rows_ref, rows_out)
    one_row, two_row = turned[0:1, :], turned[1:2, :]
    loads.finish()
    cot = cot_ref[...]
    for e in range(experts):
        at = iota_f((cap, count), 0) + float(e * cap)
        pick = jnp.where((at == one_row) | (at == two_row), 1.0, 0.0).astype(BF16)
        sent_ref[e // 2, e % 2] = mm(pick, cot).astype(BF16)
        stores.start(sent_ref.at[e // 2, e % 2], sent_out.at[e // 2, e % 2])
    stores.finish()


def pack_kernel(qkv_ref, attn_ref, gate_ref, *refs):
    vector_refs, out_ref = refs[:4], refs[4]
    rows = out_ref.shape[0]
    at = 0
    for ref in (qkv_ref, attn_ref):
        out_ref[:, at : at + ref.shape[1]] = ref[...]
        at += ref.shape[1]
    columns = gate_ref.shape[1]
    lanes = out_ref.shape[1] - at
    tile = columns // LANES * LANES
    out_ref[:, at : at + columns] = gate_ref[...]
    eye = iota((rows, rows), 0) == iota((rows, rows), 1)
    lane = iota((rows, lanes - tile), 1)
    last = out_ref[:, at + tile :].astype(F32)
    last = jnp.where(lane < columns - tile, last, 0.0)
    for i in range(4):
        column = lane_sum(jnp.where(eye, vector_refs[i][...].astype(F32), 0.0))
        last = jnp.where(lane == columns - tile + i, column, last)
    out_ref[:, at + tile :] = last.astype(BF16)


class Groups:
    def __init__(self, devices):
        bits = devices.bit_length() - 1
        mid = (bits - 1) // 2
        self.near = [1]
        self.mid = self.masks(1, mid)
        self.far = self.masks(1 + mid, bits - 1 - mid)
        self.devices = devices

    @staticmethod
    def masks(low, width):
        return [m << low for m in range(1 << width)]

    def owners(self):
        return [[n | b | c for c in self.far] for n in (0, 1) for b in self.mid]

    def swap(self, value, mask):
        return lax.ppermute(value, BOTH, [(i, i ^ mask) for i in range(self.devices)])

    def gather_far(self, shard):
        return jnp.concatenate([shard] + [self.swap(shard, m) for m in self.far[1:]], axis=0)

    def gather_near(self, far):
        mid = [far] + [self.swap(far, m) for m in self.mid[1:]]
        return mid + [self.swap(block, 1) for block in mid]


def add_kernel(parts, keep_ref, *refs):
    got, outs = refs[: len(refs) - parts], refs[len(refs) - parts :]
    rows = outs[0].shape[0]
    for i, out_ref in enumerate(outs):
        span = slice(i * rows, (i + 1) * rows)
        total = keep_ref[span, :].astype(F32)
        for ref in got:
            total = total + ref[span, :].astype(F32)
        out_ref[...] = total.astype(out_ref.dtype)


def add_parts(keep, got, parts):
    rows, columns = keep.shape
    outs = [shape((rows // parts, columns), F32 if i == 0 else BF16) for i in range(parts)]
    return call(
        functools.partial(add_kernel, parts), outs, [], [keep] + got, rows * columns * len(got), limit=SMALL_LIMIT
    )


def split_kernel(cfg, *refs):
    terms, outs = refs[:-7], refs[-7:]
    rows, width = outs[0].shape[0], outs[1].shape[1]

    def total(start, stop):
        value = terms[0][:, start:stop]
        for ref in terms[1:]:
            value = value + ref[:, start:stop].astype(F32)
        return value

    outs[0][...] = total(0, 3 * width)
    outs[1][...] = total(3 * width, 4 * width)
    outs[2][...] = total(4 * width, 4 * width + cfg.gate_columns)
    tile = 4 * width + cfg.gate_columns // LANES * LANES
    lane = cfg.gate_columns % LANES
    turned = jnp.transpose(total(tile, tile + LANES))
    for i in range(4):
        outs[3 + i][...] = turned[lane + i : lane + i + 1, :]


def gain_rows(full_ref, start, gate_columns):
    tile = start + gate_columns // LANES * LANES
    lane = gate_columns % LANES
    turned = jnp.transpose(full_ref[:, tile : tile + LANES].astype(F32))
    return [turned[lane + i : lane + i + 1, :] for i in range(4)]


def forward_kernel(cfg, me_ref, side_ref, rows_ref, tokens_ref, *refs):
    n, cap = cfg.experts, cfg.cap
    blocks, refs = refs[: cfg.blocks], refs[cfg.blocks :]
    outs, refs = refs[:6], refs[6:]
    even_out, odd_outs, refs = refs[0], refs[1 : 1 + n // 2], refs[1 + n // 2 :]
    full_ref, proj_ref, heads_ref, turned_ref, hidden_ref, gates_ref, send_all = refs[:7]
    rows_all, pick_ref_all, bias_ref, routed_ref, lse_ref, in_sems, out_sems = refs[7:]
    count, width = tokens_ref.shape
    me = me_ref[0]
    mine = me // cfg.hidden
    loads, stores = Copies(in_sems), Copies(out_sems)
    if len(blocks) == 1:
        loads.start(blocks[0], full_ref)
    else:
        for block_ref, masks in zip(blocks, cfg.owners):
            rows = block_ref.shape[0] // len(masks)
            for i, mask in enumerate(masks):
                at = pl.multiple_of((me ^ mask) * rows, rows)
                loads.start(block_ref.at[i * rows : (i + 1) * rows], full_ref.at[pl.ds(at, rows)])
    chunk = 512
    for c in range(count // chunk):
        span = slice(c * chunk, (c + 1) * chunk)
        bias_ref[span, :] = jnp.where(side_ref[span, 4:5] == rows_ref[4:5, :], 0.0, NEG_FILL)
        hidden_ref[span, :], _ = norm_parts(tokens_ref[span, :].astype(F32))
    for k in range(n):
        at = iota_f((cap, count), 0) + ((mine ^ k) * cap).astype(F32)
        pick = (at == rows_ref[0:1, :]) | (at == rows_ref[1:2, :])
        pick_ref_all[k * cap : (k + 1) * cap, :] = jnp.where(pick, 1.0, 0.0).astype(BF16)
    loads.finish()
    stores.start(full_ref, outs[0])
    gain_one, bias_one, gain_two, bias_two = gain_rows(full_ref, 4 * width, cfg.gate_columns)
    for c in range(count // chunk):
        span = slice(c * chunk, (c + 1) * chunk)
        routed_ref[span, :] = (hidden_ref[span, :] * gain_one + bias_one).astype(BF16)
    proj_ref[...] = mm(routed_ref[...], full_ref[:, : 3 * width]).astype(BF16)
    stores.start(proj_ref, outs[1])
    lse_ref[...] = jnp.zeros_like(lse_ref)
    lane = iota((1, LANES), 1)
    scale = HEAD_DIM ** (-0.5)
    block = 256

    def slab(i, carry):
        off = i * LANES
        keys = proj_ref[:, pl.ds(width + off, LANES)]
        values = proj_ref[:, pl.ds(2 * width + off, LANES)]
        halves = []
        for half in (0, 1):
            mine = jnp.where(lane // HEAD_DIM == half, 1.0, 0.0).astype(BF16)
            halves.append((keys * mine, values * mine))
        for r in range(count // block):
            span = slice(r * block, (r + 1) * block)
            queries = proj_ref[span, pl.ds(off, LANES)]
            total = jnp.zeros((block, LANES), F32)
            logs = lse_ref[span, :]
            for half, (key_half, value_half) in enumerate(halves):
                scores = contract_last(queries, key_half) * scale + bias_ref[span, :]
                highest = jnp.max(scores, axis=1, keepdims=True)
                expo = jnp.exp(scores - highest)
                sums = lane_sum(expo)
                probs = (expo * (1.0 / sums)).astype(BF16)
                total = total + mm(probs, value_half)
                logs = jnp.where(lane == 2 * i + half, highest + jnp.log(sums), logs)
            heads_ref[span, pl.ds(off, LANES)] = total.astype(BF16)
            lse_ref[span, :] = logs
        return carry

    for i in range(width // LANES):
        slab(i, 0)
    stores.start(heads_ref, outs[2])
    turned_ref[...] = jnp.transpose(lse_ref[...])[:HEADS, :]
    stores.start(turned_ref, outs[3])
    for c in range(count // chunk):
        span = slice(c * chunk, (c + 1) * chunk)
        attended = mm(heads_ref[span, :], full_ref[:, 3 * width : 4 * width])
        hidden = tokens_ref[span, :].astype(F32) + attended
        hidden_ref[span, :] = hidden
        unit, _ = norm_parts(hidden)
        routed = (unit * gain_two + bias_two).astype(BF16)
        routed_ref[span, :] = routed
        logits = mm(routed, full_ref[:, 4 * width :])
        column = iota_f(logits.shape, 1)
        one = lane_sum(jnp.where(column == side_ref[span, 2:3], logits, 0.0))
        two = lane_sum(jnp.where(column == side_ref[span, 3:4], logits, 0.0))
        top = jnp.maximum(one, two)
        expo_one, expo_two = jnp.exp(one - top), jnp.exp(two - top)
        both = expo_one + expo_two
        gates_ref[span, :] = jnp.where(
            lane == 0, expo_one / both, jnp.where(lane == 1, expo_two / both, 0.0)
        )
    stores.start(hidden_ref, outs[4])
    stores.start(gates_ref, outs[5])
    gate_lanes = round_up(cap, LANES)
    rows_all[...] = mm(pick_ref_all[...], routed_ref[...]).astype(BF16)
    for k in range(n):
        base = ((mine ^ k) * cap).astype(F32)
        out_ref = pick_ref(mine, k, even_out, odd_outs)
        stores.start(rows_all.at[k * cap : (k + 1) * cap], out_ref.at[0:cap])
        slot = iota_f((count, gate_lanes), 1) + base
        row = row_sum(
            jnp.where(slot == side_ref[:, 0:1], gates_ref[:, 0:1], 0.0)
            + jnp.where(slot == side_ref[:, 1:2], gates_ref[:, 1:2], 0.0)
        )
        put_split(send_all.at[k], 0, row)
        stores.start(send_all.at[k], out_ref.at[cap : cap + send_all.shape[1]])
    stores.finish()


def pick_ref(mine, k, even_ref, odd_refs):
    return odd_refs[k // 2] if k % 2 else even_ref.at[(mine ^ k) // 2]


def put_split(ref, cap, row):
    extra = ref.shape[0] - cap
    high = row.astype(BF16).astype(F32)
    down = iota((extra, row.shape[1]), 0)
    both = jnp.where(down == 0, high, jnp.where(down == 1, row - high, 0.0))
    ref[cap:, :] = jnp.zeros((extra, ref.shape[1]), BF16)
    ref[cap:, 0 : row.shape[1]] = both.astype(BF16)


def take_split(ref, cap, lanes):
    both = ref[cap:, 0:lanes].astype(F32)
    return both[0:1, :] + both[1:2, :]


def gelu_parts(pre):
    root = 0.7978845608028654
    cubic = 0.044715
    square = pre * pre
    upper = 0.5 + 0.5 * jnp.tanh(pre * (root + (root * cubic) * square))
    act = pre * upper
    return act, upper + act * (1.0 - upper) * (2.0 * root + (6.0 * root * cubic) * square)


class Copies:
    def __init__(self, sems):
        self.sems, self.count, self.open = sems, 0, []

    def start(self, source, target, kept=True):
        copy = pltpu.make_async_copy(source, target, self.sems.at[self.count])
        self.count += 1
        copy.start()
        if kept:
            self.open.append(copy)
        return copy

    def finish(self):
        for copy in self.open:
            copy.wait()


def expert_kernel(cfg, odd, me_ref, *refs):
    h, cap, n = cfg.hidden, cfg.cap, cfg.experts // 2
    many = n if odd else 1
    cot_ref, refs = refs[0], refs[1:]
    row_refs, refs = refs[:many], refs[many:]
    in_refs, out_refs, refs = refs[:h], refs[h : 2 * h], refs[2 * h :]
    if odd:
        before_ref, refs = refs[0], refs[1:]
    result_ref, back_refs, refs = refs[0], refs[1 : 1 + many], refs[1 + many :]
    pairs_ref, refs = refs[0], refs[1:]
    rows_all, cot_all, pairs_all, result_all, back_all, before_all, extra_in, extra_out = refs[:8]
    result_sum, back_sum, weights_all, in_sems, out_sems = refs[8:]
    total, width = rows_all.shape
    extra = extra_in.shape[1]
    mine = me_ref[0] // h
    loads, stores = Copies(in_sems), Copies(out_sems)
    ks = list(range(odd, 2 * n, 2))
    tiles = 2
    per = n // tiles
    tile = per * cap
    row_loads, weight_loads = [], []

    def load_rows(m):
        for i in range(m * per, (m + 1) * per):
            span = slice(i * cap, (i + 1) * cap)
            source = (mine ^ ks[i]) // 2
            row_ref = pick_ref(mine, ks[i], row_refs[0], row_refs)
            from_ref = cot_ref.at[source] if odd else cot_ref.at[source, mine % 2]
            row_loads.append(
                (
                    loads.start(row_ref.at[0:cap], rows_all.at[span], False),
                    loads.start(row_ref.at[cap : cap + extra], extra_in.at[i], False),
                    loads.start(from_ref, cot_all.at[span], False),
                )
            )

    load_rows(0)
    for i, ref in enumerate(in_turn(in_refs, out_refs)):
        held = weights_all.at[i, : ref.shape[0], : ref.shape[1]]
        weight_loads.append(loads.start(ref, held, False))
    for m in range(1, tiles):
        load_rows(m)
    if odd:
        before_loads = [loads.start(before_ref.at[i], before_all.at[i], False) for i in range(n)]
    gate_lanes = round_up(cap, LANES)
    eye = iota((cap, gate_lanes), 0) == iota((cap, gate_lanes), 1)
    units = in_refs[0].shape[1]
    gates = {}
    for m in range(tiles):
        span = slice(m * tile, (m + 1) * tile)
        for i in range(m * per, (m + 1) * per):
            for copy in row_loads[i]:
                copy.wait()
            rows = slice(i * cap, (i + 1) * cap)
            gates[i] = lane_sum(jnp.where(eye, take_split(extra_in.at[i], 0, gate_lanes), 0.0))
            pairs_all[rows, :] = (gates[i] * cot_all[rows, :].astype(F32)).astype(BF16)
        stores.start(pairs_all.at[span], pairs_ref.at[span])
        for b in range(h):
            if m == 0:
                weight_loads[2 * b].wait()
                weight_loads[2 * b + 1].wait()
            w_in, w_out = weights_all.at[2 * b, :, :units], weights_all.at[2 * b + 1, :units, :]
            act, slope = gelu_parts(mm(rows_all[span, :], w_in[...]))
            act_low = act.astype(BF16)
            act_grad = contract_last(pairs_all[span, :], w_out[...])
            pre_grad = (act_grad * slope).astype(BF16)
            result = mm(act_low, w_out[...])
            back = contract_last(pre_grad, w_in[...])
            if b == 0:
                result_sum[...] = result
                back_sum[...] = back
            elif b < h - 1:
                result_sum[...] += result
                back_sum[...] += back
            else:
                result_sum[...] += result
                back_all[span, :] = (back_sum[...] + back).astype(BF16)
        if odd and m == 0:
            for i in range(n):
                before_loads[i].wait()
                stores.start(before_all.at[i], result_ref.at[mine ^ (2 * i)])
        for i in range(m * per, (m + 1) * per):
            rows, k = slice(i * cap, (i + 1) * cap), ks[i]
            back_ref = pick_ref(mine, k, back_refs[0], back_refs)
            stores.start(back_all.at[rows], back_ref.at[0:cap])
            result = result_sum[(i - m * per) * cap : (i - m * per + 1) * cap, :]
            result_all[rows, :] = (gates[i] * result).astype(BF16)
            stores.start(result_all.at[rows], result_ref.at[mine ^ k if odd else i])
            dots = lane_sum(cot_all[rows, :].astype(F32) * result)
            put_split(extra_out.at[i], 0, row_sum(jnp.where(eye, dots, 0.0)))
            stores.start(extra_out.at[i], back_ref.at[cap : cap + extra])
    stores.finish()


def expert_part(cfg, odd, me, cot, rows, weights, before):
    n, h, cap, extra = cfg.experts // 2, cfg.hidden, cfg.cap, 16
    width, units = cot.shape[-1], weights[0].shape[1]
    slots = n * cap
    many = len(rows)
    side = max(width, units)
    args = [me, cot] + rows + weights + before
    outs = (
        [shape((2 * n if odd else n, cap, width), BF16)]
        + [shape(r.shape, BF16) for r in rows]
        + [shape((slots, width), BF16)]
    )
    outs = call(
        functools.partial(expert_kernel, cfg, odd),
        outs,
        [pltpu.VMEM((slots, width), BF16)] * 5
        + [pltpu.VMEM((n, cap, width), BF16)]
        + [pltpu.VMEM((n, extra, width), BF16)] * 2
        + [pltpu.VMEM((slots // 2, width), F32)] * 2
        + [pltpu.VMEM((2 * h, side, side), BF16)]
        + [pltpu.SemaphoreType.DMA((4 * n + 2 * h,)), pltpu.SemaphoreType.DMA((4 * n + 2,))],
        args,
        8 * slots * width * units * h,
        smem=(0,),
        far_in=range(1, len(args)),
        far_out=range(len(outs)),
    )
    return outs[0], outs[1 : 1 + many], outs[1 + many]


def weight_kernel(cfg, parts, me_ref, *refs):
    n, cap = cfg.experts, cfg.cap
    even_ref, odd_refs, refs = refs[0], refs[1 : 1 + n // 2], refs[1 + n // 2 :]
    pair_refs, in_refs, out_refs, refs = refs[:2], refs[2 : 2 + parts], refs[2 + parts : 2 + 2 * parts], refs[2 + 2 * parts :]
    grad_refs, refs = refs[:parts], refs[parts:]
    grads_all, refs = refs[:parts], refs[parts:]
    rows_all, pairs_all, rows_turned, pairs_turned, act_all, pre_all, weights_all, in_sems, out_sems = refs
    total, width = rows_all.shape
    half = total // 2
    units = act_all.shape[1]
    mine = me_ref[0] // cfg.hidden
    loads, stores = Copies(in_sems), Copies(out_sems)
    waits = {0: [], 1: []}
    weight_loads = []
    for odd in (0, 1):
        for i in range(n // 2):
            k = 2 * i + odd
            span = slice(odd * half + i * cap, odd * half + (i + 1) * cap)
            row_ref = pick_ref(mine, k, even_ref, odd_refs)
            waits[odd].append(loads.start(row_ref.at[0:cap], rows_all.at[span], False))
        span = slice(odd * half, (odd + 1) * half)
        waits[odd].append(loads.start(pair_refs[odd], pairs_all.at[span], False))
        if not odd:
            for i, ref in enumerate(in_turn(in_refs, out_refs)):
                held = weights_all.at[i, : ref.shape[0], : ref.shape[1]]
                weight_loads.append(loads.start(ref, held, False))
    tile = half // 2
    for p in range(parts):
        weight_loads[2 * p].wait()
        weight_loads[2 * p + 1].wait()
        w_in, w_out = weights_all.at[2 * p, :, :units], weights_all.at[2 * p + 1, :units, :]
        for m in range(4):
            if p == 0 and m % 2 == 0:
                for copy in waits[m // 2]:
                    copy.wait()
                span = slice(m // 2 * half, (m // 2 + 1) * half)
                rows_turned[:, span] = jnp.transpose(rows_all[span, :])
                pairs_turned[:, span] = jnp.transpose(pairs_all[span, :])
            span = slice(m * tile, (m + 1) * tile)
            act, slope = gelu_parts(mm(rows_all[span, :], w_in[...]))
            act_all[span, :] = act.astype(BF16)
            act_grad = contract_last(pairs_all[span, :], w_out[...])
            pre_all[span, :] = (act_grad * slope).astype(BF16)
        kept = grads_all[p]
        kept[:width, :] = mm(rows_turned[...], pre_all[...]).astype(kept.dtype)
        kept[width:, :] = mm(pairs_turned[...], act_all[...]).astype(kept.dtype)
        stores.start(kept, grad_refs[p])
    stores.finish()


def weight_part(cfg, picked, me, even_rows, odd_rows, pairs, ins, outs):
    width, units = ins[0].shape
    slots, parts = cfg.experts * cfg.cap, len(picked)
    args = [me, even_rows] + odd_rows + pairs + [ins[b] for b in picked] + [outs[b] for b in picked]
    kinds = [BF16 if b else F32 for b in picked]
    side = max(width, units)
    return call(
        functools.partial(weight_kernel, cfg, parts),
        [shape((2 * width, units), kind) for kind in kinds],
        [pltpu.VMEM((2 * width, units), kind) for kind in kinds]
        + [pltpu.VMEM((slots, width), BF16)] * 2
        + [pltpu.VMEM((width, slots), BF16)] * 2
        + [pltpu.VMEM((slots, units), BF16)] * 2
        + [pltpu.VMEM((2 * parts, side, side), BF16)]
        + [pltpu.SemaphoreType.DMA((cfg.experts + 2 + 2 * parts,)), pltpu.SemaphoreType.DMA((parts,))],
        args,
        8 * slots * width * units * parts,
        smem=(0,),
        far_in=range(1, len(args)),
        far_out=range(parts),
    )


def turn_add_kernel(*refs):
    terms, (sum_in, sum_out) = refs[:-2], refs[-2:]
    width = sum_in.shape[0]
    total = terms[0][...]
    for ref in terms[1:]:
        total = total + ref[...].astype(F32)
    sum_in[...] = total[:width, :]
    sum_out[...] = jnp.transpose(total[width:, :])


def rows_to_lanes(first, second, lane):
    down = iota((LANES, first.shape[1]), 0)
    return jnp.transpose(jnp.where(down == lane, first, jnp.where(down == lane + 1, second, 0.0)))


def backward_kernel(cfg, me_ref, side_ref, rows_ref, gates_ref, lse_ref, *refs):
    n, cap = cfg.experts, cfg.cap
    even_ref, odd_refs, refs = refs[0], refs[1 : 1 + n // 2], refs[1 + n // 2 :]
    hidden_in, cot_in, heads_in, tokens_in, proj_in, full_in, refs = *refs[:6], refs[6:]
    grad_ref, dense_outs, refs = refs[0], refs[1 : 1 + cfg.dense_outs], refs[1 + cfg.dense_outs :]
    back_all, extra_all, hidden_ref, cot_ref, heads_ref, tokens_ref, proj_ref, full_ref = refs[:8]
    routed_sum, routed_ref, logits_ref, low_ref, heads_grad_ref, bias_ref, qkv_ref = refs[8:15]
    turned_ref, dense_ref, grad_all, in_sems, out_sems = refs[15:]
    count, width = hidden_ref.shape
    extra = extra_all.shape[1]
    me = me_ref[0]
    mine = me // cfg.hidden
    loads, stores = Copies(in_sems), Copies(out_sems)
    back_loads = []
    for k in range(n):
        ref = pick_ref(mine, k, even_ref, odd_refs)
        span = slice(k * cap, (k + 1) * cap)
        back_loads.append(loads.start(ref.at[0:cap], back_all.at[span], False))
        back_loads.append(loads.start(ref.at[cap : cap + extra], extra_all.at[k], False))
    hidden_load = loads.start(hidden_in, hidden_ref, False)
    right = slice(3 * width, full_ref.shape[1])
    left = slice(0, 3 * width)
    right_load = loads.start(full_in.at[:, right], full_ref.at[:, right], False)
    cot_load = loads.start(cot_in, cot_ref, False)
    heads_load = loads.start(heads_in, heads_ref, False)
    proj_load = loads.start(proj_in, proj_ref, False)
    tokens_load = loads.start(tokens_in, tokens_ref, False)
    left_load = loads.start(full_in.at[:, left], full_ref.at[:, left], False)

    def relative(at):
        expert = side_ref[:, 5 + at : 6 + at]
        turned = (expert.astype(jnp.int32) ^ mine).astype(F32)
        return side_ref[:, at : at + 1] + (turned - expert) * cap

    one, two = relative(0), relative(1)
    slot = iota_f((count, n * cap), 1)
    pick = jnp.where((slot == one) | (slot == two), 1.0, 0.0).astype(BF16)
    chunk = 512
    for c in range(count // chunk):
        span = slice(c * chunk, (c + 1) * chunk)
        bias_ref[span, :] = jnp.where(side_ref[span, 4:5] == rows_ref[4:5, :], 0.0, NEG_FILL)
    for copy in back_loads:
        copy.wait()
    routed_sum[...] = mm(pick, back_all[...])
    gate_lanes = round_up(cap, LANES)
    dots_one = jnp.zeros((count, gate_lanes), F32)
    dots_two = jnp.zeros((count, gate_lanes), F32)
    lane_at = iota_f((count, gate_lanes), 1)
    for k in range(n):
        slot = jnp.where(lane_at < cap, lane_at + float(k * cap), -1.0)
        dots = take_split(extra_all.at[k], 0, gate_lanes)
        dots_one = dots_one + jnp.where(slot == one, dots, 0.0)
        dots_two = dots_two + jnp.where(slot == two, dots, 0.0)
    dot_one, dot_two = lane_sum(dots_one), lane_sum(dots_two)
    gate_one, gate_two = gates_ref[:, 0:1], gates_ref[:, 1:2]
    shared = gate_one * dot_one + gate_two * dot_two
    chosen_one = gate_one * (dot_one - shared)
    chosen_two = gate_two * (dot_two - shared)
    hidden_load.wait()
    right_load.wait()
    cot_load.wait()
    gain_one, bias_one, gain_two, bias_two = gain_rows(full_ref, 4 * width, cfg.gate_columns)
    gain_sum = jnp.zeros((1, width), F32)
    bias_sum = jnp.zeros((1, width), F32)
    for c in range(count // chunk):
        span = slice(c * chunk, (c + 1) * chunk)
        column = iota_f((chunk, cfg.gate_lanes), 1)
        logits = jnp.where(column == side_ref[span, 2:3], chosen_one[span], 0.0) + jnp.where(
            column == side_ref[span, 3:4], chosen_two[span], 0.0
        )
        logits = logits.astype(BF16)
        logits_ref[span, :] = logits
        routed_grad = routed_sum[span, :] + contract_last(logits, full_ref[:, 4 * width :])
        unit, inverse = norm_parts(hidden_ref[span, :])
        routed_ref[span, :] = (unit * gain_two + bias_two).astype(BF16)
        gain_sum = gain_sum + row_sum(routed_grad * unit)
        bias_sum = bias_sum + row_sum(routed_grad)
        hidden_grad = cot_ref[span, :].astype(F32) + norm_back(unit, inverse, gain_two, routed_grad)
        routed_sum[span, :] = hidden_grad
        low = hidden_grad.astype(BF16)
        low_ref[span, :] = low
        heads_grad_ref[span, :] = contract_last(low, full_ref[:, 3 * width : 4 * width]).astype(BF16)
    heads_load.wait()
    kind = dense_ref.dtype
    dense_ref[:, 3 * width : 4 * width] = contract_first(heads_ref[...], low_ref[...]).astype(kind)
    dense_ref[:, 4 * width :] = contract_first(routed_ref[...], logits_ref[...]).astype(kind)
    tile = 4 * width + cfg.gate_columns // LANES * LANES
    lane = cfg.gate_columns % LANES
    tile = slice(tile, tile + LANES)
    dense_ref[:, tile] += rows_to_lanes(gain_sum, bias_sum, lane + 2).astype(kind)
    proj_load.wait()
    lane_row = iota((1, LANES), 1)
    scale = HEAD_DIM ** (-0.5)
    block = 256

    def slab(i, carry):
        off = pl.multiple_of(i * LANES, LANES)
        queries = proj_ref[:, pl.ds(off, LANES)] * jnp.asarray(scale, BF16)
        keys = proj_ref[:, pl.ds(width + off, LANES)]
        values = proj_ref[:, pl.ds(2 * width + off, LANES)]
        grads = heads_grad_ref[:, pl.ds(off, LANES)]
        query_grad = [jnp.zeros((block, LANES), F32)] * (count // block)
        key_grad = jnp.zeros((count, LANES), F32)
        value_grad = jnp.zeros((count, LANES), F32)
        for half in (0, 1):
            part = jnp.where(lane_row // HEAD_DIM == half, 1.0, 0.0).astype(BF16)
            query_half, key_half, grads_half = queries * part, keys * part, grads * part
            logs = lse_ref[pl.ds(2 * i + half, 1), :]
            for q in range(count // block):
                span = slice(q * block, (q + 1) * block)
                scores = contract_last(key_half, queries[span]) + bias_ref[:, span] - logs[:, span]
                probs = jnp.exp(scores)
                prob_grad = contract_last(values, grads_half[span])
                score_grad = (probs * (prob_grad - row_sum(probs * prob_grad))).astype(BF16)
                value_grad = value_grad + mm(probs.astype(BF16), grads_half[span])
                key_grad = key_grad + mm(score_grad, query_half[span])
                query_grad[q] = query_grad[q] + contract_first(score_grad, key_half)
        for q in range(count // block):
            qkv_ref[q * block : (q + 1) * block, pl.ds(off, LANES)] = (query_grad[q] * scale).astype(BF16)
        qkv_ref[:, pl.ds(width + off, LANES)] = key_grad.astype(BF16)
        qkv_ref[:, pl.ds(2 * width + off, LANES)] = value_grad.astype(BF16)
        return carry

    lax.fori_loop(0, width // LANES, slab, 0)
    tokens_load.wait()
    left_load.wait()
    gain_sum = jnp.zeros((1, width), F32)
    bias_sum = jnp.zeros((1, width), F32)
    for c in range(count // chunk):
        span = slice(c * chunk, (c + 1) * chunk)
        normed_grad = contract_last(qkv_ref[span, :], full_ref[:, left])
        unit, inverse = norm_parts(tokens_ref[span, :].astype(F32))
        low_ref[span, :] = (unit * gain_one + bias_one).astype(BF16)
        gain_sum = gain_sum + row_sum(normed_grad * unit)
        bias_sum = bias_sum + row_sum(normed_grad)
        grad_all[span, :] = routed_sum[span, :] + norm_back(unit, inverse, gain_one, normed_grad)
        stores.start(grad_all.at[span], grad_ref.at[span])
    turned_ref[...] = jnp.transpose(low_ref[...])
    dense_ref[:, tile] += rows_to_lanes(gain_sum, bias_sum, lane).astype(kind)
    owners = [mask for masks in cfg.owners for mask in masks]
    rows = width // len(owners)
    for c in range(width // chunk):
        span = slice(c * chunk, (c + 1) * chunk)
        dense_ref[span, left] = mm(turned_ref[span, :], qkv_ref[...]).astype(kind)
    if len(dense_outs) == 1:
        stores.start(dense_ref, dense_outs[0])
    else:
        for at, mask in enumerate(owners):
            half = at * 2 // len(owners)
            to = (at - half * len(owners) // 2) * rows
            source = pl.multiple_of((me ^ mask) * rows, rows)
            stores.start(dense_ref.at[pl.ds(source, rows)], dense_outs[half].at[to : to + rows])
    stores.finish()


def output_kernel(cfg, side_ref, hidden_ref, result_ref, out_ref):
    count, width = hidden_ref.shape
    slot = iota_f((count, cfg.experts * cfg.cap), 1)
    pick = (slot == side_ref[:, 0:1]) | (slot == side_ref[:, 1:2])
    mixed = mm(jnp.where(pick, 1.0, 0.0).astype(BF16), result_ref[...])
    out_ref[...] = (hidden_ref[...] + mixed).astype(BF16)


class Config:
    pass


def after(value, other):
    return lax.optimization_barrier((value, other))[0]


def apart(always, part, *args):
    given = jax.eval_shape(part, *args)

    def never(*_):
        return jax.tree.map(lambda s: jnp.zeros(s.shape, s.dtype), given)

    return lax.cond(always, part, never, *args)


def swap_hidden(value, mask):
    size = lax.axis_size("hidden")
    return lax.ppermute(value, "hidden", [(i, i ^ mask) for i in range(size)])


def swap_expert(value, mask):
    size = lax.axis_size("expert")
    return lax.ppermute(value, "expert", [(i, i ^ mask) for i in range(size)])


def gather_rest(own):
    blocks = [own]
    bit = 2
    while bit < lax.axis_size("hidden"):
        blocks += [swap_hidden(block, bit) for block in blocks]
        bit *= 2
    return blocks


def gather_core(half):
    return [swap_hidden(block, 1) for block in half]


def in_turn(first, second):
    return [block for pair in zip(first, second) for block in pair]


def sum_rest(blocks):
    held = {i + 2: [b] for i, b in enumerate(blocks)}
    low = {i: v + [swap_hidden(held[i + 1][0], 1)] for i, v in held.items() if not i & 1}
    held = {0: [], **low}
    bit = 2
    while bit < len(blocks) + 2:
        low = {i: v for i, v in held.items() if not i & bit}
        for i in low:
            value = functools.reduce(jnp.add, held[i ^ bit])
            if 2 * bit == len(blocks) + 2:
                return low[0], value
            low[i] = low[i] + [swap_hidden(value, bit)]
        held = low
        bit *= 2


def body(
    tokens,
    lengths,
    task_ids,
    routes,
    w_qkv,
    w_attn_out,
    w_gate,
    ln1_gain,
    ln1_bias,
    ln2_gain,
    ln2_bias,
    w_in,
    w_out,
    cotangent,
):
    count, width = tokens.shape
    cfg = Config()
    cfg.experts = lax.axis_size("expert")
    cfg.hidden = lax.axis_size("hidden")
    experts, hidden = cfg.experts, cfg.hidden
    cfg.cap = cap = (3 * count * routes.shape[1] + 2 * experts - 1) // (2 * experts)
    cfg.gate_columns = w_gate.shape[1]
    cfg.gate_lanes = round_up(cfg.gate_columns + 4, LANES)
    devices = experts * hidden
    groups = Groups(devices)
    shard_rows = w_qkv.shape[0]
    staged = shard_rows % 16 == 0
    cfg.owners = groups.owners()
    me = (lax.axis_index("expert") * hidden + lax.axis_index("hidden")).astype(jnp.int32)[None]
    extra = 16
    units = w_in.shape[2]
    slots = experts * cap
    wide = 4 * width + cfg.gate_lanes
    one_dot = 2 * count * width * width

    packed = call(
        pack_kernel,
        shape((shard_rows, wide), BF16),
        [],
        [w_qkv, w_attn_out, w_gate]
        + [v.reshape(1, shard_rows) for v in (ln1_gain, ln1_bias, ln2_gain, ln2_bias)],
        1,
    )
    always = lengths[0, 0] > 0

    def first_part(packed, lengths, task_ids, routes, cotangent):
        far = groups.gather_far(packed) if staged else packed
        made = call(
            functools.partial(prep_kernel, cfg),
            [
                shape((count, LANES), F32),
                shape((8, count), F32),
                shape((experts // 2, 2, cap, width), BF16),
            ],
            [
                pltpu.VMEM((count, width), BF16),
                pltpu.VMEM((count, LANES), F32),
                pltpu.VMEM((8, count), F32),
                pltpu.VMEM((experts // 2, 2, cap, width), BF16),
                pltpu.SemaphoreType.DMA((1,)),
                pltpu.SemaphoreType.DMA((2 + experts,)),
            ],
            [lengths, task_ids, routes, cotangent],
            3 * one_dot,
            far_in=(3,),
            far_out=(0, 1, 2),
        )
        return far, made

    dense_far, (side, rows, sent_cot) = apart(
        always, first_part, packed, lengths, task_ids, routes.T, cotangent
    )
    if staged:
        dense_blocks = groups.gather_near(dense_far)
        reached = dense_blocks[1 : len(groups.mid)]
    else:
        dense_blocks = [lax.all_gather(packed, BOTH, axis=0, tiled=True)]
        reached = dense_blocks[0]
    cfg.blocks = len(dense_blocks)
    parity = [list(range(i, experts, 2)) for i in (0, 1)]

    def exchange_even(value):
        return lax.all_to_all(
            value, "expert", split_axis=0, concat_axis=0, axis_index_groups=parity, tiled=True
        )

    def exchange_odd(values):
        return [swap_expert(value, 2 * i + 1) for i, value in enumerate(values)]

    cot_even = exchange_even(sent_cot)
    other = 1 - lax.axis_index("expert") % 2
    cot_odd = lax.dynamic_index_in_dim(cot_even, other, 1, keepdims=False)
    in_half = gather_rest(after(w_in[0], reached))

    outs = call(
        functools.partial(forward_kernel, cfg),
        [
            shape((width, wide), BF16),
            shape((count, 3 * width), BF16),
            shape((count, width), BF16),
            shape((HEADS, count), F32),
            shape((count, width), F32),
            shape((count, LANES), F32),
        ]
        + [shape((experts // 2, cap + extra, width), BF16)]
        + [shape((cap + extra, width), BF16)] * (experts // 2),
        [
            pltpu.VMEM((width, wide), BF16),
            pltpu.VMEM((count, 3 * width), BF16),
            pltpu.VMEM((count, width), BF16),
            pltpu.VMEM((HEADS, count), F32),
            pltpu.VMEM((count, width), F32),
            pltpu.VMEM((count, LANES), F32),
            pltpu.VMEM((experts, extra, width), BF16),
            pltpu.VMEM((slots, width), BF16),
            pltpu.VMEM((slots, count), BF16),
            pltpu.VMEM((count, count), F32),
            pltpu.VMEM((count, width), BF16),
            pltpu.VMEM((count, LANES), F32),
            pltpu.SemaphoreType.DMA((devices,)),
            pltpu.SemaphoreType.DMA((6 + 2 * experts,)),
        ],
        [me, side, rows, tokens] + dense_blocks,
        12 * one_dot,
        smem=(0,),
        far_in=range(4, 4 + cfg.blocks),
        far_out=range(7 + experts // 2),
    )
    full, proj, heads, lse, hidden_one, gates = outs[:6]
    send_rows = outs[6:]
    def even_part(even_send, odd_send, cot_even, cot_odd, in_half, own_out):
        out_half = gather_rest(own_out)
        more_in, more_out = gather_core(in_half), gather_core(out_half)
        blocks = in_turn(in_half, more_in) + in_turn(out_half, more_out)
        even_rows = exchange_even(even_send)
        odd_rows = exchange_odd(odd_send)
        cot_odd = swap_expert(cot_odd, 1)
        out = expert_part(cfg, 0, me, cot_even, [even_rows], blocks, [])
        return even_rows, odd_rows, cot_odd, more_in, out_half[1:], more_out, out

    def odd_part(even_send, even_rows, odd_rows, cot_odd, in_blocks, out_blocks, before, even_pairs):
        even_back = exchange_even(even_send)
        blocks = in_blocks + out_blocks
        result, sends, pairs = expert_part(cfg, 1, me, cot_odd, odd_rows, blocks, [before])
        odd_back = exchange_odd(sends)
        sums = apart(always, far_weights, even_rows, odd_rows, [even_pairs, pairs], in_blocks, out_blocks)
        return [even_back] + odd_back, result, pairs, *sums

    def far_weights(even_rows, odd_rows, pairs, in_blocks, out_blocks):
        picked = [b for b in range(hidden) if b > 1]
        return sum_rest(
            weight_part(cfg, picked, me, even_rows, odd_rows, pairs, in_blocks, out_blocks)
        )

    def own_weights(even_rows, odd_rows, pairs, in_blocks, out_blocks):
        return weight_part(cfg, [0, 1], me, even_rows, odd_rows, pairs, in_blocks, out_blocks)

    even_rows, odd_rows, cot_odd, more_in, rest_out, more_out, even_out = apart(
        always, even_part, send_rows[0], send_rows[1:], cot_even, cot_odd, in_half, w_out[0]
    )
    out_half = [w_out[0]] + rest_out
    in_blocks, out_blocks = in_turn(in_half, more_in), in_turn(out_half, more_out)
    back, result, odd_pairs, held, value = apart(
        always,
        odd_part,
        even_out[1][0],
        even_rows,
        odd_rows,
        cot_odd,
        in_blocks,
        out_blocks,
        even_out[0],
        even_out[2],
    )
    pairs = [even_out[2], odd_pairs]
    returned = lax.all_to_all(
        after(result, back), "expert", split_axis=0, concat_axis=0, tiled=True
    )
    if staged:
        dense_shapes = [shape((width // 2, wide), BF16)] * 2
    else:
        dense_shapes = [shape((width, wide), F32)]
    cfg.dense_outs = len(dense_shapes)

    def back_kernel_part(back):
        args = [me, side, rows, gates, lse] + back + [hidden_one, cotangent, heads, tokens, proj, full]
        outs = call(
            functools.partial(backward_kernel, cfg),
            [shape((count, width), F32)] + dense_shapes,
            [
                pltpu.VMEM((slots, width), BF16),
                pltpu.VMEM((experts, extra, width), BF16),
                pltpu.VMEM((count, width), F32),
                pltpu.VMEM((count, width), BF16),
                pltpu.VMEM((count, width), BF16),
                pltpu.VMEM((count, width), BF16),
                pltpu.VMEM((count, 3 * width), BF16),
                pltpu.VMEM((width, wide), BF16),
                pltpu.VMEM((count, width), F32),
                pltpu.VMEM((count, width), BF16),
                pltpu.VMEM((count, cfg.gate_lanes), BF16),
                pltpu.VMEM((count, width), BF16),
                pltpu.VMEM((count, width), BF16),
                pltpu.VMEM((count, count), F32),
                pltpu.VMEM((count, 3 * width), BF16),
                pltpu.VMEM((width, count), BF16),
                pltpu.VMEM((width, wide), dense_shapes[0].dtype),
                pltpu.VMEM((count, width), F32),
                pltpu.SemaphoreType.DMA((2 * experts + 7,)),
                pltpu.SemaphoreType.DMA((4 + devices,)),
            ],
            args,
            19 * one_dot,
            smem=(0,),
            far_in=range(5, len(args)),
            far_out=range(1 + len(dense_shapes)),
        )
        return (*outs[:2], groups.swap(outs[2], 1)) if staged else tuple(outs)

    def back_part(value, back):
        return swap_hidden(value, hidden // 2), apart(always, back_kernel_part, back)

    last, outs = apart(always, back_part, value, back)
    reached = held + [last]
    grad_tokens = outs[0]

    def last_weights(blocks):
        got = [groups.swap(b, m) for b, m in zip(blocks[1:], groups.mid[1:])]
        return got, own_weights(even_rows, odd_rows, pairs, in_blocks, out_blocks)

    def last_sums(blocks, own, more, reached, returned):
        layer_out = call(
            functools.partial(output_kernel, cfg),
            shape((count, width), BF16),
            [],
            [side, hidden_one, returned.reshape(slots, width)],
            6 * one_dot,
        )
        got = [groups.swap(b, m) for b, m in zip(blocks[1:], groups.far[1:])]
        terms = [own, swap_hidden(more, 1)] + reached
        grad_in, grad_out = call(
            turn_add_kernel,
            [shape((width, units), F32), shape((units, width), F32)],
            [],
            terms,
            4 * width * units,
            limit=2 * SMALL_LIMIT,
        )
        return got, grad_in, grad_out, layer_out

    blocks = [None]
    if staged:
        blocks = add_parts(outs[1], [outs[2]], len(groups.mid))
    got, (own, more) = apart(always, last_weights, blocks)
    if staged:
        blocks = add_parts(blocks[0], got, len(groups.far))
    got, grad_in, grad_out, layer_out = apart(
        always, last_sums, blocks, own, more, reached, returned
    )
    if staged:
        dense_terms = blocks[:1] + got
    else:
        dense_terms = [lax.psum_scatter(outs[1], BOTH, scatter_dimension=0, tiled=True)]
    dense_outs = call(
        functools.partial(split_kernel, cfg),
        [shape((shard_rows, c), F32) for c in (3 * width, width, cfg.gate_columns)]
        + [shape((1, shard_rows), F32)] * 4,
        [],
        dense_terms,
        shard_rows * wide,
        limit=SMALL_LIMIT,
    )

    return (
        layer_out,
        grad_tokens,
        *dense_outs[:3],
        *[v.reshape(shard_rows) for v in dense_outs[3:]],
        grad_in[None],
        grad_out[None],
    )


def solution(mesh):
    split = P(BOTH, None)
    vector = P(BOTH)
    placed = (split,) * 7 + (vector,) * 4 + (P("expert", None, "hidden"), P("expert", "hidden", None), split)
    return jax.shard_map(
        body,
        mesh=mesh,
        in_specs=placed,
        out_specs=(split,) * 5
        + (vector,) * 4
        + (P("expert", None, "hidden"), P("expert", "hidden", None)),
        check_vma=False,
    )
```
